32 devices in a mesh: grp: 4 (over y, x), row: 8 (over z, core).
Axes of the slice: x: 2, y: 2, z: 4, core: 2. Of those that a mesh axis runs over, the one named last changes fastest.
Arguments:
- tokens: bfloat16 [768, 20480], P('grp', 'row'), may hold values from -11 to 11
- segments: int32 [40, 512], P('row'), may hold values from 0 to 3, never falling along the last dimension, each value on 1 to 256 neighbouring positions
- owners: int32 [12], replicated, may hold values from 0 to 7, as said below
- masters: float32 [4, 64, 36864], P('grp', 'row'), may hold values from -4 to 4
- first_moment: float32 [4, 64, 36864], P('grp', 'row'), may hold values from -429.32505 to 429.32505
- second_moment: float32 [4, 64, 36864], P('grp', 'row'), may hold values from 0 to 20480
- vectors: float32 [2, 12, 768], P(None, None, 'grp'), may hold values from -3 to 3
- vector_first: float32 [2, 12, 768], P(None, None, 'grp'), may hold values from -429.32505 to 429.32505
- vector_second: float32 [2, 12, 768], P(None, None, 'grp'), may hold values from 0 to 20480
- cotangent: float32 [768, 20480], P('grp', 'row'), may hold values from -6 to 6
Outputs:
- layer_output: float32 [768, 20480], P('grp', 'row')
- input_grad: float32 [768, 20480], P('grp', 'row')
- new_masters: float32 [4, 64, 36864], P('grp', 'row')
- new_first: float32 [4, 64, 36864], P('grp', 'row')
- new_second: float32 [4, 64, 36864], P('grp', 'row')
- new_vectors: float32 [2, 12, 768], P(None, None, 'grp')
- new_vector_first: float32 [2, 12, 768], P(None, None, 'grp')
- new_vector_second: float32 [2, 12, 768], P(None, None, 'grp')
The draws below stay inside these ranges and needn't reach their ends.
Inputs may be any that keep to these rules, and one draw needn't show every extreme that they name: `owners`: each matrix is owned whole by one index of row. The matrices of 4 blocks go two to a device, on distinct devices, which then own exactly 8 blocks; each matrix of one block goes to another device, no device owning more than 8 blocks.
All inputs are finite; a program needn't handle non-finite values.
Results may differ from the reference program's by a relative error of at most 0.03.
The reference program's roundings to bfloat16 on the way count: a program that leaves them out, or rounds other values in their place, can miss the bound.
Values may be sent and summed in bfloat16 or wider, within the bound.
No kernel may reach another device: no remote copies, remote signals or barrier semaphores. Data moves between devices by JAX's collectives and lax.ppermute only.
A program may use at most 192 MiB of HBM per device.

```python
import math
import jax
import jax.numpy as jnp
import numpy as np
from jax import lax

D = 768
HEADS = 12
HD = 64
GROUP_COUNT = 4
LEN = 512
SEQ_DEV = 5
DOCS = 4
LAYERS = 2
STEP = 7
GROUP_FEATURES = 192
FG = 768
UP_BIAS_ROWS = 4
NV = 12
ROWS = 40
TOKENS = 20480
CAP = 8
N_ROW = 8


BETA_ONE = 0.9


BETA_TWO = 0.999


def block_kinds():
    counts = []
    block_matrix = []
    block_step = []
    block_type = []
    for layer_index in range(LAYERS):
        for matrix_type in range(6):
            amount = 1 if matrix_type < 3 else GROUP_COUNT
            for position in range(amount):
                block_matrix.append(layer_index * 6 + matrix_type)
                block_step.append(position)
                block_type.append(matrix_type)
            counts.append(amount)
    return (np.array(counts, np.int32), np.array(block_matrix, np.int32), np.array(block_step, np.int32), np.array(block_type, np.int32))


def owner_list(key):
    devices_count = ROWS // SEQ_DEV
    big_ids = np.array([6 * layer_index + matrix_type for layer_index in range(LAYERS) for matrix_type in (3, 4, 5)], np.int32)
    small_ids = np.array([6 * layer_index + matrix_type for layer_index in range(LAYERS) for matrix_type in (0, 1, 2)], np.int32)
    devices = jax.random.permutation(jax.random.fold_in(key, 101), devices_count).astype(jnp.int32)
    order_big = jax.random.permutation(jax.random.fold_in(key, 102), big_ids.shape[0])
    pairs = big_ids.shape[0] // 2
    owners = jnp.zeros((6 * LAYERS,), jnp.int32)
    owners = owners.at[jnp.asarray(big_ids)[order_big]].set(devices[jnp.arange(big_ids.shape[0]) // 2])
    picks = jax.random.randint(jax.random.fold_in(key, 103), (small_ids.shape[0],), pairs, devices_count)
    owners = owners.at[jnp.asarray(small_ids)].set(devices[picks])
    return owners.astype(jnp.int32)


def slot_kinds(key):
    owners = owner_list(key)
    counts, block_matrix, block_step, block_type = block_kinds()
    matrix_ids = jnp.arange(counts.shape[0], dtype=jnp.int32)
    same_owner = owners[:, None] == owners[None, :]
    earlier = matrix_ids[None, :] < matrix_ids[:, None]
    slot_of = jnp.sum(jnp.where(same_owner & earlier, jnp.asarray(counts)[None, :], 0), axis=1)
    starts = owners * CAP + slot_of
    choose = (jnp.asarray(block_matrix)[:, None] == matrix_ids[None, :]).astype(jnp.int32)
    block_index = jnp.sum(choose * starts[None, :], axis=1) + jnp.asarray(block_step)
    return jnp.zeros((ROWS // SEQ_DEV * CAP,), jnp.int32).at[block_index].set(jnp.asarray(block_type))


def grad_scales():
    return jnp.array([1.0, 1.0, 4.0, 0.15, 0.3, 0.6], jnp.float32) * TOKENS ** 0.5


def vector_scales():
    return jnp.array([1.0, 4.0, 1.0] + [0.3] * UP_BIAS_ROWS + [1.0, 1.0, 1.0, 1.0, 1.0], jnp.float32) * TOKENS ** 0.5


def math_log_half():
    return -0.6931472


def math_log_eight():
    return 2.0794415


def draw_owners(key, part):
    return owner_list(key)


def draw_tokens(key, part):
    key = jax.random.fold_in(key, 5)
    columns = jnp.arange(D, dtype=jnp.float32) / D
    base = jnp.clip(jax.random.normal(key, (TOKENS, D), jnp.float32), -6.0, 6.0)
    return (base * (0.6 * 3.0 ** columns)[None, :]).T.astype(jnp.bfloat16)


def draw_masters(key, part):
    kinds = slot_kinds(key)
    key = jax.random.fold_in(key, 1)
    table = jnp.array([GROUP_FEATURES ** (-0.5), GROUP_FEATURES ** (-0.5), GROUP_FEATURES ** (-0.5), (D // 32) ** (-0.5), GROUP_FEATURES ** (-0.5), FG ** (-0.5)], jnp.float32)
    spread = table[kinds]
    shape = (GROUP_COUNT, ROWS // SEQ_DEV * CAP, GROUP_FEATURES * GROUP_FEATURES)
    base = jnp.clip(jax.random.normal(key, shape, jnp.float32), -6.0, 6.0)
    return base * spread[None, :, None]


def draw_first_moment(key, part):
    kinds = slot_kinds(key)
    key = jax.random.fold_in(key, 2)
    spread = grad_scales()[kinds] * ((1.0 - BETA_ONE) / BETA_ONE)
    shape = (GROUP_COUNT, ROWS // SEQ_DEV * CAP, GROUP_FEATURES * GROUP_FEATURES)
    base = jnp.clip(jax.random.normal(key, shape, jnp.float32), -6.0, 6.0)
    return base * spread[None, :, None]


def draw_second_moment(key, part):
    kinds = slot_kinds(key)
    key = jax.random.fold_in(key, 3)
    spread = jnp.square(grad_scales()[kinds]) * ((1.0 - BETA_TWO) / BETA_TWO)
    shape = (GROUP_COUNT, ROWS // SEQ_DEV * CAP, GROUP_FEATURES * GROUP_FEATURES)
    factor = jnp.exp(jax.random.uniform(key, shape, jnp.float32, math_log_half(), math_log_eight()))
    return factor * spread[None, :, None]


def draw_vectors(key, part):
    key = jax.random.fold_in(key, 4)
    columns = jnp.arange(D, dtype=jnp.float32) / D
    rows_ids = jnp.arange(NV)
    gain_rows = ((rows_ids == 4 + UP_BIAS_ROWS) | (rows_ids == 6 + UP_BIAS_ROWS))[None, :, None]
    shape = (LAYERS, NV, D)
    factor = jax.random.uniform(jax.random.fold_in(key, 1), shape, jnp.float32, 0.8, 1.2)
    gains = factor * (0.6 * 3.0 ** columns)[None, None, :]
    biases = 0.2 * jnp.clip(jax.random.normal(jax.random.fold_in(key, 2), shape, jnp.float32), -6.0, 6.0)
    return jnp.where(gain_rows, gains, biases)


def draw_vector_first(key, part):
    key = jax.random.fold_in(key, 6)
    base = jnp.clip(jax.random.normal(key, (LAYERS, NV, D), jnp.float32), -6.0, 6.0)
    return base * (vector_scales() * ((1.0 - BETA_ONE) / BETA_ONE))[None, :, None]


def draw_vector_second(key, part):
    key = jax.random.fold_in(key, 7)
    factor = jnp.exp(jax.random.uniform(key, (LAYERS, NV, D), jnp.float32, math_log_half(), math_log_eight()))
    return factor * (jnp.square(vector_scales()) * ((1.0 - BETA_TWO) / BETA_TWO))[None, :, None]


def levels(key, dims, shards, smallest, top_value):
    loudness, own = 1.0, jax.random.fold_in(key, 6)
    for axis_at, shards_of in shards:
        draws = jnp.exp(jax.random.uniform(jax.random.fold_in(own, axis_at), (shards_of,), jnp.float32, smallest / len(shards), top_value / len(shards)))
        loudness = loudness * jnp.repeat(draws, dims[axis_at] // shards_of).reshape([-1 if axis == axis_at else 1 for axis in range(len(dims))])
    return loudness


def length_profile(count, total, bound, slope):
    portions = [(1 << 20) // math.isqrt(standing ** slope) + 1 for standing in range(2, count + 1)]
    spare, holding = total - bound - (count - 1), [1] * (count - 1)
    while spare > 0:
        candidates = [i for i in range(count - 1) if holding[i] < bound]
        whole, budget = sum([portions[i] for i in candidates]), spare
        for i in candidates:
            extra = min(bound - holding[i], max(1, budget * portions[i] // whole), spare)
            holding[i] = holding[i] + extra
            spare = spare - extra
    return np.array([bound] + holding)


def ragged_sizes(rng, number_of, total, reach, slope):
    if number_of == 2:
        one = jax.random.randint(rng, (), max(1, total - reach), min(reach, total - 1) + 1)
        return jnp.stack([one, total - one])
    tallies = jnp.asarray(length_profile(number_of, total, reach, slope), jnp.int32)
    couples = (number_of - 1) // 2
    giver, taker = tallies[1:1 + 2 * couples:2], tallies[2:2 + 2 * couples:2]
    margin = jnp.minimum(giver - 1, reach - taker)
    shifted = jax.random.randint(jax.random.fold_in(rng, 1), (couples,), 0, 1 << 20) % (margin + 1)
    tallies = tallies.at[1:1 + 2 * couples:2].set(giver - shifted).at[2:2 + 2 * couples:2].set(taker + shifted)
    return tallies[jax.random.permutation(jax.random.fold_in(rng, 2), number_of)]


def scatter_about(rng, extent, width, bound, shards=(), kind=jnp.bfloat16):
    values = width * jax.random.normal(rng, extent, jnp.float32)
    if shards:
        values = values * levels(rng, extent, shards, -0.22, 0.18)
    return jnp.clip(values, -bound, bound).astype(kind)


def setup_inputs(seed: int = 0) -> dict:
    arg_keys = jax.random.split(jax.random.key(seed), 11)
    tokens = draw_tokens(jax.random.fold_in(arg_keys[10], 71), 0)
    segments = jax.vmap(lambda own: jnp.searchsorted(jnp.cumsum(ragged_sizes(own, DOCS, LEN, LEN // 2, 2)), jnp.arange(LEN), side="right"))(jax.random.split(arg_keys[1], ROWS)).reshape((ROWS, LEN)).astype(jnp.int32)
    owners = draw_owners(jax.random.fold_in(arg_keys[10], 71), 0)
    masters = draw_masters(jax.random.fold_in(arg_keys[10], 71), 0)
    first_moment = draw_first_moment(jax.random.fold_in(arg_keys[10], 71), 0)
    second_moment = draw_second_moment(jax.random.fold_in(arg_keys[10], 71), 0)
    vectors = draw_vectors(jax.random.fold_in(arg_keys[10], 71), 0)
    vector_first = draw_vector_first(jax.random.fold_in(arg_keys[10], 71), 0)
    vector_second = draw_vector_second(jax.random.fold_in(arg_keys[10], 71), 0)
    cotangent = scatter_about(arg_keys[9], (D, TOKENS), 1.0, 6.0, ((0, 4), (1, 8)), jnp.float32)
    return {"tokens": tokens, "segments": segments, "owners": owners, "masters": masters, "first_moment": first_moment, "second_moment": second_moment, "vectors": vectors, "vector_first": vector_first, "vector_second": vector_second, "cotangent": cotangent}


BETA_ONE = 0.9
BETA_TWO = 0.999
LEARN_RATE = 0.1
VECTOR_RATE = 0.5
WEIGHT_DECAY = 0.01
ADAM_EPSILON = 1e-08
NORM_EPSILON = 1e-12
MASK_FILL = -1e+30
FULL_PRECISION = lax.Precision.HIGHEST

@jax.custom_vjp
def low(v):
    return lax.optimization_barrier(v.astype(jnp.bfloat16)).astype(jnp.float32)

@jax.custom_vjp
def low_back(v):
    return v

def low_keep(v):
    return (low(v), None)

def low_pass(kept, grad):
    return (grad,)

def back_keep(v):
    return (v, None)

def back_low(kept, grad):
    return (low(grad),)
low.defvjp(low_keep, low_pass)
low_back.defvjp(back_keep, back_low)

def block_layout(groups, layers):
    counts = []
    block_matrix = []
    block_step = []
    for layer_index in range(layers):
        for matrix_type in range(6):
            amount = 1 if matrix_type < 3 else groups
            for position in range(amount):
                block_matrix.append(layer_index * 6 + matrix_type)
                block_step.append(position)
            counts.append(amount)
    return (np.array(counts, np.int32), np.array(block_matrix, np.int32), np.array(block_step, np.int32))

def slot_index(owners, groups, layers, capacity):
    counts, block_matrix, block_step = block_layout(groups, layers)
    matrix_ids = jnp.arange(counts.shape[0], dtype=jnp.int32)
    same_owner = owners[:, None] == owners[None, :]
    earlier = matrix_ids[None, :] < matrix_ids[:, None]
    slot_of = lax.optimization_barrier(jnp.sum(jnp.where(same_owner & earlier, jnp.asarray(counts, jnp.int32)[None, :], 0), axis=1)).astype(jnp.int32)
    starts = (owners * capacity + slot_of).astype(jnp.int32)
    choose = (jnp.asarray(block_matrix, jnp.int32)[:, None] == matrix_ids[None, :]).astype(jnp.int32)
    block_index = lax.optimization_barrier(jnp.sum(choose * starts[None, :], axis=1)) + jnp.asarray(block_step, jnp.int32)
    return (block_index.astype(jnp.int32), slot_of)

def layer_norm(resid, gain_row, bias_row):
    centre = lax.optimization_barrier(jnp.mean(resid, axis=-1, keepdims=True))
    spread = lax.optimization_barrier(jnp.mean(jnp.square(resid - centre), axis=-1, keepdims=True))
    return (resid - centre) * lax.rsqrt(spread + NORM_EPSILON) * gain_row + bias_row

def split_blocks(weights, layer_index):
    base = layer_index * (3 + 3 * GROUP_COUNT)
    w_query = weights[:, base]
    w_key = weights[:, base + 1]
    w_value = weights[:, base + 2]
    w_out = weights[:, base + 3:base + 3 + GROUP_COUNT].transpose(0, 2, 1, 3).reshape(GROUP_COUNT, GROUP_FEATURES, GROUP_COUNT * GROUP_FEATURES)
    w_up = weights[:, base + 3 + GROUP_COUNT:base + 3 + 2 * GROUP_COUNT].transpose(0, 2, 1, 3).reshape(GROUP_COUNT, GROUP_FEATURES, FG)
    down_weight = weights[:, base + 3 + 2 * GROUP_COUNT:base + 3 + 3 * GROUP_COUNT].reshape(GROUP_COUNT, FG, GROUP_FEATURES)
    return (w_query, w_key, w_value, w_out, w_up, down_weight)

def layer_forward(hidden, segment_rows, weights, vector_row_table, layer_index):
    rows = hidden.shape[0]
    w_query, w_key, w_value, w_out, w_up, down_weight = split_blocks(weights, layer_index)
    grouped = low(hidden).reshape(rows, LEN, GROUP_COUNT, GROUP_FEATURES)

    def convolve(matrix):
        return jnp.einsum('rlgc,gcd->rlgd', grouped, matrix, precision=FULL_PRECISION)
    queries = low(low_back(convolve(w_query)) + vector_row_table[0].reshape(GROUP_COUNT, GROUP_FEATURES))
    key_rows = low(low_back(convolve(w_key)))
    value_rows = low(low_back(convolve(w_value)) + vector_row_table[1].reshape(GROUP_COUNT, GROUP_FEATURES))
    head_query = queries.reshape(rows, LEN, HEADS, HD)
    head_key = key_rows.reshape(rows, LEN, HEADS, HD)
    head_value = value_rows.reshape(rows, LEN, HEADS, HD)
    scores = low_back(jnp.einsum('rqhd,rkhd->rhqk', head_query, head_key, precision=FULL_PRECISION) * HD ** (-0.5))
    allowed = segment_rows[:, None, :, None] == segment_rows[:, None, None, :]
    scores = jnp.where(allowed, scores, MASK_FILL)
    log_total = jax.nn.logsumexp(scores, axis=-1, keepdims=True)
    probability = jnp.exp(scores - log_total)
    context = jnp.einsum('rhqk,rkhd->rqhd', low(probability), head_value, precision=FULL_PRECISION)
    context = low(low_back(context)).reshape(rows, LEN, GROUP_COUNT, GROUP_FEATURES)
    mixed = low_back(jnp.einsum('rlgc,gcd->rld', context, w_out, precision=FULL_PRECISION)) + vector_row_table[2]
    normed = layer_norm(hidden + mixed, vector_row_table[4 + UP_BIAS_ROWS], vector_row_table[5 + UP_BIAS_ROWS])
    up_bias = vector_row_table[3:3 + UP_BIAS_ROWS].reshape(UP_BIAS_ROWS, GROUP_COUNT, GROUP_FEATURES).transpose(1, 0, 2).reshape(GROUP_COUNT, FG)
    normed_low = low(normed).reshape(rows, LEN, GROUP_COUNT, GROUP_FEATURES)
    inner = low_back(jnp.einsum('rlgc,gcf->rlgf', normed_low, w_up, precision=FULL_PRECISION)) + up_bias
    gelu_output = low(jax.nn.gelu(inner, approximate=False))
    branch_output = low_back(jnp.einsum('yhdq,dqo->yhdo', gelu_output, down_weight, precision=FULL_PRECISION)) + vector_row_table[3 + UP_BIAS_ROWS].reshape(GROUP_COUNT, GROUP_FEATURES)
    return layer_norm(normed + branch_output.reshape(rows, LEN, D), vector_row_table[6 + UP_BIAS_ROWS], vector_row_table[7 + UP_BIAS_ROWS])

def adam_step(param, grad, first, second, decay, rate):
    first_new = BETA_ONE * first + (1.0 - BETA_ONE) * grad
    second_new = BETA_TWO * second + (1.0 - BETA_TWO) * grad * grad
    first_hat = first_new / (1.0 - BETA_ONE ** STEP)
    second_hat = second_new / (1.0 - BETA_TWO ** STEP)
    updated = param - rate * (first_hat / (jnp.sqrt(second_hat) + ADAM_EPSILON) + decay * param)
    return (updated, first_new, second_new)

def reference(tokens, segments, owners, masters, first_moment, second_moment, vectors, vector_first, vector_second, cotangent):
    block_index, slot_of = slot_index(owners, GROUP_COUNT, LAYERS, CAP)
    square_masters = masters.reshape(GROUP_COUNT, N_ROW * CAP, GROUP_FEATURES, GROUP_FEATURES)
    weights = square_masters[:, block_index]
    inputs = tokens.astype(jnp.float32).T.reshape(N_ROW, SEQ_DEV, LEN, D)
    segment_blocks = segments.reshape(N_ROW, SEQ_DEV, LEN)
    grad_blocks = cotangent.astype(jnp.float32).T.reshape(N_ROW, SEQ_DEV, LEN, D)

    def step_rows(carry, item_set):
        weight_sum, vector_sum = carry
        input_rows, segment_rows, grad_rows = item_set

        def forward(weight_all, vector_all, hidden):
            rounded = low(weight_all)
            for layer_index in range(LAYERS):
                hidden = layer_forward(hidden, segment_rows, rounded, vector_all[layer_index], layer_index)
            return hidden
        result, pull = jax.vjp(forward, weights, vectors, input_rows)
        weight_grad, vector_grad, input_grad = pull(grad_rows)
        return ((weight_sum + weight_grad, vector_sum + vector_grad), (result, input_grad))
    start = (jnp.zeros(weights.shape, jnp.float32), jnp.zeros(vectors.shape, jnp.float32))
    (weight_sum, vector_sum), (results, input_grads) = lax.scan(step_rows, start, (inputs, segment_blocks, grad_blocks))
    master_grad = jnp.zeros(square_masters.shape, jnp.float32).at[:, block_index].add(weight_sum).reshape(masters.shape)
    new_masters, new_first, new_second = adam_step(masters, master_grad, first_moment, second_moment, WEIGHT_DECAY, LEARN_RATE)
    new_vectors, new_vector_first, new_vector_second = adam_step(vectors, vector_sum, vector_first, vector_second, 0.0, VECTOR_RATE)
    return (results.reshape(TOKENS, D).T, input_grads.reshape(TOKENS, D).T, new_masters, new_first, new_second, new_vectors, new_vector_first, new_vector_second)
```

```python
import functools
import math

import jax
import jax.numpy as jnp
import numpy as np
from jax import lax
from jax.experimental import pallas as pl
from jax.experimental.pallas import tpu as pltpu
from jax.sharding import PartitionSpec as P

HEADS = 12
LAYERS = 2
STEP = 7
BETA_ONE = 0.9
BETA_TWO = 0.999
LEARN_RATE = 0.1
VECTOR_RATE = 0.5
WEIGHT_DECAY = 0.01
ADAM_EPSILON = 1e-08
NORM_EPSILON = 1e-12
MASK_FILL = -1e30
AUG = 16
LANES = 128
VMEM_LIMIT = 48 * 1024 * 1024
F32 = jnp.float32
BF16 = jnp.bfloat16


def nn(a, b):
    return lax.dot_general(a, b, (((1,), (0,)), ((), ())), preferred_element_type=F32)


def nt(a, b):
    return lax.dot_general(a, b, (((1,), (1,)), ((), ())), preferred_element_type=F32)


def tn(a, b):
    return lax.dot_general(a, b, (((0,), (0,)), ((), ())), preferred_element_type=F32)


def block_layout(groups, layers):
    counts = []
    block_matrix = []
    block_step = []
    for layer_index in range(layers):
        for matrix_type in range(6):
            amount = 1 if matrix_type < 3 else groups
            for position in range(amount):
                block_matrix.append(layer_index * 6 + matrix_type)
                block_step.append(position)
            counts.append(amount)
    return (
        np.array(counts, np.int32),
        np.array(block_matrix, np.int32),
        np.array(block_step, np.int32),
    )


def slot_index(owners, groups, layers, capacity):
    counts, block_matrix, block_step = block_layout(groups, layers)
    matrix_ids = jnp.arange(counts.shape[0], dtype=jnp.int32)
    same_owner = owners[:, None] == owners[None, :]
    earlier = matrix_ids[None, :] < matrix_ids[:, None]
    slot_of = jnp.sum(
        jnp.where(same_owner & earlier, jnp.asarray(counts, jnp.int32)[None, :], 0), axis=1
    )
    starts = owners * capacity + slot_of
    choose = (jnp.asarray(block_matrix, jnp.int32)[:, None] == matrix_ids[None, :]).astype(
        jnp.int32
    )
    return jnp.sum(choose * starts[None, :], axis=1) + jnp.asarray(block_step, jnp.int32)


def lanes(value):
    total = value[:, :LANES]
    for at in range(LANES, value.shape[1], LANES):
        total = total + value[:, at : at + LANES]
    return total


def first_step():
    return pl.program_id(0) == 0


def accumulate(ref, index, value):
    @pl.when(first_step())
    def _():
        ref[index] = value

    @pl.when(jnp.logical_not(first_step()))
    def _():
        ref[index] = ref[index] + value


def col_sums(a, b):
    return jnp.concatenate(
        [jnp.sum(a, axis=0, keepdims=True), jnp.sum(b, axis=0, keepdims=True)], axis=0
    )


def gathered(stats):
    return (stats[0][...] + stats[1][...]) + (stats[2][...] + stats[3][...])


def moments(stats, full):
    total = gathered(stats)
    centre = total[0:1] * (1.0 / full)
    spread = total[1:2] * (1.0 / full) - centre * centre
    return centre, lax.rsqrt(jnp.maximum(spread, 0.0) + NORM_EPSILON)


def split3(value):
    high = value.astype(BF16)
    rest = value - high.astype(F32)
    mid = rest.astype(BF16)
    last = (rest - mid.astype(F32)).astype(BF16)
    return high, mid, last


def segment_rows(segs):
    row = lax.broadcasted_iota(jnp.int32, (AUG, segs.shape[1]), 0)
    same = row == segs
    query_rows = jnp.where(same | (row >= 4), 0.0, MASK_FILL)
    key_rows = jnp.where(same | ((row >= 4) & (row < 7)), 1.0, 0.0)
    return query_rows, key_rows.astype(BF16)


def with_rows(query_rows, value):
    high, mid, last = split3(-value)
    row = lax.broadcasted_iota(jnp.int32, query_rows.shape, 0)
    out = jnp.where(row == 4, high.astype(F32), query_rows)
    out = jnp.where(row == 5, mid.astype(F32), out)
    out = jnp.where(row == 6, last.astype(F32), out)
    return out.astype(BF16)


def norm_cdf(u):
    a = jnp.abs(u) * math.sqrt(0.5)
    t = 1.0 / (1.0 + 0.3275911 * a)
    bell = jnp.exp(-a * a)
    poly = t * (
        0.254829592
        + t * (-0.284496736 + t * (1.421413741 + t * (-1.453152027 + t * 1.061405429)))
    )
    tail = (0.5 * poly) * bell
    return jnp.where(u < 0, tail, 1.0 - tail), bell * (1.0 / math.sqrt(2.0 * math.pi))


def attend_body(first, per_group, full, *refs):
    refs = list(refs)
    if first:
        x_ref = refs.pop(0)
    else:
        r2_ref = refs.pop(0)
        stats = [refs.pop(0) for _ in range(4)]
        prev_ref = refs.pop(0)
    seg_ref, w_ref, vec_ref = refs[:3]
    refs = refs[3:]
    if not first:
        x2_ref, mi_ref = refs[:2]
        refs = refs[2:]
    qkv_ref, low_ref, high_ref, lse_ref = refs[:4]
    width = w_ref.shape[1]
    size = width // per_group
    vec = vec_ref[...]
    if first:
        x = x_ref[...]
    else:
        centre, inverse = moments(stats, full)
        prev = prev_ref[...]
        nup = prev.shape[1] - 8
        x2 = (r2_ref[...] - centre) * inverse * prev[:, 6 + nup : 7 + nup] + prev[
            :, 7 + nup : 8 + nup
        ]
        x2_ref[...] = x2
        mi_ref[...] = jnp.concatenate([centre, inverse], axis=0)
        x = x2.astype(BF16)
    q = (tn(w_ref[0], x) + vec[:, 0:1]).astype(BF16)
    k = tn(w_ref[1], x).astype(BF16)
    v = (tn(w_ref[2], x) + vec[:, 1:2]).astype(BF16)
    qkv_ref[0:width] = q
    qkv_ref[width : 2 * width] = k
    qkv_ref[2 * width : 3 * width] = v
    query_rows, key_rows = segment_rows(seg_ref[0])
    query_rows = query_rows.astype(BF16)
    scale = size ** (-0.5)
    length = x.shape[1]
    tile = 256
    for h in range(per_group):
        part = slice(h * size, (h + 1) * size)
        qa = jnp.concatenate([q[part] * jnp.asarray(scale, BF16), query_rows], axis=0)
        ka = jnp.concatenate([k[part], key_rows], axis=0)
        for at in range(0, length, tile):
            cols = slice(at, at + tile)
            s = tn(ka, qa[:, cols])
            top = jnp.max(s, axis=0, keepdims=True)
            e = jnp.exp(s - top)
            total = jnp.sum(e, axis=0, keepdims=True)
            ctx = (nn(v[part], e.astype(BF16)) * (1.0 / total)).astype(BF16)
            lse_ref[h : h + 1, cols] = top + jnp.log(total)
            half = width // 2
            lo, hi = h * size, (h + 1) * size
            if hi <= half:
                low_ref[lo:hi, cols] = ctx
            elif lo >= half:
                high_ref[lo - half : hi - half, cols] = ctx
            else:
                low_ref[lo:half, cols] = ctx[: half - lo]
                high_ref[0 : hi - half, cols] = ctx[half - lo :]


def out_body(x_ref, *refs):
    pieces = refs[:8]
    w_ref, vec_ref, r1_ref, st_ref = refs[8:]
    groups = w_ref.shape[0]
    total = x_ref[...].astype(F32) + vec_ref[...][:, 2:3]
    for g in range(groups):
        piece = jnp.concatenate([pieces[2 * g][...], pieces[2 * g + 1][...]], axis=0)
        total = total + tn(w_ref[g], piece)
    r1_ref[...] = total
    st_ref[...] = col_sums(total, total * total)


def mlp_body(full, r1_ref, s0, s1, s2, s3, wu_ref, wd_ref, vec_ref, r2_ref, mi_ref, hid_ref, gp_ref, st_ref):
    groups = wu_ref.shape[0]
    width = r1_ref.shape[0]
    vec = vec_ref[...]
    nup = vec.shape[1] - 8
    centre, inverse = moments((s0, s1, s2, s3), full)
    mi_ref[...] = jnp.concatenate([centre, inverse], axis=0)
    y1 = (r1_ref[...] - centre) * inverse * vec[:, 4 + nup : 5 + nup] + vec[:, 5 + nup : 6 + nup]
    yl = y1.astype(BF16)
    total = y1 + vec[:, 3 + nup : 4 + nup]
    for j in range(groups):
        u = tn(wu_ref[j], yl) + vec[:, 3 + j : 4 + j]
        cdf, bell = norm_cdf(u)
        hid = (u * cdf).astype(BF16)
        hid_ref[j * width : (j + 1) * width] = hid
        gp_ref[j * width : (j + 1) * width] = (cdf + u * bell).astype(BF16)
        total = total + tn(wd_ref[j], hid)
    r2_ref[...] = total
    st_ref[...] = col_sums(total, total * total)


def last_body(full, r2_ref, s0, s1, s2, s3, cot_ref, vec_ref, _, out_ref, mi_ref, st_ref, acc_ref):
    vec = vec_ref[...]
    nup = vec.shape[1] - 8
    centre, inverse = moments((s0, s1, s2, s3), full)
    mi_ref[...] = jnp.concatenate([centre, inverse], axis=0)
    n2 = (r2_ref[...] - centre) * inverse
    gain = vec[:, 6 + nup : 7 + nup]
    out_ref[...] = n2 * gain + vec[:, 7 + nup : 8 + nup]
    dy = cot_ref[...]
    e = dy * gain
    st_ref[...] = col_sums(e, e * n2)
    accumulate(acc_ref, 0, lanes(dy * n2))
    accumulate(acc_ref, 1, lanes(dy))


def mlp_back_body(
    full, dy_ref, r2_ref, mi2_ref, s0, s1, s2, s3, r1_ref, mi1_ref, hid_ref, gp_ref, wu_ref, wd_ref, vec_ref,
    dy1_ref, st_ref, gup_ref, gdown_ref, acc_ref,
):
    groups = wu_ref.shape[0]
    width = r1_ref.shape[0]
    vec = vec_ref[...]
    nup = vec.shape[1] - 8
    sums = gathered((s0, s1, s2, s3)) * (1.0 / full)
    mi2 = mi2_ref[...]
    n2 = (r2_ref[...] - mi2[0:1]) * mi2[1:2]
    e = dy_ref[...] * vec[:, 6 + nup : 7 + nup]
    dz = mi2[1:2] * (e - sums[0:1] - n2 * sums[1:2])
    accumulate(acc_ref, groups, lanes(dz))
    dzl = dz.astype(BF16)
    mi1 = mi1_ref[...]
    n1 = (r1_ref[...] - mi1[0:1]) * mi1[1:2]
    gain1 = vec[:, 4 + nup : 5 + nup]
    yl = (n1 * gain1 + vec[:, 5 + nup : 6 + nup]).astype(BF16)
    dy1 = dz
    for j in range(groups):
        rows = slice(j * width, (j + 1) * width)
        accumulate(gdown_ref, j, nt(hid_ref[rows], dzl))
        du = nn(wd_ref[j], dzl) * gp_ref[rows].astype(F32)
        accumulate(acc_ref, j, lanes(du))
        dul = du.astype(BF16)
        accumulate(gup_ref, j, nt(yl, dul))
        dy1 = dy1 + nn(wu_ref[j], dul)
    dy1_ref[...] = dy1
    e1 = dy1 * gain1
    st_ref[...] = col_sums(e1, e1 * n1)
    accumulate(acc_ref, groups + 1, lanes(dy1 * n1))
    accumulate(acc_ref, groups + 2, lanes(dy1))


def norm_back_body(full, dy1_ref, r1_ref, mi1_ref, s0, s1, s2, s3, vec_ref, dr1_ref, low_ref, high_ref, acc_ref):
    vec = vec_ref[...]
    nup = vec.shape[1] - 8
    sums = gathered((s0, s1, s2, s3)) * (1.0 / full)
    mi1 = mi1_ref[...]
    n1 = (r1_ref[...] - mi1[0:1]) * mi1[1:2]
    e = dy1_ref[...] * vec[:, 4 + nup : 5 + nup]
    dr = mi1[1:2] * (e - sums[0:1] - n1 * sums[1:2])
    dr1_ref[...] = dr
    accumulate(acc_ref, 0, lanes(dr))
    half = low_ref.shape[0]
    low = dr.astype(BF16)
    low_ref[...] = low[:half]
    high_ref[...] = low[half:]


def attend_back_body(first, per_group, *refs):
    dr1_ref = refs[0]
    pieces = refs[1:9]
    ctx_low_ref, ctx_high_ref, qkv_ref, lse_ref, x_ref, seg_ref, w_ref, wo_ref, vec_ref = refs[9:18]
    refs = refs[18:]
    if first:
        _, dx_ref, gqkv_ref, gout_ref, acc_ref = refs
    else:
        r2_ref, mi2_ref, prev_ref, dx_ref, gqkv_ref, gout_ref, acc_ref, st_ref = refs
    groups = wo_ref.shape[0]
    width = dr1_ref.shape[0]
    size = width // per_group
    scale = size ** (-0.5)
    ctx = jnp.concatenate([ctx_low_ref[...], ctx_high_ref[...]], axis=0)
    dctx = None
    for g in range(groups):
        dal = jnp.concatenate([pieces[2 * g][...], pieces[2 * g + 1][...]], axis=0)
        accumulate(gout_ref, g, nt(ctx, dal))
        term = nn(wo_ref[g], dal)
        dctx = term if dctx is None else dctx + term
    dctx = dctx.astype(BF16)
    x = x_ref[...].astype(BF16)
    query_rows, key_rows = segment_rows(seg_ref[0])
    zero_rows = jnp.zeros_like(query_rows)
    q = qkv_ref[0:width]
    k = qkv_ref[width : 2 * width]
    v = qkv_ref[2 * width : 3 * width]
    dq, dk, dv = [], [], []
    for h in range(per_group):
        part = slice(h * size, (h + 1) * size)
        qh, kh, vh, dch = q[part], k[part], v[part], dctx[part]
        qs = qh * jnp.asarray(scale, BF16)
        delta = jnp.sum(dch.astype(F32) * ctx[part].astype(F32), axis=0, keepdims=True)
        qa = jnp.concatenate([qs, with_rows(query_rows, lse_ref[h : h + 1])], axis=0)
        ka = jnp.concatenate([kh, key_rows], axis=0)
        da = jnp.concatenate([dch, with_rows(zero_rows, delta)], axis=0)
        va = jnp.concatenate([vh, key_rows], axis=0)
        p = jnp.exp(tn(ka, qa))
        ds = (p * tn(va, da)).astype(BF16)
        dv.append(nt(dch, p.astype(BF16)))
        dq.append(nn(kh, ds) * scale)
        dk.append(nt(qs, ds))
    dq = jnp.concatenate(dq, axis=0)
    dk = jnp.concatenate(dk, axis=0)
    dv = jnp.concatenate(dv, axis=0)
    accumulate(acc_ref, 0, lanes(dq))
    accumulate(acc_ref, 1, lanes(dv))
    dx = dr1_ref[...]
    for at, grad in enumerate((dq, dk, dv)):
        low = grad.astype(BF16)
        accumulate(gqkv_ref, at, nt(x, low))
        dx = dx + nn(w_ref[at], low)
    dx_ref[...] = dx
    if not first:
        prev = prev_ref[...]
        nup = prev.shape[1] - 8
        mi2 = mi2_ref[...]
        n2 = (r2_ref[...] - mi2[0:1]) * mi2[1:2]
        e = dx * prev[:, 6 + nup : 7 + nup]
        st_ref[...] = col_sums(e, e * n2)
        accumulate(acc_ref, 2, lanes(dx * n2))
        accumulate(acc_ref, 3, lanes(dx))


class Spec:
    def __init__(self, length, count, offset):
        self.length, self.count, self.offset = length, count, offset

    def tok(self, rows):
        return pl.BlockSpec((rows, self.length), lambda i: (0, i))

    def far(self, rows):
        offset = self.offset
        return pl.BlockSpec((rows, self.length), lambda i: (0, i + offset))

    def seg(self):
        offset = self.offset
        return pl.BlockSpec((1, 1, self.length), lambda i: (i + offset, 0, 0))

    def whole(self, shape):
        return pl.BlockSpec(shape, lambda i: (0,) * len(shape))

    def shape(self, rows, dtype=F32):
        return jax.ShapeDtypeStruct((rows, self.length * self.count), dtype)

    def call(self, body, name, operands, specs, outs, out_specs, flops, aliases=None):
        tokens = self.length * self.count
        moved = sum(math.prod(s.block_shape) * 4 * self.count for s in specs + out_specs if s.block_shape)
        return pl.pallas_call(
            body,
            grid=(self.count,),
            in_specs=specs,
            out_specs=out_specs,
            out_shape=outs,
            name=name,
            input_output_aliases=aliases or {},
            compiler_params=pltpu.CompilerParams(vmem_limit_bytes=VMEM_LIMIT),
            cost_estimate=pl.CostEstimate(
                flops=int(flops * tokens), bytes_accessed=moved, transcendentals=0
            ),
        )(*operands)


def peer(value, step, groups):
    return lax.ppermute(value, "grp", [(i, i ^ step) for i in range(groups)])


def exchange(stats, groups):
    return [stats] + [peer(stats, step, groups) for step in range(1, groups)]


def spread(low, high, groups):
    low_1 = peer(low, 1, groups)
    high_2 = peer(high, 2, groups)
    low_2 = peer(low, 2, groups)
    low_3 = peer(low_1, 2, groups)
    high_1 = peer(high, 1, groups)
    high_3 = peer(high_2, 1, groups)
    return [low, high, low_1, high_1, low_2, high_2, low_3, high_3]


def adam_step(param, grad, first, second, decay, rate):
    first_new = BETA_ONE * first + (1.0 - BETA_ONE) * grad
    second_new = BETA_TWO * second + (1.0 - BETA_TWO) * grad * grad
    first_hat = first_new / (1.0 - BETA_ONE**STEP)
    second_hat = second_new / (1.0 - BETA_TWO**STEP)
    updated = param - rate * (first_hat / (jnp.sqrt(second_hat) + ADAM_EPSILON) + decay * param)
    return (updated, first_new, second_new)


def shards(
    tokens,
    segments,
    owners,
    masters,
    first_moment,
    second_moment,
    vectors,
    vector_first,
    vector_second,
    cotangent,
):
    groups = lax.axis_size("grp")
    me = lax.axis_index("grp")
    capacity = masters.shape[1]
    width, tokens_here = tokens.shape
    full = float(width * groups)
    sequences, length = segments.shape
    per_group = HEADS // groups
    half = width // 2
    nv = vectors.shape[1]
    nup = nv - 8
    per_layer = 3 + 3 * groups
    segs = segments.reshape(sequences, 1, length)

    block_index = slot_index(owners, groups, LAYERS, capacity)
    local_blocks = masters[0].reshape(capacity, width, width).astype(BF16)
    everyone = lax.all_gather(local_blocks, "row", axis=0, tiled=True)
    blocks = jnp.take(everyone, block_index, axis=0).reshape(LAYERS, per_layer, width, width)
    order = jnp.array([0, 1, 2, 3], jnp.int32) ^ me
    w_qkv = [blocks[l, :3] for l in range(LAYERS)]
    w_row = [jnp.take(blocks[l, 3 : 3 + groups], order, axis=0) for l in range(LAYERS)]
    w_up = [blocks[l, 3 + groups : 3 + 2 * groups] for l in range(LAYERS)]
    w_down = [blocks[l, 3 + 2 * groups :] for l in range(LAYERS)]
    w_col = []
    for l in range(LAYERS):
        parts = [w_row[l][0]] + [peer(w_row[l][step], step, groups) for step in range(1, groups)]
        w_col.append(jnp.stack(parts))
    vecs = [vectors[l].T for l in range(LAYERS)]

    cut = (sequences + 1) // 2
    chunks = [Spec(length, cut, 0), Spec(length, sequences - cut, cut)]
    n_chunks = len(chunks)

    keep = [dict() for _ in range(n_chunks)]
    r2 = [None] * n_chunks
    st2 = [None] * n_chunks
    for l in range(LAYERS):
        for c, sp in enumerate(chunks):
            kp = keep[c]
            wspec = sp.whole((3, width, width))
            vspec = sp.whole((width, nv))
            outs = [sp.shape(3 * width, BF16), sp.shape(half, BF16), sp.shape(half, BF16), sp.shape(per_group)]
            out_specs = [sp.tok(3 * width), sp.tok(half), sp.tok(half), sp.tok(per_group)]
            flops = 6 * width * width + 4 * width * length
            body = functools.partial(attend_body, l == 0, per_group, full)
            if l == 0:
                res = sp.call(
                    body, "attend_first", (tokens, segs, w_qkv[l], vecs[l]),
                    [sp.far(width), sp.seg(), wspec, vspec], outs, out_specs, flops,
                )
            else:
                res = sp.call(
                    body, "attend_next", (r2[c], *st2[c], vecs[l - 1], segs, w_qkv[l], vecs[l]),
                    [sp.tok(width)] + [sp.tok(2)] * 4 + [vspec, sp.seg(), wspec, vspec],
                    [sp.shape(width), sp.shape(2)] + outs, [sp.tok(width), sp.tok(2)] + out_specs, flops,
                )
                kp["x", l], kp["mi2", l - 1] = res[:2]
                res = res[2:]
            kp["qkv", l], kp["low", l], kp["high", l], kp["lse", l] = res
            kp["ctx", l] = spread(kp["low", l], kp["high", l], groups)
        for c, sp in enumerate(chunks):
            kp = keep[c]
            x_spec = sp.far(width) if l == 0 else sp.tok(width)
            x = tokens if l == 0 else kp["x", l]
            r1, st1 = sp.call(
                out_body, "out_conv", (x, *kp["ctx", l], w_col[l], vecs[l]),
                [x_spec] + [sp.tok(half)] * 8 + [sp.whole((groups, width, width)), sp.whole((width, nv))],
                [sp.shape(width), sp.shape(2)], [sp.tok(width), sp.tok(2)], 2 * width * width * groups,
            )
            kp["r1", l] = r1
            kp["st1", l] = exchange(st1, groups)
        for c, sp in enumerate(chunks):
            kp = keep[c]
            gw = sp.whole((groups, width, width))
            fg = groups * width
            r2[c], kp["mi1", l], kp["hid", l], kp["gp", l], st = sp.call(
                functools.partial(mlp_body, full), "mlp",
                (kp["r1", l], *kp["st1", l], w_up[l], w_down[l], vecs[l]),
                [sp.tok(width)] + [sp.tok(2)] * 4 + [gw, gw, sp.whole((width, nv))],
                [sp.shape(width), sp.shape(2), sp.shape(fg, BF16), sp.shape(fg, BF16), sp.shape(2)],
                [sp.tok(width), sp.tok(2), sp.tok(fg), sp.tok(fg), sp.tok(2)], 4 * width * width * groups,
            )
            kp["r2", l] = r2[c]
            st2[c] = exchange(st, groups)

    layer_output = jnp.zeros((width, tokens_here), F32)
    input_grad = jnp.zeros((width, tokens_here), F32)
    top = LAYERS - 1
    back = [None] * n_chunks
    flowing = [None] * n_chunks
    norm_acc = [[None] * n_chunks for _ in range(LAYERS)]
    for c, sp in enumerate(chunks):
        kp = keep[c]
        layer_output, kp["mi2", top], st, norm_acc[top][c] = sp.call(
            functools.partial(last_body, full), "last_norm",
            (r2[c], *st2[c], cotangent, vecs[top], layer_output),
            [sp.tok(width)] + [sp.tok(2)] * 4
            + [sp.far(width), sp.whole((width, nv)), pl.BlockSpec(memory_space=pl.ANY)],
            [jax.ShapeDtypeStruct((width, tokens_here), F32), sp.shape(2), sp.shape(2),
             jax.ShapeDtypeStruct((2, width, LANES), F32)],
            [sp.far(width), sp.tok(2), sp.tok(2), sp.whole((2, width, LANES))], 10 * width,
            aliases={7: 0},
        )
        back[c] = exchange(st, groups)
        flowing[c] = cotangent

    block_grads = [None] * LAYERS
    vector_grads = [None] * LAYERS
    acc_mlp = [[None] * n_chunks for _ in range(LAYERS)]
    acc_bo = [[None] * n_chunks for _ in range(LAYERS)]
    acc_att = [[None] * n_chunks for _ in range(LAYERS)]
    summed = [None] * LAYERS
    for l in reversed(range(LAYERS)):
        g_up, g_down, g_qkv, g_out = ([None] * n_chunks for _ in range(4))
        for c, sp in enumerate(chunks):
            kp = keep[c]
            gw = sp.whole((groups, width, width))
            vspec = sp.whole((width, nv))
            fg = groups * width
            kp["dy1", l], st, g_up[c], g_down[c], acc_mlp[l][c] = sp.call(
                functools.partial(mlp_back_body, full), "mlp_back",
                (flowing[c], kp["r2", l], kp["mi2", l], *back[c], kp["r1", l], kp["mi1", l],
                 kp["hid", l], kp["gp", l], w_up[l], w_down[l], vecs[l]),
                [sp.far(width) if l == top else sp.tok(width), sp.tok(width), sp.tok(2)] + [sp.tok(2)] * 4
                + [sp.tok(width), sp.tok(2), sp.tok(fg), sp.tok(fg), gw, gw, vspec],
                [sp.shape(width), sp.shape(2), jax.ShapeDtypeStruct((groups, width, width), F32),
                 jax.ShapeDtypeStruct((groups, width, width), F32),
                 jax.ShapeDtypeStruct((groups + 3, width, LANES), F32)],
                [sp.tok(width), sp.tok(2), gw, gw, sp.whole((groups + 3, width, LANES))],
                8 * width * width * groups,
            )
            back[c] = exchange(st, groups)
        for c, sp in enumerate(chunks):
            kp = keep[c]
            kp["dr1", l], low, high, acc_bo[l][c] = sp.call(
                functools.partial(norm_back_body, full), "norm_back",
                (kp["dy1", l], kp["r1", l], kp["mi1", l], *back[c], vecs[l]),
                [sp.tok(width), sp.tok(width), sp.tok(2)] + [sp.tok(2)] * 4 + [sp.whole((width, nv))],
                [sp.shape(width), sp.shape(half, BF16), sp.shape(half, BF16),
                 jax.ShapeDtypeStruct((1, width, LANES), F32)],
                [sp.tok(width), sp.tok(half), sp.tok(half), sp.whole((1, width, LANES))], 10 * width,
            )
            kp["dal", l] = spread(low, high, groups)
        for c, sp in enumerate(chunks):
            kp = keep[c]
            gw = sp.whole((groups, width, width))
            w3 = sp.whole((3, width, width))
            vspec = sp.whole((width, nv))
            rows = 2 if l == 0 else 4
            operands = [kp["dr1", l], *kp["dal", l], kp["low", l], kp["high", l], kp["qkv", l], kp["lse", l],
                        tokens if l == 0 else kp["x", l], segs, w_qkv[l], w_row[l], vecs[l]]
            specs = [sp.tok(width)] + [sp.tok(half)] * 10 + [
                sp.tok(3 * width), sp.tok(per_group), sp.far(width) if l == 0 else sp.tok(width),
                sp.seg(), w3, gw, vspec]
            outs = [sp.shape(width), jax.ShapeDtypeStruct((3, width, width), F32),
                    jax.ShapeDtypeStruct((groups, width, width), F32),
                    jax.ShapeDtypeStruct((rows, width, LANES), F32)]
            out_specs = [sp.tok(width), w3, gw, sp.whole((rows, width, LANES))]
            aliases = None
            if l == 0:
                operands.append(input_grad)
                specs.append(pl.BlockSpec(memory_space=pl.ANY))
                outs[0] = jax.ShapeDtypeStruct((width, tokens_here), F32)
                out_specs[0] = sp.far(width)
                aliases = {len(operands) - 1: 0}
            else:
                operands += [kp["r2", l - 1], kp["mi2", l - 1], vecs[l - 1]]
                specs += [sp.tok(width), sp.tok(2), vspec]
                outs.append(sp.shape(2))
                out_specs.append(sp.tok(2))
            res = sp.call(
                functools.partial(attend_back_body, l == 0, per_group),
                "attend_back_first" if l == 0 else "attend_back_next", tuple(operands), specs, outs, out_specs,
                4 * width * width * groups + 12 * width * width + 10 * width * length, aliases,
            )
            if l == 0:
                input_grad, g_qkv[c], g_out[c], acc_att[l][c] = res
            else:
                flowing[c], g_qkv[c], g_out[c], acc_att[l][c], st = res
                norm_acc[l - 1][c] = acc_att[l][c][2:4]
                back[c] = exchange(st, groups)
        own_out = sum(g_out)
        inverse_order = order
        own_out = jnp.take(own_out, inverse_order, axis=0)
        grads = jnp.concatenate([sum(g_qkv), own_out, sum(g_up), sum(g_down)], axis=0)
        block_grads[l] = grads

    for l in range(LAYERS):
        def over(parts):
            return jnp.sum(sum(parts), axis=-1)

        att, bo, mlp, norm2 = over(acc_att[l]), over(acc_bo[l]), over(acc_mlp[l]), over(norm_acc[l])
        vector_grads[l] = jnp.concatenate(
            [att[0:2], bo, mlp[0:groups], mlp[groups:], norm2], axis=0
        )
        table = jnp.zeros((1, width, width), F32).at[0, :nv].set(vector_grads[l])
        summed[l] = lax.psum(jnp.concatenate([block_grads[l], table], axis=0).astype(BF16), "row")

    summed_blocks = jnp.concatenate([s[:per_layer] for s in summed], axis=0)
    summed_vectors = jnp.stack([s[per_layer, :nv] for s in summed], axis=0).astype(F32)
    flat = summed_blocks.reshape(LAYERS * per_layer, width * width)
    own_row = lax.axis_index("row")
    targets = own_row * capacity + jnp.arange(capacity, dtype=jnp.int32)
    selector = (block_index[None, :] == targets[:, None]).astype(BF16)
    own_grads = jnp.dot(selector, flat, preferred_element_type=F32)[None]
    new_masters, new_first, new_second = adam_step(
        masters, own_grads, first_moment, second_moment, WEIGHT_DECAY, LEARN_RATE
    )
    new_vectors, new_vector_first, new_vector_second = adam_step(
        vectors, summed_vectors, vector_first, vector_second, 0.0, VECTOR_RATE
    )
    return (
        layer_output,
        input_grad,
        new_masters,
        new_first,
        new_second,
        new_vectors,
        new_vector_first,
        new_vector_second,
    )


def solution(mesh):
    in_specs = (
        P("grp", "row"),
        P("row", None),
        P(),
        P("grp", "row", None),
        P("grp", "row", None),
        P("grp", "row", None),
        P(None, None, "grp"),
        P(None, None, "grp"),
        P(None, None, "grp"),
        P("grp", "row"),
    )
    out_specs = (
        P("grp", "row"),
        P("grp", "row"),
        P("grp", "row", None),
        P("grp", "row", None),
        P("grp", "row", None),
        P(None, None, "grp"),
        P(None, None, "grp"),
        P(None, None, "grp"),
    )
    return jax.shard_map(shards, mesh=mesh, in_specs=in_specs, out_specs=out_specs, check_vma=False)
```

```python
import functools
import math

import jax
import jax.numpy as jnp
import numpy as np
from jax import lax
from jax.experimental import pallas as pl
from jax.experimental.pallas import tpu as pltpu
from jax.sharding import PartitionSpec as P

HEADS = 12
LAYERS = 2
STEP = 7
BETA_ONE = 0.9
BETA_TWO = 0.999
LEARN_RATE = 0.1
VECTOR_RATE = 0.5
WEIGHT_DECAY = 0.01
ADAM_EPSILON = 1e-08
NORM_EPSILON = 1e-12
MASK_FILL = -1e30
AUG = 16
QUARTER = 128
LANES = 128
VMEM_LIMIT = 56 * 1024 * 1024
F32 = jnp.float32
BF16 = jnp.bfloat16


def CHUNKS(sequences):
    return [(sequences + 1) // 2, sequences // 2]


def nn(a, b):
    return lax.dot_general(a, b, (((1,), (0,)), ((), ())), preferred_element_type=F32)


def nt(a, b):
    return lax.dot_general(a, b, (((1,), (1,)), ((), ())), preferred_element_type=F32)


def tn(a, b):
    return lax.dot_general(a, b, (((0,), (0,)), ((), ())), preferred_element_type=F32)


def block_layout(groups, layers):
    counts = []
    block_matrix = []
    block_step = []
    for layer_index in range(layers):
        for matrix_type in range(6):
            amount = 1 if matrix_type < 3 else groups
            for position in range(amount):
                block_matrix.append(layer_index * 6 + matrix_type)
                block_step.append(position)
            counts.append(amount)
    return (
        np.array(counts, np.int32),
        np.array(block_matrix, np.int32),
        np.array(block_step, np.int32),
    )


def slot_index(owners, groups, layers, capacity):
    counts, block_matrix, block_step = block_layout(groups, layers)
    matrix_ids = jnp.arange(counts.shape[0], dtype=jnp.int32)
    same_owner = owners[:, None] == owners[None, :]
    earlier = matrix_ids[None, :] < matrix_ids[:, None]
    slot_of = jnp.sum(
        jnp.where(same_owner & earlier, jnp.asarray(counts, jnp.int32)[None, :], 0), axis=1
    )
    starts = owners * capacity + slot_of
    choose = (jnp.asarray(block_matrix, jnp.int32)[:, None] == matrix_ids[None, :]).astype(
        jnp.int32
    )
    return jnp.sum(choose * starts[None, :], axis=1) + jnp.asarray(block_step, jnp.int32)


def pack(square):
    half = square.shape[0] // 2
    return jnp.concatenate([square[:half], square[half:]], axis=1)


def unpack(packed):
    width = packed.shape[1] // 2
    return jnp.concatenate([packed[:, :width], packed[:, width:]], axis=0)


def lanes(value):
    total = value[:, :LANES]
    for at in range(LANES, value.shape[1], LANES):
        total = total + value[:, at : at + LANES]
    return total


def row_totals(value):
    return jnp.sum(lanes(value), axis=1, keepdims=True)


def accumulate(ref, index, value):
    first = pl.program_id(0) == 0

    @pl.when(first)
    def _():
        ref[index] = value

    @pl.when(jnp.logical_not(first))
    def _():
        ref[index] = ref[index] + value


def split3(value):
    high = value.astype(BF16)
    rest = value - high.astype(F32)
    mid = rest.astype(BF16)
    last = (rest - mid.astype(F32)).astype(BF16)
    return high, mid, last


def segment_rows(segs):
    row = lax.broadcasted_iota(jnp.int32, (AUG, segs.shape[1]), 0)
    same = row == segs
    query_rows = jnp.where(same | (row >= 4), 0.0, MASK_FILL)
    key_rows = jnp.where(same | ((row >= 4) & (row < 7)), 1.0, 0.0)
    return query_rows, key_rows.astype(BF16)


def with_rows(query_rows, value):
    high, mid, last = split3(-value)
    row = lax.broadcasted_iota(jnp.int32, query_rows.shape, 0)
    out = jnp.where(row == 4, high.astype(F32), query_rows)
    out = jnp.where(row == 5, mid.astype(F32), out)
    out = jnp.where(row == 6, last.astype(F32), out)
    return out.astype(BF16)


def norm_cdf(u):
    a = jnp.abs(u) * math.sqrt(0.5)
    t = 1.0 / (1.0 + 0.3275911 * a)
    bell = jnp.exp(-a * a)
    poly = t * (
        0.254829592
        + t * (-0.284496736 + t * (1.421413741 + t * (-1.453152027 + t * 1.061405429)))
    )
    tail = (0.5 * poly) * bell
    return jnp.where(u < 0, tail, 1.0 - tail), bell * (1.0 / math.sqrt(2.0 * math.pi))


def attend_body(first, per_group, groups, *refs):
    if first:
        x_ref, seg_ref, w_ref, vec_ref, qkv_ref, ctx_ref, lse_ref, sent = refs
    else:
        pieces, seg_ref, w_ref, vec_ref, x_ref, qkv_ref, ctx_ref, lse_ref, sent = refs
        for j in range(groups):
            x_ref[:, j * QUARTER : (j + 1) * QUARTER] = pieces[j]
    x = x_ref[...]
    width = x.shape[0]
    size = width // per_group
    vec = vec_ref[...]
    q = (nn(w_ref[0], x) + vec[:, 0:1]).astype(BF16)
    k = nn(w_ref[1], x).astype(BF16)
    v = (nn(w_ref[2], x) + vec[:, 1:2]).astype(BF16)
    qkv_ref[0:width] = q
    qkv_ref[width : 2 * width] = k
    qkv_ref[2 * width : 3 * width] = v
    query_rows, key_rows = segment_rows(seg_ref[0])
    query_rows = query_rows.astype(BF16)
    scale = size ** (-0.5)
    length = x.shape[1]
    tile = 256
    for h in range(per_group):
        part = slice(h * size, (h + 1) * size)
        qa = jnp.concatenate([q[part] * jnp.asarray(scale, BF16), query_rows], axis=0)
        ka = jnp.concatenate([k[part], key_rows], axis=0)
        for at in range(0, length, tile):
            cols = slice(at, at + tile)
            s = tn(ka, qa[:, cols])
            top = jnp.max(s, axis=0, keepdims=True)
            e = jnp.exp(s - top)
            total = jnp.sum(e, axis=0, keepdims=True)
            p = (e * (1.0 / total)).astype(BF16)
            ctx_ref[part, cols] = nn(v[part], p).astype(BF16)
            lse_ref[h : h + 1, cols] = top + jnp.log(total)
    for j in range(groups):
        sent[j] = ctx_ref[:, j * QUARTER : (j + 1) * QUARTER]


def attend_back_body(first, per_group, groups, follows, pieces, *refs):
    ctx_ref, qkv_ref, lse_ref, x_ref, seg_ref, w_ref = refs[:6]
    refs = refs[6 + follows :]
    if first:
        dx_ref, gqkv_ref, acc_ref, dctx_ref, gsum_ref, asum_ref = refs
    else:
        out_ref, sent, gqkv_ref, acc_ref, dctx_ref, gsum_ref, asum_ref, dx_ref = refs
    width, length = ctx_ref.shape
    size = width // per_group
    scale = size ** (-0.5)
    for j in range(groups):
        cols = slice(j * QUARTER, (j + 1) * QUARTER)
        dctx_ref[:, cols] = pieces[j, :width]
        if not first:
            out_ref[:, cols] = pieces[j, width:].astype(F32)
    ctx = ctx_ref[...]
    dctx = dctx_ref[...]
    x = x_ref[...]
    query_rows, key_rows = segment_rows(seg_ref[0])
    zero_rows = jnp.zeros_like(query_rows)
    q = qkv_ref[0:width]
    k = qkv_ref[width : 2 * width]
    v = qkv_ref[2 * width : 3 * width]
    dq, dk, dv = [], [], []
    for h in range(per_group):
        part = slice(h * size, (h + 1) * size)
        qh, kh, vh, dch = q[part], k[part], v[part], dctx[part]
        qs = qh * jnp.asarray(scale, BF16)
        delta = jnp.sum(dch.astype(F32) * ctx[part].astype(F32), axis=0, keepdims=True)
        qa = jnp.concatenate([qs, with_rows(query_rows, lse_ref[h : h + 1])], axis=0)
        ka = jnp.concatenate([kh, key_rows], axis=0)
        da = jnp.concatenate([dch, with_rows(zero_rows, delta)], axis=0)
        va = jnp.concatenate([vh, key_rows], axis=0)
        p = jnp.exp(tn(ka, qa))
        ds = (p * tn(va, da)).astype(BF16)
        dv.append(nt(dch, p.astype(BF16)))
        dq.append(nn(kh, ds) * scale)
        dk.append(nt(qs, ds))
    dq = jnp.concatenate(dq, axis=0)
    dk = jnp.concatenate(dk, axis=0)
    dv = jnp.concatenate(dv, axis=0)
    accumulate(asum_ref, 0, lanes(dq))
    accumulate(asum_ref, 1, lanes(dv))
    dx = None
    for at, grad in enumerate((dq, dk, dv)):
        low = grad.astype(BF16)
        accumulate(gsum_ref, at, nt(x, low))
        term = nn(w_ref[at], low)
        dx = term if dx is None else dx + term
    dx_ref[...] = dx
    for j in range(groups):
        cols = slice(j * QUARTER, (j + 1) * QUARTER)
        if first:
            dx_ref[:, cols] = dx_ref[:, cols] + pieces[j, width:].astype(F32)
        else:
            sent[j] = dx_ref[:, cols].astype(BF16)

    @pl.when(pl.program_id(0) == pl.num_programs(0) - 1)
    def _():
        for at in range(3):
            gqkv_ref[at] = pack(gsum_ref[at].astype(BF16))
        acc_ref[...] = jnp.concatenate(
            [jnp.sum(asum_ref[row], axis=1, keepdims=True) for row in range(2)], axis=1
        )


def norm(value):
    centre = jnp.mean(value, axis=0, keepdims=True)
    off = value - centre
    inverse = lax.rsqrt(jnp.mean(off * off, axis=0, keepdims=True) + NORM_EPSILON)
    return off * inverse, inverse


def norm_back(grad, gain, normed, inverse):
    e = grad * gain
    return inverse * (
        e - jnp.mean(e, axis=0, keepdims=True) - normed * jnp.mean(e * normed, axis=0, keepdims=True)
    )


def columns(vec_ref, row):
    return jnp.concatenate([vec_ref[a][:, row : row + 1] for a in range(vec_ref.shape[0])], axis=0)


def layer_forward(x, ctx, w, vec_ref, hid_ref, gp_ref):
    groups, width, nv = vec_ref.shape
    nup = nv - 8
    r1 = x + (nn(w["out_t"][...], ctx) + columns(vec_ref, 2))
    n1, i1 = norm(r1)
    y1 = n1 * columns(vec_ref, 4 + nup) + columns(vec_ref, 5 + nup)
    yl = y1.astype(BF16)
    branch = []
    for a in range(groups):
        own = yl[a * width : (a + 1) * width]
        for j in range(nup):
            rows = slice(j * width, (j + 1) * width)
            u = nn(w["up_t"][a, rows], own) + vec_ref[a][:, 3 + j : 4 + j]
            cdf, bell = norm_cdf(u)
            at = slice((a * nup + j) * width, (a * nup + j + 1) * width)
            hid_ref[at] = (u * cdf).astype(BF16)
            gp_ref[at] = (cdf + u * bell).astype(BF16)
        branch.append(nn(w["down_t"][a], hid_ref[a * nup * width : (a + 1) * nup * width]))
    r2 = y1 + (jnp.concatenate(branch, axis=0) + columns(vec_ref, 3 + nup))
    n2, i2 = norm(r2)
    x2 = n2 * columns(vec_ref, 6 + nup) + columns(vec_ref, 7 + nup)
    return x2, n1, i1, yl, n2, i2


def layer_backward(dy, ctx, w, vec_ref, n1, i1, yl, n2, i2, hid_ref, gp_ref, sums_out):
    put = sums_out.put
    groups, width, nv = vec_ref.shape
    nup = nv - 8
    hidden = nup * width
    sums = [None] * (nv - 2)
    sums[6 + nup - 2 + 0] = row_totals(dy * n2)
    sums[7 + nup - 2 + 0] = row_totals(dy)
    dz = norm_back(dy, columns(vec_ref, 6 + nup), n2, i2)
    sums[3 + nup - 2] = row_totals(dz)
    dzl = dz.astype(BF16)
    sums_out.ready()
    back = []
    bias = [[] for _ in range(nup)]
    for a in range(groups):
        own = slice(a * width, (a + 1) * width)
        total = None
        for j in range(nup):
            at = slice((a * nup + j) * width, (a * nup + j + 1) * width)
            rows = slice(j * width, (j + 1) * width)
            put(a, groups + nup + j, nt(hid_ref[at], dzl[own]))
            du = nn(w["down"][a, rows], dzl[own]) * gp_ref[at].astype(F32)
            bias[j].append(row_totals(du))
            dul = du.astype(BF16)
            put(a, groups + j, nt(yl[own], dul))
            term = nn(w["up"][a, :, rows], dul)
            total = term if total is None else total + term
        back.append(total)
        sums_out.send(a, groups, 2 * nup)
    for j in range(nup):
        sums[3 + j - 2] = jnp.concatenate(bias[j], axis=0)
    dy1 = dz + jnp.concatenate(back, axis=0)
    sums[4 + nup - 2] = row_totals(dy1 * n1)
    sums[5 + nup - 2] = row_totals(dy1)
    dr1 = norm_back(dy1, columns(vec_ref, 4 + nup), n1, i1)
    sums[0] = row_totals(dr1)
    dal = dr1.astype(BF16)
    dctx = nn(w["out"][...], dal).astype(BF16)
    for a in range(groups):
        own = nt(ctx[a * width : (a + 1) * width], dal)
        for b in range(groups):
            put(a, a ^ b, own[:, b * width : (b + 1) * width])
        sums_out.send(a, 0, groups)
    stack = jnp.concatenate(sums, axis=1)
    for a in range(groups):
        flat = jnp.concatenate(
            [stack[a * width : (a + 1) * width], jnp.zeros((width, LANES - len(sums)), F32)], axis=1
        ).T
        flat = flat[: width // 2]
        put(a, groups + 2 * nup, jnp.concatenate([flat, jnp.zeros_like(flat)], axis=1), packed=True)
        sums_out.send(a, groups + 2 * nup, 1)
    return dr1, dctx


WEIGHTS = ("out", "out_t", "up", "up_t", "down", "down_t")


class Fetched:
    def __init__(self, names, sources, places, sems):
        self.places = dict(zip(names, places))
        self.copies = {
            name: pltpu.make_async_copy(source, place, sems.at[at])
            for at, (name, source, place) in enumerate(zip(names, sources, places))
        }
        for copy in self.copies.values():
            copy.start()

    def __getitem__(self, name):
        copy = self.copies.pop(name, None)
        if copy is not None:
            copy.wait()
        return self.places[name]


class Sums:
    def __init__(self, me, core, keep_ref, give_ref, held_ref, before, sems):
        self.me, self.core, self.refs, self.held, self.sems = me, core, (keep_ref, give_ref), held_ref, sems
        self.run = keep_ref.shape[1]
        self.used, self.sent, self.loads, self.before = 0, [], [], before is not None
        if self.before:
            for a in range(held_ref.shape[0]):
                for side in range(2):
                    held = held_ref.at[a, pl.ds(side * self.run, self.run)]
                    self.loads.append(self.either(side, [ref.at[a ^ me] for ref in before], held, False))

    def either(self, side, places, held, out):
        sem = self.sems.at[self.used]
        self.used += 1
        keep, give = (
            pltpu.make_async_copy(held, place, sem) if out else pltpu.make_async_copy(place, held, sem)
            for place in places
        )
        pl.when(self.core == side)(keep.start)
        pl.when(self.core != side)(give.start)
        return keep

    def ready(self):
        for load in self.loads:
            load.wait()

    def put(self, a, j, block, packed=False):
        block = block if packed else pack(block)
        if self.before:
            block = block + self.held[a, j].astype(F32)
        self.held[a, j] = block.astype(BF16)

    def send(self, a, first, count):
        for side in range(2):
            low, high = max(first, side * self.run), min(first + count, (side + 1) * self.run)
            if low < high:
                part = pl.ds(low - side * self.run, high - low)
                places = [ref.at[a ^ self.me, part] for ref in self.refs]
                self.sent.append(self.either(side, places, self.held.at[a, pl.ds(low, high - low)], True))

    def finish(self):
        for copy in self.sent:
            copy.wait()


def joined(me, ref, rows=slice(None), cols=slice(None)):
    return jnp.concatenate([ref[a ^ me, rows, cols] for a in range(ref.shape[0])], axis=0)


def early_body(groups, first, count, me_ref, ctx_ref, x_ref, *refs):
    names = ("out_t", "up_t", "down_t")
    w_refs, vec_ref, sent = refs[:3], refs[3], refs[4]
    x2_ref, n1_ref, n2_ref, inv_ref, hid_ref, gp_ref = refs[5:11]
    w = Fetched(names, w_refs, refs[11:14], refs[14])
    me, width = me_ref[0], vec_ref.shape[1]
    start = joined(me, x_ref, cols=slice(first, first + count)).astype(F32)
    x2, n1, i1, _, n2, i2 = layer_forward(start, joined(me, ctx_ref), w, vec_ref, hid_ref, gp_ref)
    x2_ref[...] = x2
    for a in range(groups):
        sent[a ^ me] = x2[a * width : (a + 1) * width].astype(BF16)
    n1_ref[...] = n1.astype(BF16)
    n2_ref[...] = n2.astype(BF16)
    inv_ref[...] = jnp.concatenate([i1, i2], axis=0)


def middle_body(groups, first, count, follows, me_ref, core_ref, ctx_ref, cot_ref, x_ref, *refs):
    names = ("out_t", "up_t", "down_t", "down", "up", "out")
    w_refs, vec_ref, refs = refs[:6], refs[6], refs[7:]
    before = None
    if follows:
        before, refs = refs[:2], refs[2:]
    sent, dr_ref, keep_ref, give_ref, hid_ref, gp_ref, held_ref, grad_sems = refs[:8]
    w = Fetched(names, w_refs, refs[8:14], refs[14])
    me, width = me_ref[0], vec_ref.shape[1]
    sums_out = Sums(me, core_ref[0], keep_ref, give_ref, held_ref, before, grad_sems)
    ctx = joined(me, ctx_ref)
    x2, n1, i1, yl, n2, i2 = layer_forward(x_ref[...], ctx, w, vec_ref, hid_ref, gp_ref)
    for a in range(groups):
        sent[a ^ me, width:] = x2[a * width : (a + 1) * width].astype(BF16)
    dy = joined(me, cot_ref, cols=slice(first, first + count)).astype(F32)
    dr1, dctx = layer_backward(dy, ctx, w, vec_ref, n1, i1, yl, n2, i2, hid_ref, gp_ref, sums_out)
    dr_ref[...] = dr1
    for a in range(groups):
        sent[a ^ me, :width] = dctx[a * width : (a + 1) * width]
    sums_out.finish()


def late_body(groups, follows, me_ref, core_ref, got_ref, ctx_ref, *refs):
    names = ("down", "up", "out")
    dr_ref, n1_ref, n2_ref, inv_ref, hid_ref, gp_ref = refs[:6]
    w_refs, vec_ref, refs = refs[6:9], refs[9], refs[10:]
    before = None
    if follows:
        before, refs = refs[:2], refs[2:]
    sent, keep_ref, give_ref, held_ref, grad_sems = refs[:5]
    w = Fetched(names, w_refs, refs[5:8], refs[8])
    me, width = me_ref[0], vec_ref.shape[1]
    sums_out = Sums(me, core_ref[0], keep_ref, give_ref, held_ref, before, grad_sems)
    nup = vec_ref.shape[2] - 8
    dy = dr_ref[...] + joined(me, got_ref).astype(F32)
    n1, n2 = n1_ref[...].astype(F32), n2_ref[...].astype(F32)
    yl = (n1 * columns(vec_ref, 4 + nup) + columns(vec_ref, 5 + nup)).astype(BF16)
    inv = inv_ref[...]
    dr1, dctx = layer_backward(
        dy, joined(me, ctx_ref), w, vec_ref, n1, inv[0:1], yl, n2, inv[1:2], hid_ref, gp_ref, sums_out
    )
    for a in range(groups):
        sent[a ^ me, :width] = dctx[a * width : (a + 1) * width]
        sent[a ^ me, width:] = dr1[a * width : (a + 1) * width].astype(BF16)
    sums_out.finish()


def scatter_body(groups, *refs):
    for source, out in zip(refs[: len(refs) // 2], refs[len(refs) // 2 :]):
        for j in range(groups):
            out[j] = source[:, j * QUARTER : (j + 1) * QUARTER].astype(BF16)


def scatter_quarters(arrays, groups):
    width, tokens = arrays[0].shape
    length = QUARTER * groups
    count = tokens // length
    return pl.pallas_call(
        functools.partial(scatter_body, groups),
        grid=(count,),
        in_specs=[pl.BlockSpec((width, length), lambda i: (0, i))] * len(arrays),
        out_specs=[pl.BlockSpec((groups, width, QUARTER), lambda i: (0, 0, i))] * len(arrays),
        out_shape=[jax.ShapeDtypeStruct((groups, width, QUARTER * count), BF16)] * len(arrays),
        name="scatter_quarters",
    )(*arrays)


def pick_body(plain, turned, ids_ref, source, *refs):
    held, sems = refs[-2], refs[-1]
    count = held.shape[0]
    copies = []
    for at in range(count):
        copies.append(pltpu.make_async_copy(source.at[ids_ref[at]], held.at[at], sems.at[at]))
        copies[-1].start()
    for at in range(count):
        copies[at].wait()
        if plain:
            for copy in range(plain):
                refs[0][copy, at] = held[at]
        else:
            block = unpack(held[at])
            refs[0][at] = block
            if turned:
                refs[1][at] = block.T


def pick(ids, source, plain=0, turned=False):
    count = ids.shape[0]
    half, double = source.shape[1:]
    shape = (plain, count, half, double) if plain else (count, double // 2, double // 2)
    outs = 2 if turned else 1
    res = pl.pallas_call(
        functools.partial(pick_body, plain, turned),
        grid_spec=pltpu.PrefetchScalarGridSpec(
            num_scalar_prefetch=1,
            grid=(1,),
            in_specs=[pl.BlockSpec(memory_space=pltpu.HBM)],
            out_specs=[pl.BlockSpec(shape, lambda i, ids: (0,) * len(shape))] * outs,
            scratch_shapes=[pltpu.VMEM((count, half, double), BF16), pltpu.SemaphoreType.DMA((count,))],
        ),
        out_shape=[jax.ShapeDtypeStruct(shape, BF16)] * outs,
        name="pick",
    )(ids, source)
    return res if turned else res[0]


def arrange_body(groups, nup, core_ref, me_ref, *refs):
    w = dict(zip(WEIGHTS, refs[-6:]))
    got, other = refs[0], refs[1] if len(refs) == 8 else None
    me = me_ref[0]
    share = got.shape[1]
    width = got.shape[3] // 2
    even = core_ref[0] == 0

    def block(a, j):
        if other is None:
            return unpack(got[a ^ me, j])
        near, far = got[a ^ me, j % share], other[a ^ me, j % share]
        return unpack(jnp.where(even, near, far) if j < share else jnp.where(even, far, near))

    for a in range(groups):
        rows = slice(a * width, (a + 1) * width)
        line = [block(a, a ^ b) for b in range(groups)]
        w["out"][rows] = jnp.concatenate(line, axis=1)
        ups = [block(a, groups + j) for j in range(nup)]
        w["up"][a] = jnp.concatenate(ups, axis=1)
        w["up_t"][a] = jnp.concatenate([up.T for up in ups], axis=0)
        downs = [block(a, groups + nup + j) for j in range(nup)]
        w["down"][a] = jnp.concatenate(downs, axis=0)
        w["down_t"][a] = jnp.concatenate([down.T for down in downs], axis=1)
    for b in range(groups):
        w["out_t"][b * width : (b + 1) * width] = jnp.concatenate(
            [block(a, a ^ b).T for a in range(groups)], axis=1
        )


def collect_body(edges, ids_ref, *refs):
    out_ref = refs[-1]
    at = ids_ref[pl.program_id(0)]
    low = 0
    out_ref[...] = jnp.zeros_like(out_ref)
    for ref, high in zip(refs[:-1], edges):

        @pl.when((at >= low) & (at < high))
        def _(ref=ref):
            out_ref[0] = unpack(ref[0]).astype(F32)

        low = high


def collect(places, sources, width):
    specs, edges, low = [], [], 0
    for source in sources:
        count, size = source.shape[0], source.shape[1:]

        def index(i, ids, low=low, count=count):
            return (jnp.clip(ids[i] - low, 0, count - 1), 0, 0)

        specs.append(pl.BlockSpec((1, *size), index))
        low += count
        edges.append(low)
    slots = places.shape[0]
    return pl.pallas_call(
        functools.partial(collect_body, tuple(edges)),
        grid_spec=pltpu.PrefetchScalarGridSpec(
            num_scalar_prefetch=1,
            grid=(slots,),
            in_specs=specs,
            out_specs=pl.BlockSpec((1, width, width), lambda i, ids: (i, 0, 0)),
        ),
        out_shape=table(slots, width, width),
        name="collect",
    )(places, *sources)


def table(*shape):
    return jax.ShapeDtypeStruct(shape, F32)


class Line:
    token = None


HBM_SPEC = pl.BlockSpec(memory_space=pltpu.HBM)


def call(body, name, operands, outs, scalars=(), grid=None, specs=None, out_specs=None, scratch=(), aliases=None,
         flops=0, after=(), far=(), far_outs=()):
    behind = [array for array in (Line.token, *after) if array is not None]
    skip, ahead = len(behind), len(scalars)
    plain, made = body, len(outs)
    inputs = len(operands)
    whole = pl.BlockSpec(memory_space=pltpu.VMEM)

    def body(*refs):
        first, refs = refs[:ahead], refs[ahead + skip :]
        ins, results, rest = refs[:inputs], refs[inputs : inputs + made], refs[inputs + made + 1 :]
        refs[inputs + made][...] = jnp.zeros((8, LANES), F32)
        plain(*first, *ins, *results, *rest)

    any_spec = pl.BlockSpec(memory_space=pl.ANY)
    moved = sum(math.prod(array.shape) * array.dtype.itemsize for array in (*operands, *outs))
    common = dict(
        out_shape=[*outs, table(8, LANES)],
        name=name,
        input_output_aliases={at + ahead + skip: to for at, to in (aliases or {}).items()},
        compiler_params=pltpu.CompilerParams(vmem_limit_bytes=VMEM_LIMIT),
        cost_estimate=pl.CostEstimate(flops=int(flops), bytes_accessed=int(moved), transcendentals=0),
    )
    if grid is None:
        smem = pl.BlockSpec(memory_space=pltpu.SMEM)
        res = pl.pallas_call(
            body,
            in_specs=[smem] * ahead + [any_spec] * skip
            + [HBM_SPEC if at in far else whole for at in range(inputs)],
            out_specs=[HBM_SPEC if at in far_outs else whole for at in range(made)] + [whole],
            scratch_shapes=list(scratch),
            **common,
        )(*scalars, *behind, *operands)
    else:
        res = pl.pallas_call(
            body,
            grid_spec=pltpu.PrefetchScalarGridSpec(
                num_scalar_prefetch=ahead,
                grid=grid,
                in_specs=[any_spec] * skip + list(specs),
                out_specs=list(out_specs) + [pl.BlockSpec((8, LANES), lambda i, *s: (0, 0))],
                scratch_shapes=list(scratch),
            ),
            **common,
        )(*scalars, *behind, *operands)
    Line.token = res[-1]
    return list(res[:-1])


def peer(value, step, axis="grp"):
    count = lax.axis_size(axis)
    return lax.ppermute(value, axis, [(i, i ^ step) for i in range(count)])


def swap(parts, after=None):
    if after is not None:
        parts, _ = lax.optimization_barrier((parts, after))
    return lax.all_to_all(parts, "grp", split_axis=0, concat_axis=0)


def adam_step(param, grad, first, second, decay, rate):
    first_new = BETA_ONE * first + (1.0 - BETA_ONE) * grad
    second_new = BETA_TWO * second + (1.0 - BETA_TWO) * grad * grad
    first_hat = first_new / (1.0 - BETA_ONE**STEP)
    second_hat = second_new / (1.0 - BETA_TWO**STEP)
    updated = param - rate * (first_hat / (jnp.sqrt(second_hat) + ADAM_EPSILON) + decay * param)
    return (updated, first_new, second_new)


def shards(
    tokens,
    segments,
    owners,
    masters,
    first_moment,
    second_moment,
    vectors,
    vector_first,
    vector_second,
    cotangent,
):
    groups = lax.axis_size("grp")
    me = lax.axis_index("grp").astype(jnp.int32)
    own_row = lax.axis_index("row").astype(jnp.int32)
    core = lax.rem(own_row, 2)
    capacity = masters.shape[1]
    width, tokens_here = tokens.shape
    half = width // 2
    fg = groups * width
    sequences, length = segments.shape
    per_group = HEADS // groups
    nv = vectors.shape[1]
    nup = nv - 8
    per_layer = 3 + 3 * groups
    segs = segments.reshape(sequences, 1, length)
    order = jnp.arange(groups, dtype=jnp.int32) ^ me
    here, core_at = me.reshape(1), core.reshape(1)
    square = width * width

    block_index = slot_index(owners, groups, LAYERS, capacity)
    ids = block_index.reshape(LAYERS, per_layer)
    relative = jnp.take(ids[:, 3 : 3 + groups], order, axis=1, mode="clip")
    ids = jnp.concatenate([ids[:, :3], relative, ids[:, 3 + groups :]], axis=1)
    local_blocks = masters[0].astype(BF16).reshape(capacity, 2, half, width)
    local_blocks = jnp.concatenate([local_blocks[:, 0], local_blocks[:, 1]], axis=2)
    everyone = lax.all_gather(local_blocks, "row", axis=0, tiled=True)

    x_parts, cot_parts = (swap(part) for part in scatter_quarters([tokens, cotangent], groups))
    vec_all = jnp.stack([vectors] + [peer(vectors, k) for k in range(1, groups)]).transpose(1, 0, 3, 2)
    vecs = [vec_all[l] for l in range(LAYERS)]
    own_vecs = [vec_all[l, 0] for l in range(LAYERS)]

    share = (3 * groups) // 2
    w_qkv, w_turned, dense, exchanged = [None] * LAYERS, [None] * LAYERS, [None] * LAYERS, [None] * LAYERS

    def fetch(l, after=None):
        source, _ = lax.optimization_barrier((everyone, (vec_all, x_parts, cot_parts) if after is None else after))
        mine = ids[l, 3:] if l else lax.dynamic_slice(ids[l], (3 + core * share,), (share,))
        send = pick(mine, source, plain=1 if l else groups)
        w_qkv[l], w_turned[l] = pick(ids[l, :3], source, turned=True)
        if l == 0:
            exchanged[l] = swap(send)
        else:
            exchanged[l] = lax.all_gather(send[0], "grp", axis=0)

    def arrange(l):
        got = [exchanged[l]]
        if l == 0:
            got.append(peer(got[0], 1, "row"))
        shapes = [(fg, fg), (fg, fg), (groups, width, fg), (groups, fg, width), (groups, fg, width), (groups, width, fg)]
        smem, vmem = pl.BlockSpec(memory_space=pltpu.SMEM), pl.BlockSpec(memory_space=pltpu.VMEM)
        res = pl.pallas_call(
            functools.partial(arrange_body, groups, nup),
            in_specs=[smem, smem] + [vmem] * len(got),
            out_specs=[vmem] * 6,
            out_shape=[jax.ShapeDtypeStruct(shape, BF16) for shape in shapes],
            name="arrange",
            compiler_params=pltpu.CompilerParams(vmem_limit_bytes=VMEM_LIMIT),
        )(core_at, here, *got)
        dense[l] = dict(zip(WEIGHTS, res))

    def weight_places(names):
        shapes = {"out": (fg, fg), "up": (groups, width, fg), "down": (groups, fg, width)}
        shapes |= {"out_t": (fg, fg), "up_t": (groups, fg, width), "down_t": (groups, width, fg)}
        return [pltpu.VMEM(shapes[name], BF16) for name in names] + [pltpu.SemaphoreType.DMA((len(names),))]

    fetch(0)

    chunks, at = [], 0
    for count in CHUNKS(sequences):
        chunks.append((at, count))
        at += count
    keep = [dict() for _ in chunks]
    state = {"out": None, "grad": None}
    Line.token = None

    def tok(rows):
        return pl.BlockSpec((rows, length), lambda i, *s: (0, i))

    def quart(rows=width):
        return pl.BlockSpec((groups, rows, QUARTER), lambda i, *s: (0, 0, i))

    def parts(count, rows=width):
        return jax.ShapeDtypeStruct((groups, rows, count * QUARTER), BF16)

    def whole(*shape):
        return pl.BlockSpec(shape, lambda i, *s: (0,) * len(shape))

    def sent(c, key):
        return keep[c - 1][key] if c else None

    def attend(c, l):
        first, count = chunks[c]
        kp = keep[c]
        here_tokens = count * length
        shifted = pl.BlockSpec((width, length), lambda i, *s: (0, i + first))
        seg_spec = pl.BlockSpec((1, 1, length), lambda i, *s: (i + first, 0, 0))
        operands = [segs, w_turned[l], own_vecs[l]]
        specs = [seg_spec, whole(3, width, width), whole(width, nv)]
        outs = [jax.ShapeDtypeStruct((3 * width, here_tokens), BF16), jax.ShapeDtypeStruct((width, here_tokens), BF16),
                table(per_group, here_tokens)]
        out_specs = [tok(3 * width), tok(width), tok(per_group)]
        outs.append(parts(count))
        out_specs.append(quart())
        if l == 0:
            operands, specs = [tokens] + operands, [shifted] + specs
        else:
            operands, specs = [kp["x", l]] + operands, [quart()] + specs
            outs = [jax.ShapeDtypeStruct((width, here_tokens), BF16)] + outs
            out_specs = [tok(width)] + out_specs
        res = call(
            functools.partial(attend_body, l == 0, per_group, groups), "attend", operands, outs, (),
            (count,), specs, out_specs, flops=here_tokens * (6 * square + 4 * width * length),
        )
        if l:
            kp["xl", l] = res.pop(0)
        kp["qkv", l], kp["ctx", l], kp["lse", l] = res[:3]
        if l:
            kp["far", l] = swap(res[3], sent(c, ("far", l)))
        else:
            kp["parts"] = res[3]

    def early(c, l):
        first, count = chunks[c]
        kp = keep[c]
        n = count * QUARTER
        names = ("out_t", "up_t", "down_t")
        outs = [parts(count), table(fg, n), jax.ShapeDtypeStruct((fg, n), BF16), jax.ShapeDtypeStruct((fg, n), BF16),
                                 table(2, n), jax.ShapeDtypeStruct((groups * nup * width, n), BF16),
                                 jax.ShapeDtypeStruct((groups * nup * width, n), BF16)]
        res = call(
            functools.partial(early_body, groups, first * QUARTER, n), "early",
            [kp["far", l], x_parts, *(dense[l][name] for name in names), vecs[l]], outs, [here],
            scratch=weight_places(names), far=range(2, 5), after=[keep[-1]["far", 0]] if c == 0 else (),
            flops=2 * n * groups * square * (groups + 2 * nup),
        )
        kp["x", l + 1] = swap(res[0], sent(c, ("x", l + 1)))
        kp["res", l] = res[1]
        kp["kept", l] = res[2:]

    def grads_before(c, key):
        return [] if c == 0 else list(keep[c - 1][key])

    side_run = (3 * groups + 2) // 2
    stash = jax.ShapeDtypeStruct((groups, side_run, half, 2 * width), BF16)
    stash_places = [
        pltpu.VMEM((groups, 2 * side_run, half, 2 * width), BF16),
        pltpu.SemaphoreType.DMA((8 * groups,)),
    ]

    def middle(c, l):
        first, count = chunks[c]
        kp = keep[c]
        n = count * QUARTER
        before = grads_before(c, ("grads", l))
        hidden = pltpu.VMEM((groups * nup * width, n), BF16)
        names = ("out_t", "up_t", "down_t", "down", "up", "out")
        w_at = 3
        res = call(
            functools.partial(middle_body, groups, first * QUARTER, n, bool(before)), "middle",
            [kp["far", l], cot_parts, kp["res", l - 1], *(dense[l][name] for name in names), vecs[l], *before],
            [parts(count, 2 * width), table(fg, n), stash, stash], [here, core_at],
            scratch=[hidden, hidden, *stash_places, *weight_places(names)],
            far=[*range(w_at, w_at + 6), w_at + 7, w_at + 8], far_outs=[2, 3],
            flops=6 * n * groups * square * (groups + 2 * nup),
        )
        kp["dctx", l] = swap(res[0], sent(c, ("dctx", l)))
        kp["dr", l], kp["grads", l] = res[1], res[2:]

    def late(c, l):
        first, count = chunks[c]
        kp = keep[c]
        n = count * QUARTER
        before = grads_before(c, ("grads", l))
        names = ("down", "up", "out")
        w_at = 8
        res = call(
            functools.partial(late_body, groups, bool(before)), "late",
            [kp["dx", l + 1], kp["far", l], kp["dr", l + 1], *kp["kept", l],
             *(dense[l][name] for name in names), vecs[l], *before],
            [parts(count, 2 * width), stash, stash], [here, core_at],
            scratch=[*stash_places, *weight_places(names)],
            far=[*range(w_at, w_at + 3), w_at + 4, w_at + 5], far_outs=[1, 2],
            flops=4 * n * groups * square * (groups + 2 * nup),
        )
        kp["dctx", l] = swap(res[0], sent(c, ("dctx", l)))
        kp["grads", l] = res[1:]

    def attend_back(c, l):
        first, count = chunks[c]
        kp = keep[c]
        here_tokens = count * length
        shifted = pl.BlockSpec((width, length), lambda i, *s: (0, i + first))
        seg_spec = pl.BlockSpec((1, 1, length), lambda i, *s: (i + first, 0, 0))
        operands = [kp["dctx", l], kp["ctx", l], kp["qkv", l], kp["lse", l], tokens if l == 0 else kp["xl", l], segs,
                    w_qkv[l]]
        specs = [quart(2 * width), tok(width), tok(3 * width), tok(per_group), shifted if l == 0 else tok(width),
                                      seg_spec, whole(3, width, width)]
        outs = [jax.ShapeDtypeStruct((3, half, 2 * width), BF16), table(width, 2)]
        out_specs = [whole(3, half, 2 * width), whole(width, 2)]
        scratch = [pltpu.VMEM((width, length), BF16), pltpu.VMEM((3, width, width), F32),
                   pltpu.VMEM((2, width, LANES), F32)]
        name = "grad" if l == 0 else "out"
        aliases, follows = None, state[name] is not None
        if follows:
            aliases = {len(operands): 0}
            operands.append(state[name])
            specs.append(pl.BlockSpec(memory_space=pl.ANY))
        if l:
            outs = [parts(count)] + outs
            out_specs = [quart()] + out_specs
            scratch.append(pltpu.VMEM((width, length), F32))
        res = call(
            functools.partial(attend_back_body, l == 0, per_group, groups, follows), "attend_back", operands,
            [table(width, tokens_here)] + outs, (), (count,), specs, [shifted] + out_specs, scratch, aliases,
            here_tokens * (12 * square + 10 * width * length),
            after=[gate] if l == 0 and follows else (),
        )
        state[name] = res[0]
        if l:
            kp["dx", l] = swap(res[1], sent(c, ("dx", l)))
        kp["gqkv", l], kp["gvec", l] = res[-2:]

    def both(key, l):
        return sum(kp[key, l].astype(F32) for kp in keep)

    def scattered(l):
        kept, give = keep[-1]["grads", l]
        give, _ = lax.optimization_barrier((give, keep[0]["dctx", l]))
        got = peer(give, 1, "row")
        if l:
            return lax.psum_scatter(kept + got, "grp", scatter_dimension=0)

        def part(k):
            return lax.dynamic_index_in_dim(kept, me ^ k, 0, False) + lax.dynamic_index_in_dim(got, me ^ k, 0, False)

        return sum(peer(part(k), k).astype(F32) if k else part(k).astype(F32) for k in range(groups)).astype(BF16)

    def side_blocks(l, after=None):
        rows = jnp.pad(both("gvec", l).T, ((0, half - 2), (0, width)))
        all_four = jnp.concatenate([both("gqkv", l), rows[None]], axis=0).astype(BF16)
        if after is not None:
            all_four, _ = lax.optimization_barrier((all_four, after))
        mine = lax.dynamic_slice_in_dim(all_four, 2 * core, 2)
        return mine + peer(lax.dynamic_slice_in_dim(all_four, 2 - 2 * core, 2), 1, "row")

    class ChipSum:
        def __init__(self, value):
            self.shape = value.shape
            self.flat = value.reshape(-1, 2 * width)
            self.rows = self.flat.shape[0] // 2
            self.high = lax.rem(own_row // 2, 2)

        def first(self, after=None):
            give = lax.dynamic_slice_in_dim(self.flat, (1 - self.high) * self.rows, self.rows)
            if after is not None:
                give, _ = lax.optimization_barrier((give, after))
            got = peer(give, 2, "row")
            self.mine = lax.dynamic_slice_in_dim(self.flat, self.high * self.rows, self.rows) + got
            return got

        def second(self, after=None):
            got, step = None, 4
            while step < lax.axis_size("row"):
                give = self.mine
                if after is not None:
                    give, _ = lax.optimization_barrier((give, after))
                got = peer(give, step, "row")
                self.mine = self.mine + got
                step *= 2
            return got

        def third(self):
            return peer(self.mine, 2, "row")

        def whole(self, other):
            first = self.high == 0
            parts = [jnp.where(first, self.mine, other), jnp.where(first, other, self.mine)]
            return jnp.concatenate(parts, axis=0).reshape(self.shape)

        def all(self, after=None):
            self.first(after)
            self.second()
            return self.whole(self.third())

    assert LAYERS == 2
    count = len(chunks)
    ends = [None] * LAYERS

    def run(f, l):
        for c in range(count):
            f(c, l)

    run(attend, 0)
    ahead = (exchanged[0], Line.token)
    for kp in keep:
        kp["far", 0] = ahead = swap(kp["parts"], ahead)
    arrange(0)
    run(early, 0)
    fetch(1, keep[-1]["far", 0])
    run(attend, 1)
    arrange(1)
    run(middle, 1)
    run(attend_back, 1)
    chips = ChipSum(jnp.concatenate([scattered(1), side_blocks(1)], axis=0))
    run(late, 0)
    gate = chips.first(keep[0]["dctx", 0])
    big = ChipSum(scattered(0)).all()
    run(attend_back, 0)
    second = chips.second()
    third = chips.third()
    total = chips.whole(third)
    ends[1] = [total, peer(total, 1, "row")]
    total = jnp.concatenate([big, ChipSum(side_blocks(0, second)).all()], axis=0)
    ends[0] = [total, peer(total, 1, "row")]
    sources = ends[0] + ends[1]

    span = side_run + 2

    def places_of(side, at):
        return jnp.where(side == core, 0, span) + at

    j, i = jnp.arange(3 * groups, dtype=jnp.int32), jnp.arange(3, dtype=jnp.int32)
    one = jnp.concatenate([places_of(i // 2, side_run + i % 2), places_of(j // side_run, j % side_run)])
    places = (jnp.arange(LAYERS, dtype=jnp.int32)[:, None] * (2 * span) + one[None, :]).reshape(-1)
    targets = own_row * capacity + jnp.arange(capacity, dtype=jnp.int32)
    match = ids.reshape(-1)[None, :] == targets[:, None]
    place = jnp.sum(jnp.where(match, places[None, :], 0), axis=1)
    place = jnp.where(jnp.any(match, axis=1), place, 1 << 20).astype(jnp.int32)
    own_grads = collect(place, sources, width).reshape(1, capacity, square)

    def vector_rows(l):
        odd = jnp.where(core == 1, sources[2 * l], sources[2 * l + 1])
        rest = odd[3 * groups - side_run]
        return jnp.concatenate([odd[side_run + 1, :2, :width], rest[: nv - 2, :width]], axis=0).astype(F32)

    summed_vectors = jnp.stack([vector_rows(l) for l in range(LAYERS)], axis=0)
    new_masters, new_first, new_second = adam_step(
        masters, own_grads, first_moment, second_moment, WEIGHT_DECAY, LEARN_RATE
    )
    new_vectors, new_vector_first, new_vector_second = adam_step(
        vectors, summed_vectors, vector_first, vector_second, 0.0, VECTOR_RATE
    )
    return (
        state["out"],
        state["grad"],
        new_masters,
        new_first,
        new_second,
        new_vectors,
        new_vector_first,
        new_vector_second,
    )


def solution(mesh):
    in_specs = (
        P("grp", "row"),
        P("row", None),
        P(),
        P("grp", "row", None),
        P("grp", "row", None),
        P("grp", "row", None),
        P(None, None, "grp"),
        P(None, None, "grp"),
        P(None, None, "grp"),
        P("grp", "row"),
    )
    out_specs = (
        P("grp", "row"),
        P("grp", "row"),
        P("grp", "row", None),
        P("grp", "row", None),
        P("grp", "row", None),
        P(None, None, "grp"),
        P(None, None, "grp"),
        P(None, None, "grp"),
    )
    return jax.shard_map(shards, mesh=mesh, in_specs=in_specs, out_specs=out_specs, check_vma=False)
```

```python
import functools
import math

import jax
import jax.numpy as jnp
import numpy as np
from jax import lax
from jax.experimental import pallas as pl
from jax.experimental.pallas import tpu as pltpu
from jax.sharding import PartitionSpec as P

HEADS = 12
LAYERS = 2
STEP = 7
BETA_ONE = 0.9
BETA_TWO = 0.999
LEARN_RATE = 0.1
VECTOR_RATE = 0.5
WEIGHT_DECAY = 0.01
ADAM_EPSILON = 1e-08
NORM_EPSILON = 1e-12
MASK_FILL = -1e30
AUG = 16
QUARTER = 128
LANES = 128
VMEM_LIMIT = 56 * 1024 * 1024
VMEM_ATTEND = 56 * 1024 * 1024
F32 = jnp.float32
BF16 = jnp.bfloat16


def CHUNKS(sequences):
    return [(sequences + 1) // 2, sequences // 2]


def nn(a, b):
    return lax.dot_general(a, b, (((1,), (0,)), ((), ())), preferred_element_type=F32)


def nt(a, b):
    return lax.dot_general(a, b, (((1,), (1,)), ((), ())), preferred_element_type=F32)


def tn(a, b):
    return lax.dot_general(a, b, (((0,), (0,)), ((), ())), preferred_element_type=F32)


def block_layout(groups, layers):
    counts = []
    block_matrix = []
    block_step = []
    for layer_index in range(layers):
        for matrix_type in range(6):
            amount = 1 if matrix_type < 3 else groups
            for position in range(amount):
                block_matrix.append(layer_index * 6 + matrix_type)
                block_step.append(position)
            counts.append(amount)
    return (
        np.array(counts, np.int32),
        np.array(block_matrix, np.int32),
        np.array(block_step, np.int32),
    )


def slot_index(owners, groups, layers, capacity):
    counts, block_matrix, block_step = block_layout(groups, layers)
    matrix_ids = jnp.arange(counts.shape[0], dtype=jnp.int32)
    same_owner = owners[:, None] == owners[None, :]
    earlier = matrix_ids[None, :] < matrix_ids[:, None]
    slot_of = jnp.sum(
        jnp.where(same_owner & earlier, jnp.asarray(counts, jnp.int32)[None, :], 0), axis=1
    )
    starts = owners * capacity + slot_of
    choose = (jnp.asarray(block_matrix, jnp.int32)[:, None] == matrix_ids[None, :]).astype(
        jnp.int32
    )
    return jnp.sum(choose * starts[None, :], axis=1) + jnp.asarray(block_step, jnp.int32)


def pack(square):
    half = square.shape[0] // 2
    return jnp.concatenate([square[:half], square[half:]], axis=1)


def unpack(packed):
    width = packed.shape[1] // 2
    return jnp.concatenate([packed[:, :width], packed[:, width:]], axis=0)


def lanes(value):
    total = value[:, :LANES]
    for at in range(LANES, value.shape[1], LANES):
        total = total + value[:, at : at + LANES]
    return total


def row_totals(value):
    return jnp.sum(lanes(value), axis=1, keepdims=True)


def accumulate(ref, index, value):
    first = pl.program_id(0) == 0

    @pl.when(first)
    def _():
        ref[index] = value

    @pl.when(jnp.logical_not(first))
    def _():
        ref[index] = ref[index] + value


def split3(value):
    high = value.astype(BF16)
    rest = value - high.astype(F32)
    mid = rest.astype(BF16)
    last = (rest - mid.astype(F32)).astype(BF16)
    return high, mid, last


def segment_rows(segs):
    row = lax.broadcasted_iota(jnp.int32, (AUG, segs.shape[1]), 0)
    same = row == segs
    query_rows = jnp.where(same | (row >= 4), 0.0, MASK_FILL)
    key_rows = jnp.where(same | ((row >= 4) & (row < 7)), 1.0, 0.0)
    return query_rows, key_rows.astype(BF16)


def with_rows(query_rows, value):
    high, mid, last = split3(-value)
    row = lax.broadcasted_iota(jnp.int32, query_rows.shape, 0)
    out = jnp.where(row == 4, high.astype(F32), query_rows)
    out = jnp.where(row == 5, mid.astype(F32), out)
    out = jnp.where(row == 6, last.astype(F32), out)
    return out.astype(BF16)


def norm_cdf(u):
    a = jnp.abs(u) * math.sqrt(0.5)
    t = 1.0 / (1.0 + 0.3275911 * a)
    bell = jnp.exp(-a * a)
    poly = t * (
        0.254829592
        + t * (-0.284496736 + t * (1.421413741 + t * (-1.453152027 + t * 1.061405429)))
    )
    tail = (0.5 * poly) * bell
    return jnp.where(u < 0, tail, 1.0 - tail), bell * (1.0 / math.sqrt(2.0 * math.pi))


def attend_body(first, per_group, groups, *refs):
    if first:
        x_ref, seg_ref, w_ref, vec_ref, qkv_ref, ctx_ref, lse_ref, sent = refs
    else:
        pieces, seg_ref, w_ref, vec_ref, x_ref, qkv_ref, ctx_ref, lse_ref, sent = refs
        for j in range(groups):
            x_ref[:, j * QUARTER : (j + 1) * QUARTER] = pieces[j]
    x = x_ref[...]
    width = x.shape[0]
    size = width // per_group
    vec = vec_ref[...]
    q = (nn(w_ref[0], x) + vec[:, 0:1]).astype(BF16)
    k = nn(w_ref[1], x).astype(BF16)
    v = (nn(w_ref[2], x) + vec[:, 1:2]).astype(BF16)
    qkv_ref[0:width] = q
    qkv_ref[width : 2 * width] = k
    qkv_ref[2 * width : 3 * width] = v
    query_rows, key_rows = segment_rows(seg_ref[0])
    query_rows = query_rows.astype(BF16)
    parts = [slice(h * size, (h + 1) * size) for h in range(per_group)]
    scaled = q * jnp.asarray(size ** (-0.5), BF16)
    scores = [
        tn(jnp.concatenate([k[p], key_rows], axis=0), jnp.concatenate([scaled[p], query_rows], axis=0))
        for p in parts
    ]
    tops = [jnp.max(s, axis=0, keepdims=True) for s in scores]
    powers = [jnp.exp(s - top) for s, top in zip(scores, tops)]
    totals = [jnp.sum(e, axis=0, keepdims=True) for e in powers]
    chances = [(e * (1.0 / total)).astype(BF16) for e, total in zip(powers, totals)]
    for h, p in enumerate(parts):
        ctx_ref[p] = nn(v[p], chances[h]).astype(BF16)
        lse_ref[h : h + 1] = tops[h] + jnp.log(totals[h])
    for j in range(groups):
        sent[j] = ctx_ref[:, j * QUARTER : (j + 1) * QUARTER]


def attend_back_body(first, per_group, groups, follows, pieces, *refs):
    ctx_ref, qkv_ref, lse_ref, x_ref, seg_ref, w_ref = refs[:6]
    refs = refs[6 + follows :]
    if first:
        dx_ref, gqkv_ref, acc_ref, dctx_ref, gsum_ref, asum_ref = refs
    else:
        out_ref, sent, gqkv_ref, acc_ref, dctx_ref, gsum_ref, asum_ref, dx_ref = refs
    width, length = ctx_ref.shape
    size = width // per_group
    scale = size ** (-0.5)
    for j in range(groups):
        cols = slice(j * QUARTER, (j + 1) * QUARTER)
        dctx_ref[:, cols] = pieces[j, :width]
        if not first:
            out_ref[:, cols] = pieces[j, width:].astype(F32)
    ctx = ctx_ref[...]
    dctx = dctx_ref[...]
    x = x_ref[...]
    query_rows, key_rows = segment_rows(seg_ref[0])
    zero_rows = jnp.zeros_like(query_rows)
    q = qkv_ref[0:width]
    k = qkv_ref[width : 2 * width]
    v = qkv_ref[2 * width : 3 * width]
    dq, dk, dv = [], [], []
    for h in range(per_group):
        part = slice(h * size, (h + 1) * size)
        qh, kh, vh, dch = q[part], k[part], v[part], dctx[part]
        qs = qh * jnp.asarray(scale, BF16)
        delta = jnp.sum(dch.astype(F32) * ctx[part].astype(F32), axis=0, keepdims=True)
        qa = jnp.concatenate([qs, with_rows(query_rows, lse_ref[h : h + 1])], axis=0)
        ka = jnp.concatenate([kh, key_rows], axis=0)
        da = jnp.concatenate([dch, with_rows(zero_rows, delta)], axis=0)
        va = jnp.concatenate([vh, key_rows], axis=0)
        p = jnp.exp(tn(ka, qa))
        ds = (p * tn(va, da)).astype(BF16)
        dv.append(nt(dch, p.astype(BF16)))
        dq.append(nn(kh, ds) * scale)
        dk.append(nt(qs, ds))
    dq, dk, dv = (jnp.concatenate(parts, axis=0) for parts in (dq, dk, dv))
    accumulate(asum_ref, 0, lanes(dq))
    accumulate(asum_ref, 1, lanes(dv))
    low = jnp.concatenate([grad.astype(BF16) for grad in (dq, dk, dv)], axis=0)
    dx = nn(jnp.concatenate([w_ref[at] for at in range(3)], axis=1), low)
    grads = nt(x, low)
    for at in range(3):
        accumulate(gsum_ref, at, grads[:, at * width : (at + 1) * width])
    dx_ref[...] = dx
    for j in range(groups):
        cols = slice(j * QUARTER, (j + 1) * QUARTER)
        if first:
            dx_ref[:, cols] = dx_ref[:, cols] + pieces[j, width:].astype(F32)
        else:
            sent[j] = dx_ref[:, cols].astype(BF16)

    @pl.when(pl.program_id(0) == pl.num_programs(0) - 1)
    def _():
        for at in range(3):
            gqkv_ref[at] = pack(gsum_ref[at].astype(BF16))
        acc_ref[...] = jnp.concatenate(
            [jnp.sum(asum_ref[row], axis=1, keepdims=True) for row in range(2)], axis=1
        )


def norm(value):
    centre = jnp.mean(value, axis=0, keepdims=True)
    off = value - centre
    inverse = lax.rsqrt(jnp.mean(off * off, axis=0, keepdims=True) + NORM_EPSILON)
    return off * inverse, inverse


def norm_back(grad, gain, normed, inverse):
    e = grad * gain
    return inverse * (
        e - jnp.mean(e, axis=0, keepdims=True) - normed * jnp.mean(e * normed, axis=0, keepdims=True)
    )


def columns(vec_ref, row):
    return jnp.concatenate([vec_ref[a][:, row : row + 1] for a in range(vec_ref.shape[0])], axis=0)


def layer_forward(x, ctx, w, vec_ref, hid_ref, gp_ref, done=lambda a: None):
    groups, width, nv = vec_ref.shape
    nup = nv - 8
    r1 = x + (nn(w["out_t"][...], ctx) + columns(vec_ref, 2))
    n1, i1 = norm(r1)
    y1 = n1 * columns(vec_ref, 4 + nup) + columns(vec_ref, 5 + nup)
    yl = y1.astype(BF16)
    branch = []
    for a in range(groups):
        own = yl[a * width : (a + 1) * width]
        for j in range(nup):
            rows = slice(j * width, (j + 1) * width)
            u = nn(w["up_t"][a, rows], own) + vec_ref[a][:, 3 + j : 4 + j]
            cdf, bell = norm_cdf(u)
            at = slice((a * nup + j) * width, (a * nup + j + 1) * width)
            hid_ref[at] = (u * cdf).astype(BF16)
            gp_ref[at] = (cdf + u * bell).astype(BF16)
        done(a)
        branch.append(nn(w["down_t"][a], hid_ref[a * nup * width : (a + 1) * nup * width]))
    r2 = y1 + (jnp.concatenate(branch, axis=0) + columns(vec_ref, 3 + nup))
    n2, i2 = norm(r2)
    x2 = n2 * columns(vec_ref, 6 + nup) + columns(vec_ref, 7 + nup)
    return x2, n1, i1, yl, n2, i2


def layer_backward(dy, ctx, w, vec_ref, n1, i1, yl, n2, i2, hid_ref, gp_ref, sums_out, ready=lambda a: None):
    put = sums_out.put
    groups, width, nv = vec_ref.shape
    nup = nv - 8
    hidden = nup * width
    sums = [None] * (nv - 2)
    sums[6 + nup - 2 + 0] = row_totals(dy * n2)
    sums[7 + nup - 2 + 0] = row_totals(dy)
    dz = norm_back(dy, columns(vec_ref, 6 + nup), n2, i2)
    sums[3 + nup - 2] = row_totals(dz)
    dzl = dz.astype(BF16)
    sums_out.ready()
    back = []
    bias = [[] for _ in range(nup)]
    for a in range(groups):
        own = slice(a * width, (a + 1) * width)
        every = slice(a * nup * width, (a + 1) * nup * width)
        ready(a)
        grads = nt(hid_ref[every], dzl[own])
        dh = nn(w["down"][a], dzl[own])
        lows = []
        for j in range(nup):
            rows = slice(j * width, (j + 1) * width)
            put(a, groups + nup + j, grads[rows])
            du = dh[rows] * gp_ref[(a * nup + j) * width : (a * nup + j + 1) * width].astype(F32)
            bias[j].append(row_totals(du))
            lows.append(du.astype(BF16))
        dul = jnp.concatenate(lows, axis=0)
        grads = nt(yl[own], dul)
        for j in range(nup):
            put(a, groups + j, grads[:, j * width : (j + 1) * width])
        back.append(nn(w["up"][a], dul))
        sums_out.send(a, groups, 2 * nup)
    for j in range(nup):
        sums[3 + j - 2] = jnp.concatenate(bias[j], axis=0)
    dy1 = dz + jnp.concatenate(back, axis=0)
    sums[4 + nup - 2] = row_totals(dy1 * n1)
    sums[5 + nup - 2] = row_totals(dy1)
    dr1 = norm_back(dy1, columns(vec_ref, 4 + nup), n1, i1)
    sums[0] = row_totals(dr1)
    dal = dr1.astype(BF16)
    dctx = nn(w["out"][...], dal).astype(BF16)
    for a in range(groups):
        own = nt(ctx[a * width : (a + 1) * width], dal)
        for b in range(groups):
            put(a, a ^ b, own[:, b * width : (b + 1) * width])
        sums_out.send(a, 0, groups)
    stack = jnp.concatenate(sums, axis=1)
    for a in range(groups):
        flat = jnp.concatenate(
            [stack[a * width : (a + 1) * width], jnp.zeros((width, LANES - len(sums)), F32)], axis=1
        ).T
        flat = flat[: width // 2]
        put(a, groups + 2 * nup, jnp.concatenate([flat, jnp.zeros_like(flat)], axis=1), packed=True)
        sums_out.send(a, groups + 2 * nup, 1)
    return dr1, dctx


WEIGHTS = ("out", "out_t", "up", "up_t", "down", "down_t")


class Fetched:
    def __init__(self, names, sources, places, sems):
        self.places = dict(zip(names, places))
        self.copies = {
            name: pltpu.make_async_copy(source, place, sems.at[at])
            for at, (name, source, place) in enumerate(zip(names, sources, places))
        }
        for copy in self.copies.values():
            copy.start()

    def __getitem__(self, name):
        copy = self.copies.pop(name, None)
        if copy is not None:
            copy.wait()
        return self.places[name]


class Sums:
    def __init__(self, me, core, keep_ref, give_ref, held_ref, before, sems):
        self.me, self.core, self.refs, self.held, self.sems = me, core, (keep_ref, give_ref), held_ref, sems
        self.run = keep_ref.shape[1]
        self.used, self.sent, self.loads, self.before = 0, [], [], before is not None
        if self.before:
            for a in range(held_ref.shape[0]):
                for side in range(2):
                    held = held_ref.at[a, pl.ds(side * self.run, self.run)]
                    self.loads.append(self.either(side, [ref.at[a ^ me] for ref in before], held, False))

    def either(self, side, places, held, out):
        sem = self.sems.at[self.used]
        self.used += 1
        keep, give = (
            pltpu.make_async_copy(held, place, sem) if out else pltpu.make_async_copy(place, held, sem)
            for place in places
        )
        pl.when(self.core == side)(keep.start)
        pl.when(self.core != side)(give.start)
        return keep

    def ready(self):
        for load in self.loads:
            load.wait()

    def put(self, a, j, block, packed=False):
        block = block if packed else pack(block)
        if self.before:
            block = block + self.held[a, j].astype(F32)
        self.held[a, j] = block.astype(BF16)

    def send(self, a, first, count):
        for side in range(2):
            low, high = max(first, side * self.run), min(first + count, (side + 1) * self.run)
            if low < high:
                part = pl.ds(low - side * self.run, high - low)
                places = [ref.at[a ^ self.me, part] for ref in self.refs]
                self.sent.append(self.either(side, places, self.held.at[a, pl.ds(low, high - low)], True))

    def finish(self):
        for copy in self.sent:
            copy.wait()


def joined(me, ref, rows=slice(None), cols=slice(None)):
    return jnp.concatenate([ref[a ^ me, rows, cols] for a in range(ref.shape[0])], axis=0)


def early_body(groups, first, count, me_ref, ctx_ref, x_ref, *refs):
    names = ("out_t", "up_t", "down_t")
    w_refs, vec_ref, sent = refs[:3], refs[3], refs[4]
    x2_ref, n1_ref, n2_ref, inv_ref, far_hid, far_gp = refs[5:11]
    w = Fetched(names, w_refs, refs[11:14], refs[14])
    hid_ref, gp_ref, sems = refs[15:]
    me, width = me_ref[0], vec_ref.shape[1]
    copies = []

    def done(a):
        rows = pl.ds(a * (hid_ref.shape[0] // groups), hid_ref.shape[0] // groups)
        for ref, far in ((hid_ref, far_hid), (gp_ref, far_gp)):
            copies.append(pltpu.make_async_copy(ref.at[rows], far.at[rows], sems.at[len(copies)]))
            copies[-1].start()

    start = joined(me, x_ref, cols=slice(first, first + count)).astype(F32)
    x2, n1, i1, _, n2, i2 = layer_forward(start, joined(me, ctx_ref), w, vec_ref, hid_ref, gp_ref, done)
    x2_ref[...] = x2
    for a in range(groups):
        sent[a ^ me] = x2[a * width : (a + 1) * width].astype(BF16)
    n1_ref[...] = n1.astype(BF16)
    n2_ref[...] = n2.astype(BF16)
    inv_ref[...] = jnp.concatenate([i1, i2], axis=0)
    for copy in copies:
        copy.wait()


def middle_body(groups, first, count, follows, me_ref, core_ref, ctx_ref, cot_ref, x_ref, *refs):
    names = ("out_t", "up_t", "down_t", "down", "up", "out")
    w_refs, vec_ref, refs = refs[:6], refs[6], refs[7:]
    before = None
    if follows:
        before, refs = refs[:2], refs[2:]
    sent, dr_ref, keep_ref, give_ref, hid_ref, gp_ref, held_ref, grad_sems = refs[:8]
    w = Fetched(names, w_refs, refs[8:14], refs[14])
    me, width = me_ref[0], vec_ref.shape[1]
    sums_out = Sums(me, core_ref[0], keep_ref, give_ref, held_ref, before, grad_sems)
    ctx = joined(me, ctx_ref)
    x2, n1, i1, yl, n2, i2 = layer_forward(x_ref[...], ctx, w, vec_ref, hid_ref, gp_ref)
    for a in range(groups):
        sent[a ^ me, width:] = x2[a * width : (a + 1) * width].astype(BF16)
    dy = joined(me, cot_ref, cols=slice(first, first + count)).astype(F32)
    dr1, dctx = layer_backward(dy, ctx, w, vec_ref, n1, i1, yl, n2, i2, hid_ref, gp_ref, sums_out)
    dr_ref[...] = dr1
    for a in range(groups):
        sent[a ^ me, :width] = dctx[a * width : (a + 1) * width]
    sums_out.finish()


def late_body(groups, follows, me_ref, core_ref, got_ref, ctx_ref, *refs):
    names = ("down", "up", "out")
    dr_ref, n1_ref, n2_ref, inv_ref, far_hid, far_gp = refs[:6]
    w_refs, vec_ref, refs = refs[6:9], refs[9], refs[10:]
    before = None
    if follows:
        before, refs = refs[:2], refs[2:]
    sent, keep_ref, give_ref, held_ref, grad_sems = refs[:5]
    w = Fetched(names, w_refs, refs[5:8], refs[8])
    hid_ref, gp_ref, sems = refs[9:]
    copies = []
    for a in range(groups):
        rows = pl.ds(a * (hid_ref.shape[0] // groups), hid_ref.shape[0] // groups)
        for ref, far in ((hid_ref, far_hid), (gp_ref, far_gp)):
            copies.append(pltpu.make_async_copy(far.at[rows], ref.at[rows], sems.at[len(copies)]))
            copies[-1].start()

    def ready(a):
        copies[2 * a].wait()
        copies[2 * a + 1].wait()

    me, width = me_ref[0], vec_ref.shape[1]
    sums_out = Sums(me, core_ref[0], keep_ref, give_ref, held_ref, before, grad_sems)
    nup = vec_ref.shape[2] - 8
    dy = dr_ref[...] + joined(me, got_ref).astype(F32)
    n1, n2 = n1_ref[...].astype(F32), n2_ref[...].astype(F32)
    yl = (n1 * columns(vec_ref, 4 + nup) + columns(vec_ref, 5 + nup)).astype(BF16)
    inv = inv_ref[...]
    dr1, dctx = layer_backward(
        dy, joined(me, ctx_ref), w, vec_ref, n1, inv[0:1], yl, n2, inv[1:2], hid_ref, gp_ref, sums_out, ready
    )
    for a in range(groups):
        sent[a ^ me, :width] = dctx[a * width : (a + 1) * width]
        sent[a ^ me, width:] = dr1[a * width : (a + 1) * width].astype(BF16)
    sums_out.finish()


def scatter_body(groups, *refs):
    for source, out in zip(refs[: len(refs) // 2], refs[len(refs) // 2 :]):
        for j in range(groups):
            out[j] = source[:, j * QUARTER : (j + 1) * QUARTER].astype(BF16)


def scatter_quarters(arrays, groups):
    width, tokens = arrays[0].shape
    length = QUARTER * groups
    count = tokens // length
    return pl.pallas_call(
        functools.partial(scatter_body, groups),
        grid=(count,),
        in_specs=[pl.BlockSpec((width, length), lambda i: (0, i))] * len(arrays),
        out_specs=[pl.BlockSpec((groups, width, QUARTER), lambda i: (0, 0, i))] * len(arrays),
        out_shape=[jax.ShapeDtypeStruct((groups, width, QUARTER * count), BF16)] * len(arrays),
        name="scatter_quarters",
    )(*arrays)


def pick_body(plain, turned, ids_ref, source, *refs):
    held, sems = refs[-2], refs[-1]
    count = held.shape[0]
    copies = []
    for at in range(count):
        copies.append(pltpu.make_async_copy(source.at[ids_ref[at]], held.at[at], sems.at[at]))
        copies[-1].start()
    for at in range(count):
        copies[at].wait()
        if plain:
            for copy in range(plain):
                refs[0][copy, at] = held[at]
        else:
            block = unpack(held[at])
            refs[0][at] = block
            if turned:
                refs[1][at] = block.T


def pick(ids, source, plain=0, turned=False):
    count = ids.shape[0]
    half, double = source.shape[1:]
    shape = (plain, count, half, double) if plain else (count, double // 2, double // 2)
    outs = 2 if turned else 1
    res = pl.pallas_call(
        functools.partial(pick_body, plain, turned),
        grid_spec=pltpu.PrefetchScalarGridSpec(
            num_scalar_prefetch=1,
            grid=(1,),
            in_specs=[pl.BlockSpec(memory_space=pltpu.HBM)],
            out_specs=[pl.BlockSpec(shape, lambda i, ids: (0,) * len(shape))] * outs,
            scratch_shapes=[pltpu.VMEM((count, half, double), BF16), pltpu.SemaphoreType.DMA((count,))],
        ),
        out_shape=[jax.ShapeDtypeStruct(shape, BF16)] * outs,
        name="pick",
    )(ids, source)
    return res if turned else res[0]


def arrange_body(groups, nup, core_ref, me_ref, *refs):
    w = dict(zip(WEIGHTS, refs[-6:]))
    got, other = refs[0], refs[1] if len(refs) == 8 else None
    me = me_ref[0]
    share = got.shape[1]
    width = got.shape[3] // 2
    even = core_ref[0] == 0

    def block(a, j):
        if other is None:
            return unpack(got[a ^ me, j])
        near, far = got[a ^ me, j % share], other[a ^ me, j % share]
        return unpack(jnp.where(even, near, far) if j < share else jnp.where(even, far, near))

    for a in range(groups):
        rows = slice(a * width, (a + 1) * width)
        line = [block(a, a ^ b) for b in range(groups)]
        w["out"][rows] = jnp.concatenate(line, axis=1)
        ups = [block(a, groups + j) for j in range(nup)]
        w["up"][a] = jnp.concatenate(ups, axis=1)
        w["up_t"][a] = jnp.concatenate([up.T for up in ups], axis=0)
        downs = [block(a, groups + nup + j) for j in range(nup)]
        w["down"][a] = jnp.concatenate(downs, axis=0)
        w["down_t"][a] = jnp.concatenate([down.T for down in downs], axis=1)
    for b in range(groups):
        w["out_t"][b * width : (b + 1) * width] = jnp.concatenate(
            [block(a, a ^ b).T for a in range(groups)], axis=1
        )


def collect_body(edges, ids_ref, *refs):
    sources, out_ref, held, sems = refs[: len(edges)], refs[-3], refs[-2], refs[-1]
    slots = out_ref.shape[0]
    for slot in range(slots):
        at, low = ids_ref[slot], 0
        for source, high in zip(sources, edges):

            @pl.when((at >= low) & (at < high))
            def _(source=source, place=at - low, slot=slot):
                pltpu.make_async_copy(source.at[place], held.at[slot], sems.at[slot]).start()

            low = high
    for slot in range(slots):
        there = ids_ref[slot] < edges[-1]

        @pl.when(there)
        def _(slot=slot):
            pltpu.make_async_copy(sources[0].at[0], held.at[slot], sems.at[slot]).wait()
            out_ref[slot] = unpack(held[slot]).astype(F32)

        @pl.when(jnp.logical_not(there))
        def _(slot=slot):
            out_ref[slot] = jnp.zeros(out_ref.shape[1:], F32)


def collect(places, sources, width):
    edges = tuple(int(edge) for edge in np.cumsum([source.shape[0] for source in sources]))
    slots, size = places.shape[0], sources[0].shape[1:]
    return pl.pallas_call(
        functools.partial(collect_body, edges),
        grid_spec=pltpu.PrefetchScalarGridSpec(
            num_scalar_prefetch=1,
            grid=(1,),
            in_specs=[HBM_SPEC] * len(sources),
            out_specs=pl.BlockSpec((slots, width, width), lambda i, ids: (0, 0, 0)),
            scratch_shapes=[pltpu.VMEM((slots, *size), BF16), pltpu.SemaphoreType.DMA((slots,))],
        ),
        out_shape=table(slots, width, width),
        name="collect",
    )(places, *sources)


def table(*shape):
    return jax.ShapeDtypeStruct(shape, F32)


class Line:
    token = None


HBM_SPEC = pl.BlockSpec(memory_space=pltpu.HBM)


def call(body, name, operands, outs, scalars=(), grid=None, specs=None, out_specs=None, scratch=(), aliases=None,
         flops=0, after=(), far=(), far_outs=(), vmem=VMEM_LIMIT):
    behind = [array for array in (Line.token, *after) if array is not None]
    skip, ahead = len(behind), len(scalars)
    plain, made = body, len(outs)
    inputs = len(operands)
    whole = pl.BlockSpec(memory_space=pltpu.VMEM)

    def body(*refs):
        first, refs = refs[:ahead], refs[ahead + skip :]
        ins, results, rest = refs[:inputs], refs[inputs : inputs + made], refs[inputs + made + 1 :]
        refs[inputs + made][...] = jnp.zeros((8, LANES), F32)
        plain(*first, *ins, *results, *rest)

    any_spec = pl.BlockSpec(memory_space=pl.ANY)
    moved = sum(math.prod(array.shape) * array.dtype.itemsize for array in (*operands, *outs))
    common = dict(
        out_shape=[*outs, table(8, LANES)],
        name=name,
        input_output_aliases={at + ahead + skip: to for at, to in (aliases or {}).items()},
        compiler_params=pltpu.CompilerParams(vmem_limit_bytes=vmem),
        cost_estimate=pl.CostEstimate(flops=int(flops), bytes_accessed=int(moved), transcendentals=0),
    )
    if grid is None:
        smem = pl.BlockSpec(memory_space=pltpu.SMEM)
        res = pl.pallas_call(
            body,
            in_specs=[smem] * ahead + [any_spec] * skip
            + [HBM_SPEC if at in far else whole for at in range(inputs)],
            out_specs=[HBM_SPEC if at in far_outs else whole for at in range(made)] + [whole],
            scratch_shapes=list(scratch),
            **common,
        )(*scalars, *behind, *operands)
    else:
        res = pl.pallas_call(
            body,
            grid_spec=pltpu.PrefetchScalarGridSpec(
                num_scalar_prefetch=ahead,
                grid=grid,
                in_specs=[any_spec] * skip + list(specs),
                out_specs=list(out_specs) + [pl.BlockSpec((8, LANES), lambda i, *s: (0, 0))],
                scratch_shapes=list(scratch),
            ),
            **common,
        )(*scalars, *behind, *operands)
    Line.token = res[-1]
    return list(res[:-1])


def peer(value, step, axis="grp"):
    count = lax.axis_size(axis)
    return lax.ppermute(value, axis, [(i, i ^ step) for i in range(count)])


def swap(parts, after=None):
    if after is not None:
        parts, _ = lax.optimization_barrier((parts, after))
    return lax.all_to_all(parts, "grp", split_axis=0, concat_axis=0)


def adam_step(param, grad, first, second, decay, rate):
    first_new = BETA_ONE * first + (1.0 - BETA_ONE) * grad
    second_new = BETA_TWO * second + (1.0 - BETA_TWO) * grad * grad
    first_hat = first_new / (1.0 - BETA_ONE**STEP)
    second_hat = second_new / (1.0 - BETA_TWO**STEP)
    updated = param - rate * (first_hat / (jnp.sqrt(second_hat) + ADAM_EPSILON) + decay * param)
    return (updated, first_new, second_new)


def shards(
    tokens,
    segments,
    owners,
    masters,
    first_moment,
    second_moment,
    vectors,
    vector_first,
    vector_second,
    cotangent,
):
    groups = lax.axis_size("grp")
    me = lax.axis_index("grp").astype(jnp.int32)
    own_row = lax.axis_index("row").astype(jnp.int32)
    core = lax.rem(own_row, 2)
    capacity = masters.shape[1]
    width, tokens_here = tokens.shape
    half = width // 2
    fg = groups * width
    sequences, length = segments.shape
    per_group = HEADS // groups
    nv = vectors.shape[1]
    nup = nv - 8
    per_layer = 3 + 3 * groups
    segs = segments.reshape(sequences, 1, length)
    order = jnp.arange(groups, dtype=jnp.int32) ^ me
    here, core_at = me.reshape(1), core.reshape(1)
    square = width * width

    block_index = slot_index(owners, groups, LAYERS, capacity)
    ids = block_index.reshape(LAYERS, per_layer)
    relative = jnp.take(ids[:, 3 : 3 + groups], order, axis=1, mode="clip")
    ids = jnp.concatenate([ids[:, :3], relative, ids[:, 3 + groups :]], axis=1)
    local_blocks = masters[0].astype(BF16).reshape(capacity, 2, half, width)
    local_blocks = jnp.concatenate([local_blocks[:, 0], local_blocks[:, 1]], axis=2)
    everyone = lax.all_gather(local_blocks, "row", axis=0, tiled=True)

    x_parts, cot_parts = (swap(part) for part in scatter_quarters([tokens, cotangent], groups))
    vec_all = jnp.stack([vectors] + [peer(vectors, k) for k in range(1, groups)]).transpose(1, 0, 3, 2)
    vecs = [vec_all[l] for l in range(LAYERS)]
    own_vecs = [vec_all[l, 0] for l in range(LAYERS)]

    share = (3 * groups) // 2
    w_qkv, w_turned, dense, exchanged = [None] * LAYERS, [None] * LAYERS, [None] * LAYERS, [None] * LAYERS

    def fetch(l, after=None):
        source, _ = lax.optimization_barrier((everyone, (vec_all, x_parts, cot_parts) if after is None else after))
        mine = ids[l, 3:] if l else lax.dynamic_slice(ids[l], (3 + core * share,), (share,))
        send = pick(mine, source, plain=1 if l else groups)
        w_qkv[l], w_turned[l] = pick(ids[l, :3], source, turned=True)
        if l == 0:
            exchanged[l] = [swap(send)]
        else:
            exchanged[l] = [lax.all_gather(send[0], "grp", axis=0)]

    def arrange(l):
        got = exchanged[l]
        shapes = [(fg, fg), (fg, fg), (groups, width, fg), (groups, fg, width), (groups, fg, width), (groups, width, fg)]
        smem, vmem = pl.BlockSpec(memory_space=pltpu.SMEM), pl.BlockSpec(memory_space=pltpu.VMEM)
        res = pl.pallas_call(
            functools.partial(arrange_body, groups, nup),
            in_specs=[smem, smem] + [vmem] * len(got),
            out_specs=[vmem] * 6,
            out_shape=[pltpu.HBM(shape, BF16) for shape in shapes],
            name="arrange",
            compiler_params=pltpu.CompilerParams(vmem_limit_bytes=VMEM_LIMIT),
        )(core_at, here, *got)
        dense[l] = dict(zip(WEIGHTS, res))

    def weight_places(names):
        shapes = {"out": (fg, fg), "up": (groups, width, fg), "down": (groups, fg, width)}
        shapes |= {"out_t": (fg, fg), "up_t": (groups, fg, width), "down_t": (groups, width, fg)}
        return [pltpu.VMEM(shapes[name], BF16) for name in names] + [pltpu.SemaphoreType.DMA((len(names),))]

    fetch(0)

    chunks, at = [], 0
    for count in CHUNKS(sequences):
        chunks.append((at, count))
        at += count
    keep = [dict() for _ in chunks]
    state = {"out": None, "grad": None}
    Line.token = None

    def tok(rows):
        return pl.BlockSpec((rows, length), lambda i, *s: (0, i))

    def quart(rows=width):
        return pl.BlockSpec((groups, rows, QUARTER), lambda i, *s: (0, 0, i))

    def parts(count, rows=width):
        return jax.ShapeDtypeStruct((groups, rows, count * QUARTER), BF16)

    def whole(*shape):
        return pl.BlockSpec(shape, lambda i, *s: (0,) * len(shape))

    def sent(c, key):
        return keep[c - 1][key] if c else None

    def attend(c, l):
        first, count = chunks[c]
        kp = keep[c]
        here_tokens = count * length
        shifted = pl.BlockSpec((width, length), lambda i, *s: (0, i + first))
        seg_spec = pl.BlockSpec((1, 1, length), lambda i, *s: (i + first, 0, 0))
        operands = [segs, w_turned[l], own_vecs[l]]
        specs = [seg_spec, whole(3, width, width), whole(width, nv)]
        outs = [pltpu.HBM((3 * width, here_tokens), BF16), pltpu.HBM((width, here_tokens), BF16),
                pltpu.HBM((per_group, here_tokens), F32)]
        out_specs = [tok(3 * width), tok(width), tok(per_group)]
        outs.append(parts(count))
        out_specs.append(quart())
        if l == 0:
            operands, specs = [tokens] + operands, [shifted] + specs
        else:
            operands, specs = [kp["x", l]] + operands, [quart()] + specs
            outs = [pltpu.HBM((width, here_tokens), BF16)] + outs
            out_specs = [tok(width)] + out_specs
        res = call(
            functools.partial(attend_body, l == 0, per_group, groups), "attend", operands, outs, (),
            (count,), specs, out_specs, flops=here_tokens * (6 * square + 4 * width * length), vmem=VMEM_ATTEND,
        )
        if l:
            kp["xl", l] = res.pop(0)
        kp["qkv", l], kp["ctx", l], kp["lse", l] = res[:3]
        if l:
            kp["far", l] = swap(res[3], sent(c, ("far", l)))
        else:
            kp["parts"] = res[3]

    def early(c, l):
        first, count = chunks[c]
        kp = keep[c]
        n = count * QUARTER
        names = ("out_t", "up_t", "down_t")
        hidden = pltpu.VMEM((groups * nup * width, n), BF16)
        outs = [parts(count), pltpu.HBM((fg, n), F32), pltpu.HBM((fg, n), BF16), pltpu.HBM((fg, n), BF16),
                pltpu.HBM((2, n), F32)] + [pltpu.HBM((groups * nup * width, n), BF16)] * 2
        res = call(
            functools.partial(early_body, groups, first * QUARTER, n), "early",
            [kp["far", l], x_parts, *(dense[l][name] for name in names), vecs[l]], outs, [here],
            scratch=[*weight_places(names), hidden, hidden, pltpu.SemaphoreType.DMA((2 * groups,))],
            far=range(2, 5), far_outs=[5, 6],
            flops=2 * n * groups * square * (groups + 2 * nup),
        )
        kp["x", l + 1] = swap(res[0], sent(c, ("x", l + 1)))
        kp["res", l] = res[1]
        kp["kept", l] = res[2:]

    def grads_before(c, key):
        return [] if c == 0 else list(keep[c - 1][key])

    side_run = (3 * groups + 2) // 2
    stash = pltpu.HBM((groups, side_run, half, 2 * width), BF16)
    stash_places = [
        pltpu.VMEM((groups, 2 * side_run, half, 2 * width), BF16),
        pltpu.SemaphoreType.DMA((8 * groups,)),
    ]

    def middle(c, l):
        first, count = chunks[c]
        kp = keep[c]
        n = count * QUARTER
        before = grads_before(c, ("grads", l))
        hidden = pltpu.VMEM((groups * nup * width, n), BF16)
        names = ("out_t", "up_t", "down_t", "down", "up", "out")
        w_at = 3
        res = call(
            functools.partial(middle_body, groups, first * QUARTER, n, bool(before)), "middle",
            [kp["far", l], cot_parts, kp["res", l - 1], *(dense[l][name] for name in names), vecs[l], *before],
            [parts(count, 2 * width), pltpu.HBM((fg, n), F32), stash, stash], [here, core_at],
            scratch=[hidden, hidden, *stash_places, *weight_places(names)],
            far=[*range(w_at, w_at + 6), w_at + 7, w_at + 8], far_outs=[2, 3],
            flops=6 * n * groups * square * (groups + 2 * nup),
        )
        kp["dctx", l] = swap(res[0], sent(c, ("dctx", l)))
        kp["dr", l], kp["grads", l] = res[1], res[2:]

    def late(c, l):
        first, count = chunks[c]
        kp = keep[c]
        n = count * QUARTER
        before = grads_before(c, ("grads", l))
        names = ("down", "up", "out")
        w_at = 8
        hidden = pltpu.VMEM((groups * nup * width, n), BF16)
        res = call(
            functools.partial(late_body, groups, bool(before)), "late",
            [kp["dx", l + 1], kp["far", l], kp["dr", l + 1], *kp["kept", l],
             *(dense[l][name] for name in names), vecs[l], *before],
            [parts(count, 2 * width), stash, stash], [here, core_at],
            scratch=[*stash_places, *weight_places(names), hidden, hidden, pltpu.SemaphoreType.DMA((2 * groups,))],
            far=[w_at - 2, w_at - 1, *range(w_at, w_at + 3), w_at + 4, w_at + 5], far_outs=[1, 2],
            flops=4 * n * groups * square * (groups + 2 * nup),
        )
        kp["dctx", l] = swap(res[0], sent(c, ("dctx", l)))
        kp["grads", l] = res[1:]

    def attend_back(c, l):
        first, count = chunks[c]
        kp = keep[c]
        here_tokens = count * length
        shifted = pl.BlockSpec((width, length), lambda i, *s: (0, i + first))
        seg_spec = pl.BlockSpec((1, 1, length), lambda i, *s: (i + first, 0, 0))
        operands = [kp["dctx", l], kp["ctx", l], kp["qkv", l], kp["lse", l], tokens if l == 0 else kp["xl", l], segs,
                    w_qkv[l]]
        specs = [quart(2 * width), tok(width), tok(3 * width), tok(per_group), shifted if l == 0 else tok(width),
                                      seg_spec, whole(3, width, width)]
        outs = [jax.ShapeDtypeStruct((3, half, 2 * width), BF16), table(width, 2)]
        out_specs = [whole(3, half, 2 * width), whole(width, 2)]
        scratch = [pltpu.VMEM((width, length), BF16), pltpu.VMEM((3, width, width), F32),
                   pltpu.VMEM((2, width, LANES), F32)]
        name = "grad" if l == 0 else "out"
        aliases, follows = None, state[name] is not None
        if follows:
            aliases = {len(operands): 0}
            operands.append(state[name])
            specs.append(pl.BlockSpec(memory_space=pl.ANY))
        if l:
            outs = [parts(count)] + outs
            out_specs = [quart()] + out_specs
            scratch.append(pltpu.VMEM((width, length), F32))
        res = call(
            functools.partial(attend_back_body, l == 0, per_group, groups, follows), "attend_back", operands,
            [table(width, tokens_here)] + outs, (), (count,), specs, [shifted] + out_specs, scratch, aliases,
            here_tokens * (12 * square + 10 * width * length),
            after=[gate] if l == 0 and follows else (), vmem=VMEM_ATTEND,
        )
        state[name] = res[0]
        if l:
            kp["dx", l] = swap(res[1], sent(c, ("dx", l)))
        kp["gqkv", l], kp["gvec", l] = res[-2:]

    def both(key, l):
        return sum(kp[key, l].astype(F32) for kp in keep)

    def scattered(l):
        kept, give = keep[-1]["grads", l]
        give, _ = lax.optimization_barrier((give, keep[0]["dctx", l]))
        got = peer(give, 1, "row")
        if l:
            return lax.psum_scatter(kept + got, "grp", scatter_dimension=0)

        def part(k):
            return lax.dynamic_index_in_dim(kept, me ^ k, 0, False) + lax.dynamic_index_in_dim(got, me ^ k, 0, False)

        return sum(peer(part(k), k).astype(F32) if k else part(k).astype(F32) for k in range(groups)).astype(BF16)

    def side_blocks(l, after=None):
        rows = jnp.pad(both("gvec", l).T, ((0, half - 2), (0, width)))
        all_four = jnp.concatenate([both("gqkv", l), rows[None]], axis=0).astype(BF16)
        if after is not None:
            all_four, _ = lax.optimization_barrier((all_four, after))
        mine = lax.dynamic_slice_in_dim(all_four, 2 * core, 2)
        return mine + peer(lax.dynamic_slice_in_dim(all_four, 2 - 2 * core, 2), 1, "row")

    class ChipSum:
        def __init__(self, value):
            self.shape = value.shape
            self.flat = value.reshape(-1, 2 * width)
            self.rows = self.flat.shape[0] // 2
            self.high = lax.rem(own_row // 2, 2)

        def first(self, after=None):
            give = lax.dynamic_slice_in_dim(self.flat, (1 - self.high) * self.rows, self.rows)
            if after is not None:
                give, _ = lax.optimization_barrier((give, after))
            got = peer(give, 2, "row")
            self.mine = lax.dynamic_slice_in_dim(self.flat, self.high * self.rows, self.rows) + got
            return got

        def second(self, after=None):
            got, step = None, 4
            while step < lax.axis_size("row"):
                give = self.mine
                if after is not None:
                    give, _ = lax.optimization_barrier((give, after))
                got = peer(give, step, "row")
                self.mine = self.mine + got
                step *= 2
            return got

        def third(self):
            return peer(self.mine, 2, "row")

        def whole(self, other):
            first = self.high == 0
            parts = [jnp.where(first, self.mine, other), jnp.where(first, other, self.mine)]
            return jnp.concatenate(parts, axis=0).reshape(self.shape)

        def all(self, after=None):
            self.first(after)
            self.second()
            return self.whole(self.third())

    assert LAYERS == 2
    count = len(chunks)
    ends = [None] * LAYERS

    def run(f, l):
        for c in range(count):
            f(c, l)

    run(attend, 0)
    got, _ = lax.optimization_barrier((exchanged[0][0], Line.token))
    exchanged[0] = ahead = [got, peer(got, 1, "row")]
    for kp in keep:
        kp["far", 0] = ahead = swap(kp["parts"], ahead)
    arrange(0)
    run(early, 0)
    fetch(1, (keep[0]["far", 0], dense[0]["out"]))
    run(attend, 1)
    arrange(1)
    run(middle, 1)
    run(attend_back, 1)
    chips = ChipSum(jnp.concatenate([scattered(1), side_blocks(1)], axis=0))
    run(late, 0)
    gate = chips.first(keep[0]["dctx", 0])
    big = ChipSum(scattered(0)).all()
    run(attend_back, 0)
    second = chips.second()
    third = chips.third()
    total = chips.whole(third)
    ends[1] = [total, peer(total, 1, "row")]
    total = jnp.concatenate([big, ChipSum(side_blocks(0, second)).all()], axis=0)
    ends[0] = [total, peer(total, 1, "row")]
    sources = ends[0] + ends[1]

    span = side_run + 2

    def places_of(side, at):
        return jnp.where(side == core, 0, span) + at

    j, i = jnp.arange(3 * groups, dtype=jnp.int32), jnp.arange(3, dtype=jnp.int32)
    one = jnp.concatenate([places_of(i // 2, side_run + i % 2), places_of(j // side_run, j % side_run)])
    places = (jnp.arange(LAYERS, dtype=jnp.int32)[:, None] * (2 * span) + one[None, :]).reshape(-1)
    targets = own_row * capacity + jnp.arange(capacity, dtype=jnp.int32)
    match = ids.reshape(-1)[None, :] == targets[:, None]
    place = jnp.sum(jnp.where(match, places[None, :], 0), axis=1)
    place = jnp.where(jnp.any(match, axis=1), place, 1 << 20).astype(jnp.int32)
    own_grads = collect(place, sources, width).reshape(1, capacity, square)

    def vector_rows(l):
        odd = jnp.where(core == 1, sources[2 * l], sources[2 * l + 1])
        rest = odd[3 * groups - side_run]
        return jnp.concatenate([odd[side_run + 1, :2, :width], rest[: nv - 2, :width]], axis=0).astype(F32)

    summed_vectors = jnp.stack([vector_rows(l) for l in range(LAYERS)], axis=0)
    new_masters, new_first, new_second = adam_step(
        masters, own_grads, first_moment, second_moment, WEIGHT_DECAY, LEARN_RATE
    )
    new_vectors, new_vector_first, new_vector_second = adam_step(
        vectors, summed_vectors, vector_first, vector_second, 0.0, VECTOR_RATE
    )
    return (
        state["out"],
        state["grad"],
        new_masters,
        new_first,
        new_second,
        new_vectors,
        new_vector_first,
        new_vector_second,
    )


def solution(mesh):
    in_specs = (
        P("grp", "row"),
        P("row", None),
        P(),
        P("grp", "row", None),
        P("grp", "row", None),
        P("grp", "row", None),
        P(None, None, "grp"),
        P(None, None, "grp"),
        P(None, None, "grp"),
        P("grp", "row"),
    )
    out_specs = (
        P("grp", "row"),
        P("grp", "row"),
        P("grp", "row", None),
        P("grp", "row", None),
        P("grp", "row", None),
        P(None, None, "grp"),
        P(None, None, "grp"),
        P(None, None, "grp"),
    )
    return jax.shard_map(shards, mesh=mesh, in_specs=in_specs, out_specs=out_specs, check_vma=False)
```

```python
import functools
import math

import jax
import jax.numpy as jnp
import numpy as np
from jax import lax
from jax.experimental import pallas as pl
from jax.experimental.pallas import tpu as pltpu
from jax.sharding import PartitionSpec as P

HEADS = 12
LAYERS = 2
STEP = 7
BETA_ONE = 0.9
BETA_TWO = 0.999
LEARN_RATE = 0.1
VECTOR_RATE = 0.5
WEIGHT_DECAY = 0.01
ADAM_EPSILON = 1e-08
NORM_EPSILON = 1e-12
MASK_FILL = -1e30
AUG = 16
QUARTER = 128
LANES = 128
VMEM_LIMIT = 56 * 1024 * 1024
VMEM_ATTEND = 56 * 1024 * 1024
F32 = jnp.float32
BF16 = jnp.bfloat16


def CHUNKS(sequences):
    return [(sequences + 1) // 2, sequences // 2]


def nn(a, b):
    return lax.dot_general(a, b, (((1,), (0,)), ((), ())), preferred_element_type=F32)


def nt(a, b):
    return lax.dot_general(a, b, (((1,), (1,)), ((), ())), preferred_element_type=F32)


def tn(a, b):
    return lax.dot_general(a, b, (((0,), (0,)), ((), ())), preferred_element_type=F32)


def block_layout(groups, layers):
    counts = []
    block_matrix = []
    block_step = []
    for layer_index in range(layers):
        for matrix_type in range(6):
            amount = 1 if matrix_type < 3 else groups
            for position in range(amount):
                block_matrix.append(layer_index * 6 + matrix_type)
                block_step.append(position)
            counts.append(amount)
    return (
        np.array(counts, np.int32),
        np.array(block_matrix, np.int32),
        np.array(block_step, np.int32),
    )


def slot_index(owners, groups, layers, capacity):
    counts, block_matrix, block_step = block_layout(groups, layers)
    matrix_ids = jnp.arange(counts.shape[0], dtype=jnp.int32)
    same_owner = owners[:, None] == owners[None, :]
    earlier = matrix_ids[None, :] < matrix_ids[:, None]
    slot_of = jnp.sum(
        jnp.where(same_owner & earlier, jnp.asarray(counts, jnp.int32)[None, :], 0), axis=1
    )
    starts = owners * capacity + slot_of
    choose = (jnp.asarray(block_matrix, jnp.int32)[:, None] == matrix_ids[None, :]).astype(
        jnp.int32
    )
    return jnp.sum(choose * starts[None, :], axis=1) + jnp.asarray(block_step, jnp.int32)


def pack(square):
    half = square.shape[0] // 2
    return jnp.concatenate([square[:half], square[half:]], axis=1)


def unpack(packed):
    width = packed.shape[1] // 2
    return jnp.concatenate([packed[:, :width], packed[:, width:]], axis=0)


def lanes(value):
    total = value[:, :LANES]
    for at in range(LANES, value.shape[1], LANES):
        total = total + value[:, at : at + LANES]
    return total


def row_totals(value):
    return jnp.sum(lanes(value), axis=1, keepdims=True)


def accumulate(ref, index, value):
    first = pl.program_id(0) == 0

    @pl.when(first)
    def _():
        ref[index] = value

    @pl.when(jnp.logical_not(first))
    def _():
        ref[index] = ref[index] + value


def split3(value):
    high = value.astype(BF16)
    rest = value - high.astype(F32)
    mid = rest.astype(BF16)
    last = (rest - mid.astype(F32)).astype(BF16)
    return high, mid, last


def segment_rows(segs):
    row = lax.broadcasted_iota(jnp.int32, (AUG, segs.shape[1]), 0)
    same = row == segs
    query_rows = jnp.where(same | (row >= 4), 0.0, MASK_FILL)
    key_rows = jnp.where(same | ((row >= 4) & (row < 7)), 1.0, 0.0)
    return query_rows, key_rows.astype(BF16)


def with_rows(query_rows, value):
    high, mid, last = split3(-value)
    row = lax.broadcasted_iota(jnp.int32, query_rows.shape, 0)
    out = jnp.where(row == 4, high.astype(F32), query_rows)
    out = jnp.where(row == 5, mid.astype(F32), out)
    out = jnp.where(row == 6, last.astype(F32), out)
    return out.astype(BF16)


def norm_cdf(u):
    a = jnp.abs(u) * math.sqrt(0.5)
    t = 1.0 / (1.0 + 0.3275911 * a)
    bell = jnp.exp(-a * a)
    poly = t * (
        0.254829592
        + t * (-0.284496736 + t * (1.421413741 + t * (-1.453152027 + t * 1.061405429)))
    )
    tail = (0.5 * poly) * bell
    return jnp.where(u < 0, tail, 1.0 - tail), bell * (1.0 / math.sqrt(2.0 * math.pi))


def attend_body(first, per_group, groups, *refs):
    if first:
        x_ref, seg_ref, w_ref, vec_ref, qkv_ref, ctx_ref, lse_ref, sent = refs
    else:
        pieces, seg_ref, w_ref, vec_ref, x_ref, qkv_ref, ctx_ref, lse_ref, sent = refs
        for j in range(groups):
            x_ref[:, j * QUARTER : (j + 1) * QUARTER] = pieces[j]
    x = x_ref[...]
    width = x.shape[0]
    size = width // per_group
    vec = vec_ref[...]
    q = (nn(w_ref[0], x) + vec[:, 0:1]).astype(BF16)
    k = nn(w_ref[1], x).astype(BF16)
    v = (nn(w_ref[2], x) + vec[:, 1:2]).astype(BF16)
    qkv_ref[0:width] = q
    qkv_ref[width : 2 * width] = k
    qkv_ref[2 * width : 3 * width] = v
    query_rows, key_rows = segment_rows(seg_ref[0])
    query_rows = query_rows.astype(BF16)
    parts = [slice(h * size, (h + 1) * size) for h in range(per_group)]
    scaled = q * jnp.asarray(size ** (-0.5), BF16)
    scores = [
        tn(jnp.concatenate([k[p], key_rows], axis=0), jnp.concatenate([scaled[p], query_rows], axis=0))
        for p in parts
    ]
    tops = [jnp.max(s, axis=0, keepdims=True) for s in scores]
    powers = [jnp.exp(s - top) for s, top in zip(scores, tops)]
    totals = [jnp.sum(e, axis=0, keepdims=True) for e in powers]
    chances = [(e * (1.0 / total)).astype(BF16) for e, total in zip(powers, totals)]
    for h, p in enumerate(parts):
        ctx_ref[p] = nn(v[p], chances[h]).astype(BF16)
        lse_ref[h : h + 1] = tops[h] + jnp.log(totals[h])
    for j in range(groups):
        sent[j] = ctx_ref[:, j * QUARTER : (j + 1) * QUARTER]


def attend_back_body(first, per_group, groups, follows, pieces, *refs):
    ctx_ref, qkv_ref, lse_ref, x_ref, seg_ref, w_ref = refs[:6]
    refs = refs[6 + follows :]
    if first:
        dx_ref, gqkv_ref, acc_ref, dctx_ref, gsum_ref, asum_ref = refs
    else:
        out_ref, sent, gqkv_ref, acc_ref, dctx_ref, gsum_ref, asum_ref, dx_ref = refs
    width, length = ctx_ref.shape
    size = width // per_group
    scale = size ** (-0.5)
    for j in range(groups):
        cols = slice(j * QUARTER, (j + 1) * QUARTER)
        dctx_ref[:, cols] = pieces[j, :width]
        if not first:
            out_ref[:, cols] = pieces[j, width:].astype(F32)
    ctx = ctx_ref[...]
    dctx = dctx_ref[...]
    x = x_ref[...]
    query_rows, key_rows = segment_rows(seg_ref[0])
    zero_rows = jnp.zeros_like(query_rows)
    q = qkv_ref[0:width]
    k = qkv_ref[width : 2 * width]
    v = qkv_ref[2 * width : 3 * width]
    dq, dk, dv = [], [], []
    for h in range(per_group):
        part = slice(h * size, (h + 1) * size)
        qh, kh, vh, dch = q[part], k[part], v[part], dctx[part]
        qs = qh * jnp.asarray(scale, BF16)
        delta = jnp.sum(dch.astype(F32) * ctx[part].astype(F32), axis=0, keepdims=True)
        qa = jnp.concatenate([qs, with_rows(query_rows, lse_ref[h : h + 1])], axis=0)
        ka = jnp.concatenate([kh, key_rows], axis=0)
        da = jnp.concatenate([dch, with_rows(zero_rows, delta)], axis=0)
        va = jnp.concatenate([vh, key_rows], axis=0)
        p = jnp.exp(tn(ka, qa))
        ds = (p * tn(va, da)).astype(BF16)
        dv.append(nt(dch, p.astype(BF16)))
        dq.append(nn(kh, ds) * scale)
        dk.append(nt(qs, ds))
    dq, dk, dv = (jnp.concatenate(parts, axis=0) for parts in (dq, dk, dv))
    accumulate(asum_ref, 0, lanes(dq))
    accumulate(asum_ref, 1, lanes(dv))
    low = jnp.concatenate([grad.astype(BF16) for grad in (dq, dk, dv)], axis=0)
    dx = nn(jnp.concatenate([w_ref[at] for at in range(3)], axis=1), low)
    grads = nt(x, low)
    for at in range(3):
        accumulate(gsum_ref, at, grads[:, at * width : (at + 1) * width])
    dx_ref[...] = dx
    for j in range(groups):
        cols = slice(j * QUARTER, (j + 1) * QUARTER)
        if first:
            dx_ref[:, cols] = dx_ref[:, cols] + pieces[j, width:].astype(F32)
        else:
            sent[j] = dx_ref[:, cols].astype(BF16)

    @pl.when(pl.program_id(0) == pl.num_programs(0) - 1)
    def _():
        for at in range(3):
            gqkv_ref[at] = pack(gsum_ref[at].astype(BF16))
        acc_ref[...] = jnp.concatenate(
            [jnp.sum(asum_ref[row], axis=1, keepdims=True) for row in range(2)], axis=1
        )


def norm(value):
    centre = jnp.mean(value, axis=0, keepdims=True)
    off = value - centre
    inverse = lax.rsqrt(jnp.mean(off * off, axis=0, keepdims=True) + NORM_EPSILON)
    return off * inverse, inverse


def norm_back(grad, gain, normed, inverse):
    e = grad * gain
    return inverse * (
        e - jnp.mean(e, axis=0, keepdims=True) - normed * jnp.mean(e * normed, axis=0, keepdims=True)
    )


def columns(vec_ref, row):
    return jnp.concatenate([vec_ref[a][:, row : row + 1] for a in range(vec_ref.shape[0])], axis=0)


def layer_forward(x, ctx, w, vec_ref, hid_ref, gp_ref, done=lambda a: None):
    groups, width, nv = vec_ref.shape
    nup = nv - 8
    r1 = x + (nn(w["out_t"][...], ctx) + columns(vec_ref, 2))
    n1, i1 = norm(r1)
    y1 = n1 * columns(vec_ref, 4 + nup) + columns(vec_ref, 5 + nup)
    yl = y1.astype(BF16)
    branch = []
    for a in range(groups):
        own = yl[a * width : (a + 1) * width]
        for j in range(nup):
            rows = slice(j * width, (j + 1) * width)
            u = nn(w["up_t"][a, rows], own) + vec_ref[a][:, 3 + j : 4 + j]
            cdf, bell = norm_cdf(u)
            at = slice((a * nup + j) * width, (a * nup + j + 1) * width)
            hid_ref[at] = (u * cdf).astype(BF16)
            gp_ref[at] = (cdf + u * bell).astype(BF16)
        done(a)
        branch.append(nn(w["down_t"][a], hid_ref[a * nup * width : (a + 1) * nup * width]))
    r2 = y1 + (jnp.concatenate(branch, axis=0) + columns(vec_ref, 3 + nup))
    n2, i2 = norm(r2)
    x2 = n2 * columns(vec_ref, 6 + nup) + columns(vec_ref, 7 + nup)
    return x2, n1, i1, yl, n2, i2


def layer_backward(dy, ctx, w, vec_ref, n1, i1, yl, n2, i2, hid_ref, gp_ref, sums_out, ready=lambda a: None):
    put = sums_out.put
    groups, width, nv = vec_ref.shape
    nup = nv - 8
    hidden = nup * width
    sums = [None] * (nv - 2)
    sums[6 + nup - 2 + 0] = row_totals(dy * n2)
    sums[7 + nup - 2 + 0] = row_totals(dy)
    dz = norm_back(dy, columns(vec_ref, 6 + nup), n2, i2)
    sums[3 + nup - 2] = row_totals(dz)
    dzl = dz.astype(BF16)
    sums_out.ready()
    back = []
    bias = [[] for _ in range(nup)]
    for a in range(groups):
        own = slice(a * width, (a + 1) * width)
        every = slice(a * nup * width, (a + 1) * nup * width)
        ready(a)
        grads = nt(hid_ref[every], dzl[own])
        dh = nn(w["down"][a], dzl[own])
        lows = []
        for j in range(nup):
            rows = slice(j * width, (j + 1) * width)
            put(a, groups + nup + j, grads[rows])
            du = dh[rows] * gp_ref[(a * nup + j) * width : (a * nup + j + 1) * width].astype(F32)
            bias[j].append(row_totals(du))
            lows.append(du.astype(BF16))
        dul = jnp.concatenate(lows, axis=0)
        grads = nt(yl[own], dul)
        for j in range(nup):
            put(a, groups + j, grads[:, j * width : (j + 1) * width])
        back.append(nn(w["up"][a], dul))
        sums_out.send(a, groups, 2 * nup)
    for j in range(nup):
        sums[3 + j - 2] = jnp.concatenate(bias[j], axis=0)
    dy1 = dz + jnp.concatenate(back, axis=0)
    sums[4 + nup - 2] = row_totals(dy1 * n1)
    sums[5 + nup - 2] = row_totals(dy1)
    dr1 = norm_back(dy1, columns(vec_ref, 4 + nup), n1, i1)
    sums[0] = row_totals(dr1)
    dal = dr1.astype(BF16)
    dctx = nn(w["out"][...], dal).astype(BF16)
    for a in range(groups):
        own = nt(ctx[a * width : (a + 1) * width], dal)
        for b in range(groups):
            put(a, a ^ b, own[:, b * width : (b + 1) * width])
        sums_out.send(a, 0, groups)
    stack = jnp.concatenate(sums, axis=1)
    for a in range(groups):
        flat = jnp.concatenate(
            [stack[a * width : (a + 1) * width], jnp.zeros((width, LANES - len(sums)), F32)], axis=1
        ).T
        flat = flat[: width // 2]
        put(a, groups + 2 * nup, jnp.concatenate([flat, jnp.zeros_like(flat)], axis=1), packed=True)
        sums_out.send(a, groups + 2 * nup, 1)
    return dr1, dctx


WEIGHTS = ("out", "out_t", "up", "up_t", "down", "down_t")


class Fetched:
    def __init__(self, names, sources, places, sems):
        self.places = dict(zip(names, places))
        self.copies = {
            name: pltpu.make_async_copy(source, place, sems.at[at])
            for at, (name, source, place) in enumerate(zip(names, sources, places))
        }
        for copy in self.copies.values():
            copy.start()

    def __getitem__(self, name):
        copy = self.copies.pop(name, None)
        if copy is not None:
            copy.wait()
        return self.places[name]


class Sums:
    def __init__(self, me, core, keep_ref, give_ref, held_ref, before, sems):
        self.me, self.core, self.refs, self.held, self.sems = me, core, (keep_ref, give_ref), held_ref, sems
        self.run = keep_ref.shape[1]
        self.used, self.sent, self.loads, self.before = 0, [], [], before is not None
        if self.before:
            for a in range(held_ref.shape[0]):
                for side in range(2):
                    held = held_ref.at[a, pl.ds(side * self.run, self.run)]
                    self.loads.append(self.either(side, [ref.at[a ^ me] for ref in before], held, False))

    def either(self, side, places, held, out):
        sem = self.sems.at[self.used]
        self.used += 1
        keep, give = (
            pltpu.make_async_copy(held, place, sem) if out else pltpu.make_async_copy(place, held, sem)
            for place in places
        )
        pl.when(self.core == side)(keep.start)
        pl.when(self.core != side)(give.start)
        return keep

    def ready(self):
        for load in self.loads:
            load.wait()

    def put(self, a, j, block, packed=False):
        block = block if packed else pack(block)
        if self.before:
            block = block + self.held[a, j].astype(F32)
        self.held[a, j] = block.astype(BF16)

    def send(self, a, first, count):
        for side in range(2):
            low, high = max(first, side * self.run), min(first + count, (side + 1) * self.run)
            if low < high:
                part = pl.ds(low - side * self.run, high - low)
                places = [ref.at[a ^ self.me, part] for ref in self.refs]
                self.sent.append(self.either(side, places, self.held.at[a, pl.ds(low, high - low)], True))

    def finish(self):
        for copy in self.sent:
            copy.wait()


def joined(me, ref, rows=slice(None), cols=slice(None)):
    return jnp.concatenate([ref[a ^ me, rows, cols] for a in range(ref.shape[0])], axis=0)


def early_body(groups, first, count, me_ref, ctx_ref, x_ref, *refs):
    names = ("out_t", "up_t", "down_t")
    w_refs, vec_ref, sent = refs[:3], refs[3], refs[4]
    x2_ref, n1_ref, n2_ref, inv_ref, far_hid, far_gp = refs[5:11]
    w = Fetched(names, w_refs, refs[11:14], refs[14])
    hid_ref, gp_ref, sems = refs[15:]
    me, width = me_ref[0], vec_ref.shape[1]
    copies = []

    def done(a):
        rows = pl.ds(a * (hid_ref.shape[0] // groups), hid_ref.shape[0] // groups)
        for ref, far in ((hid_ref, far_hid), (gp_ref, far_gp)):
            copies.append(pltpu.make_async_copy(ref.at[rows], far.at[rows], sems.at[len(copies)]))
            copies[-1].start()

    start = joined(me, x_ref, cols=slice(first, first + count)).astype(F32)
    x2, n1, i1, _, n2, i2 = layer_forward(start, joined(me, ctx_ref), w, vec_ref, hid_ref, gp_ref, done)
    x2_ref[...] = x2
    for a in range(groups):
        sent[a ^ me] = x2[a * width : (a + 1) * width].astype(BF16)
    n1_ref[...] = n1.astype(BF16)
    n2_ref[...] = n2.astype(BF16)
    inv_ref[...] = jnp.concatenate([i1, i2], axis=0)
    for copy in copies:
        copy.wait()


def middle_body(groups, first, count, follows, me_ref, core_ref, ctx_ref, cot_ref, x_ref, *refs):
    names = ("out_t", "up_t", "down_t", "down", "up", "out")
    w_refs, vec_ref, refs = refs[:6], refs[6], refs[7:]
    before = None
    if follows:
        before, refs = refs[:2], refs[2:]
    sent, dr_ref, keep_ref, give_ref, hid_ref, gp_ref, held_ref, grad_sems = refs[:8]
    w = Fetched(names, w_refs, refs[8:14], refs[14])
    me, width = me_ref[0], vec_ref.shape[1]
    sums_out = Sums(me, core_ref[0], keep_ref, give_ref, held_ref, before, grad_sems)
    ctx = joined(me, ctx_ref)
    x2, n1, i1, yl, n2, i2 = layer_forward(x_ref[...], ctx, w, vec_ref, hid_ref, gp_ref)
    for a in range(groups):
        sent[a ^ me, width:] = x2[a * width : (a + 1) * width].astype(BF16)
    dy = joined(me, cot_ref, cols=slice(first, first + count)).astype(F32)
    dr1, dctx = layer_backward(dy, ctx, w, vec_ref, n1, i1, yl, n2, i2, hid_ref, gp_ref, sums_out)
    dr_ref[...] = dr1
    for a in range(groups):
        sent[a ^ me, :width] = dctx[a * width : (a + 1) * width]
    sums_out.finish()


def late_body(groups, follows, me_ref, core_ref, got_ref, ctx_ref, *refs):
    names = ("down", "up", "out")
    dr_ref, n1_ref, n2_ref, inv_ref, far_hid, far_gp = refs[:6]
    w_refs, vec_ref, refs = refs[6:9], refs[9], refs[10:]
    before = None
    if follows:
        before, refs = refs[:2], refs[2:]
    sent, keep_ref, give_ref, held_ref, grad_sems = refs[:5]
    w = Fetched(names, w_refs, refs[5:8], refs[8])
    hid_ref, gp_ref, sems = refs[9:]
    copies = []
    for a in range(groups):
        rows = pl.ds(a * (hid_ref.shape[0] // groups), hid_ref.shape[0] // groups)
        for ref, far in ((hid_ref, far_hid), (gp_ref, far_gp)):
            copies.append(pltpu.make_async_copy(far.at[rows], ref.at[rows], sems.at[len(copies)]))
            copies[-1].start()

    def ready(a):
        copies[2 * a].wait()
        copies[2 * a + 1].wait()

    me, width = me_ref[0], vec_ref.shape[1]
    sums_out = Sums(me, core_ref[0], keep_ref, give_ref, held_ref, before, grad_sems)
    nup = vec_ref.shape[2] - 8
    dy = dr_ref[...] + joined(me, got_ref).astype(F32)
    n1, n2 = n1_ref[...].astype(F32), n2_ref[...].astype(F32)
    yl = (n1 * columns(vec_ref, 4 + nup) + columns(vec_ref, 5 + nup)).astype(BF16)
    inv = inv_ref[...]
    dr1, dctx = layer_backward(
        dy, joined(me, ctx_ref), w, vec_ref, n1, inv[0:1], yl, n2, inv[1:2], hid_ref, gp_ref, sums_out, ready
    )
    for a in range(groups):
        sent[a ^ me, :width] = dctx[a * width : (a + 1) * width]
        sent[a ^ me, width:] = dr1[a * width : (a + 1) * width].astype(BF16)
    sums_out.finish()


def scatter_body(groups, *refs):
    for source, out in zip(refs[: len(refs) // 2], refs[len(refs) // 2 :]):
        for j in range(groups):
            out[j] = source[:, j * QUARTER : (j + 1) * QUARTER].astype(BF16)


def scatter_quarters(arrays, groups):
    width, tokens = arrays[0].shape
    length = QUARTER * groups
    count = tokens // length
    return pl.pallas_call(
        functools.partial(scatter_body, groups),
        grid=(count,),
        in_specs=[pl.BlockSpec((width, length), lambda i: (0, i))] * len(arrays),
        out_specs=[pl.BlockSpec((groups, width, QUARTER), lambda i: (0, 0, i))] * len(arrays),
        out_shape=[jax.ShapeDtypeStruct((groups, width, QUARTER * count), BF16)] * len(arrays),
        name="scatter_quarters",
    )(*arrays)


def pick_body(jobs, ids_ref, source, *refs):
    outs, held, sems = refs[:-2], refs[-2], refs[-1]
    copies = []
    for at in range(held.shape[0]):
        copies.append(pltpu.make_async_copy(source.at[ids_ref[at]], held.at[at], sems.at[at]))
        copies[-1].start()
    at, out = 0, 0
    for count, times in jobs:
        for one in range(count):
            copies[at].wait()
            if times:
                for copy in range(times):
                    outs[out][copy, one] = held[at]
            else:
                block = unpack(held[at])
                outs[out][one] = block
                outs[out + 1][one] = block.T
            at += 1
        out += 1 if times else 2


def pick(jobs, ids, source):
    half, double = source.shape[1:]
    shapes = []
    for count, times in jobs:
        shapes += [(times, count, half, double)] if times else [(count, double // 2, double // 2)] * 2
    total = sum(count for count, _ in jobs)
    return pl.pallas_call(
        functools.partial(pick_body, jobs),
        grid_spec=pltpu.PrefetchScalarGridSpec(
            num_scalar_prefetch=1,
            grid=(1,),
            in_specs=[pl.BlockSpec(memory_space=pltpu.HBM)],
            out_specs=[pl.BlockSpec(shape, lambda i, ids, n=len(shape): (0,) * n) for shape in shapes],
            scratch_shapes=[pltpu.VMEM((total, half, double), BF16), pltpu.SemaphoreType.DMA((total,))],
        ),
        out_shape=[jax.ShapeDtypeStruct(shape, BF16) for shape in shapes],
        name="pick",
    )(ids, source)


def arrange_body(groups, nup, core_ref, me_ref, *refs):
    sems, places = refs[-1], dict(zip(WEIGHTS, refs[-7:-1]))
    w, refs = dict(zip(WEIGHTS, refs[-13:-7])), refs[:-13]
    got, other = refs[0], refs[1] if len(refs) == 2 else None
    far, w, copies = w, places, []

    def send(name, index):
        copies.append(pltpu.make_async_copy(w[name].at[index], far[name].at[index], sems.at[len(copies)]))
        copies[-1].start()

    me = me_ref[0]
    share = got.shape[1]
    width = got.shape[3] // 2
    even = core_ref[0] == 0

    def block(a, j):
        if other is None:
            return unpack(got[a ^ me, j])
        near, far = got[a ^ me, j % share], other[a ^ me, j % share]
        return unpack(jnp.where(even, near, far) if j < share else jnp.where(even, far, near))

    for a in range(groups):
        rows = slice(a * width, (a + 1) * width)
        line = [block(a, a ^ b) for b in range(groups)]
        w["out"][rows] = jnp.concatenate(line, axis=1)
        ups = [block(a, groups + j) for j in range(nup)]
        w["up"][a] = jnp.concatenate(ups, axis=1)
        w["up_t"][a] = jnp.concatenate([up.T for up in ups], axis=0)
        downs = [block(a, groups + nup + j) for j in range(nup)]
        w["down"][a] = jnp.concatenate(downs, axis=0)
        w["down_t"][a] = jnp.concatenate([down.T for down in downs], axis=1)
        for name in WEIGHTS[2:]:
            send(name, a)
    for b in range(groups):
        w["out_t"][b * width : (b + 1) * width] = jnp.concatenate(
            [block(a, a ^ b).T for a in range(groups)], axis=1
        )
        send("out", pl.ds(b * width, width))
        send("out_t", pl.ds(b * width, width))
    for copy in copies:
        copy.wait()


def collect_body(edges, ids_ref, *refs):
    sources, out_ref, held, sems = refs[: len(edges)], refs[-3], refs[-2], refs[-1]
    slots = out_ref.shape[0]
    for slot in range(slots):
        at, low = ids_ref[slot], 0
        for source, high in zip(sources, edges):

            @pl.when((at >= low) & (at < high))
            def _(source=source, place=at - low, slot=slot):
                pltpu.make_async_copy(source.at[place], held.at[slot], sems.at[slot]).start()

            low = high
    for slot in range(slots):
        there = ids_ref[slot] < edges[-1]

        @pl.when(there)
        def _(slot=slot):
            pltpu.make_async_copy(sources[0].at[0], held.at[slot], sems.at[slot]).wait()
            out_ref[slot] = unpack(held[slot]).astype(F32)

        @pl.when(jnp.logical_not(there))
        def _(slot=slot):
            out_ref[slot] = jnp.zeros(out_ref.shape[1:], F32)


def collect(places, sources, width):
    edges = tuple(int(edge) for edge in np.cumsum([source.shape[0] for source in sources]))
    slots, size = places.shape[0], sources[0].shape[1:]
    return pl.pallas_call(
        functools.partial(collect_body, edges),
        grid_spec=pltpu.PrefetchScalarGridSpec(
            num_scalar_prefetch=1,
            grid=(1,),
            in_specs=[HBM_SPEC] * len(sources),
            out_specs=pl.BlockSpec((slots, width, width), lambda i, ids: (0, 0, 0)),
            scratch_shapes=[pltpu.VMEM((slots, *size), BF16), pltpu.SemaphoreType.DMA((slots,))],
        ),
        out_shape=table(slots, width, width),
        name="collect",
    )(places, *sources)


def table(*shape):
    return jax.ShapeDtypeStruct(shape, F32)


class Line:
    token = None


HBM_SPEC = pl.BlockSpec(memory_space=pltpu.HBM)


def call(body, name, operands, outs, scalars=(), grid=None, specs=None, out_specs=None, scratch=(), aliases=None,
         flops=0, after=(), far=(), far_outs=(), vmem=VMEM_LIMIT):
    behind = [array for array in (Line.token, *after) if array is not None]
    skip, ahead = len(behind), len(scalars)
    plain, made = body, len(outs)
    inputs = len(operands)
    whole = pl.BlockSpec(memory_space=pltpu.VMEM)

    def body(*refs):
        first, refs = refs[:ahead], refs[ahead + skip :]
        ins, results, rest = refs[:inputs], refs[inputs : inputs + made], refs[inputs + made + 1 :]
        refs[inputs + made][...] = jnp.zeros((8, LANES), F32)
        plain(*first, *ins, *results, *rest)

    any_spec = pl.BlockSpec(memory_space=pl.ANY)
    moved = sum(math.prod(array.shape) * array.dtype.itemsize for array in (*operands, *outs))
    common = dict(
        out_shape=[*outs, table(8, LANES)],
        name=name,
        input_output_aliases={at + ahead + skip: to for at, to in (aliases or {}).items()},
        compiler_params=pltpu.CompilerParams(vmem_limit_bytes=vmem),
        cost_estimate=pl.CostEstimate(flops=int(flops), bytes_accessed=int(moved), transcendentals=0),
    )
    if grid is None:
        smem = pl.BlockSpec(memory_space=pltpu.SMEM)
        res = pl.pallas_call(
            body,
            in_specs=[smem] * ahead + [any_spec] * skip
            + [HBM_SPEC if at in far else whole for at in range(inputs)],
            out_specs=[HBM_SPEC if at in far_outs else whole for at in range(made)] + [whole],
            scratch_shapes=list(scratch),
            **common,
        )(*scalars, *behind, *operands)
    else:
        res = pl.pallas_call(
            body,
            grid_spec=pltpu.PrefetchScalarGridSpec(
                num_scalar_prefetch=ahead,
                grid=grid,
                in_specs=[any_spec] * skip + list(specs),
                out_specs=list(out_specs) + [pl.BlockSpec((8, LANES), lambda i, *s: (0, 0))],
                scratch_shapes=list(scratch),
            ),
            **common,
        )(*scalars, *behind, *operands)
    Line.token = res[-1]
    return list(res[:-1])


def peer(value, step, axis="grp"):
    count = lax.axis_size(axis)
    return lax.ppermute(value, axis, [(i, i ^ step) for i in range(count)])


def swap(parts, after=None):
    if after is not None:
        parts, _ = lax.optimization_barrier((parts, after))
    return lax.all_to_all(parts, "grp", split_axis=0, concat_axis=0)


def adam_step(param, grad, first, second, decay, rate):
    first_new = BETA_ONE * first + (1.0 - BETA_ONE) * grad
    second_new = BETA_TWO * second + (1.0 - BETA_TWO) * grad * grad
    first_hat = first_new / (1.0 - BETA_ONE**STEP)
    second_hat = second_new / (1.0 - BETA_TWO**STEP)
    updated = param - rate * (first_hat / (jnp.sqrt(second_hat) + ADAM_EPSILON) + decay * param)
    return (updated, first_new, second_new)


def shards(
    tokens,
    segments,
    owners,
    masters,
    first_moment,
    second_moment,
    vectors,
    vector_first,
    vector_second,
    cotangent,
):
    groups = lax.axis_size("grp")
    me = lax.axis_index("grp").astype(jnp.int32)
    own_row = lax.axis_index("row").astype(jnp.int32)
    core = lax.rem(own_row, 2)
    capacity = masters.shape[1]
    width, tokens_here = tokens.shape
    half = width // 2
    fg = groups * width
    sequences, length = segments.shape
    per_group = HEADS // groups
    nv = vectors.shape[1]
    nup = nv - 8
    per_layer = 3 + 3 * groups
    segs = segments.reshape(sequences, 1, length)
    order = jnp.arange(groups, dtype=jnp.int32) ^ me
    here, core_at = me.reshape(1), core.reshape(1)
    square = width * width

    block_index = slot_index(owners, groups, LAYERS, capacity)
    ids = block_index.reshape(LAYERS, per_layer)
    relative = jnp.take(ids[:, 3 : 3 + groups], order, axis=1, mode="clip")
    ids = jnp.concatenate([ids[:, :3], relative, ids[:, 3 + groups :]], axis=1)
    local_blocks = masters[0].astype(BF16).reshape(capacity, 2, half, width)
    local_blocks = jnp.concatenate([local_blocks[:, 0], local_blocks[:, 1]], axis=2)
    everyone = lax.all_gather(local_blocks, "row", axis=0, tiled=True)

    x_parts, cot_parts = (swap(part) for part in scatter_quarters([tokens, cotangent], groups))
    vec_all = jnp.stack([vectors] + [peer(vectors, k) for k in range(1, groups)]).transpose(1, 0, 3, 2)
    vecs = [vec_all[l] for l in range(LAYERS)]
    own_vecs = [vec_all[l, 0] for l in range(LAYERS)]

    share = (3 * groups) // 2
    dense, exchanged = [None] * LAYERS, [None] * LAYERS
    source, _ = lax.optimization_barrier((everyone, (vec_all, x_parts, cot_parts)))
    mine = lax.dynamic_slice(ids[0], (3 + core * share,), (share,))
    (send,) = pick([(share, groups)], mine, source)
    exchanged[0] = [swap(send)]
    others = [(3, 0) for _ in range(LAYERS)] + [(3 * groups, 1) for _ in range(1, LAYERS)]
    wanted = [ids[l, :3] for l in range(LAYERS)] + [ids[l, 3:] for l in range(1, LAYERS)]
    picked = pick(others, jnp.concatenate(wanted), source)
    w_qkv, w_turned = picked[0 : 2 * LAYERS : 2], picked[1 : 2 * LAYERS : 2]

    def fetch(l, after):
        own, _ = lax.optimization_barrier((picked[2 * LAYERS + l - 1][0], after))
        exchanged[l] = [lax.all_gather(own, "grp", axis=0)]

    def arrange(l):
        got = exchanged[l]
        shapes = [(fg, fg), (fg, fg), (groups, width, fg), (groups, fg, width), (groups, fg, width), (groups, width, fg)]
        smem, vmem = pl.BlockSpec(memory_space=pltpu.SMEM), pl.BlockSpec(memory_space=pltpu.VMEM)
        res = pl.pallas_call(
            functools.partial(arrange_body, groups, nup),
            in_specs=[smem, smem] + [vmem] * len(got),
            out_specs=[HBM_SPEC] * 6,
            scratch_shapes=[pltpu.VMEM(shape, BF16) for shape in shapes] + [pltpu.SemaphoreType.DMA((6 * groups,))],
            out_shape=[pltpu.HBM(shape, BF16) for shape in shapes],
            name="arrange",
            compiler_params=pltpu.CompilerParams(vmem_limit_bytes=VMEM_LIMIT),
        )(core_at, here, *got)
        dense[l] = dict(zip(WEIGHTS, res))

    def weight_places(names):
        shapes = {"out": (fg, fg), "up": (groups, width, fg), "down": (groups, fg, width)}
        shapes |= {"out_t": (fg, fg), "up_t": (groups, fg, width), "down_t": (groups, width, fg)}
        return [pltpu.VMEM(shapes[name], BF16) for name in names] + [pltpu.SemaphoreType.DMA((len(names),))]

    chunks, at = [], 0
    for count in CHUNKS(sequences):
        chunks.append((at, count))
        at += count
    keep = [dict() for _ in chunks]
    state = {"out": None, "grad": None}
    Line.token = None

    def tok(rows):
        return pl.BlockSpec((rows, length), lambda i, *s: (0, i))

    def quart(rows=width):
        return pl.BlockSpec((groups, rows, QUARTER), lambda i, *s: (0, 0, i))

    def parts(count, rows=width):
        return jax.ShapeDtypeStruct((groups, rows, count * QUARTER), BF16)

    def whole(*shape):
        return pl.BlockSpec(shape, lambda i, *s: (0,) * len(shape))

    def sent(c, key):
        return keep[c - 1][key] if c else None

    def attend(c, l):
        first, count = chunks[c]
        kp = keep[c]
        here_tokens = count * length
        shifted = pl.BlockSpec((width, length), lambda i, *s: (0, i + first))
        seg_spec = pl.BlockSpec((1, 1, length), lambda i, *s: (i + first, 0, 0))
        operands = [segs, w_turned[l], own_vecs[l]]
        specs = [seg_spec, whole(3, width, width), whole(width, nv)]
        outs = [pltpu.HBM((3 * width, here_tokens), BF16), pltpu.HBM((width, here_tokens), BF16),
                pltpu.HBM((per_group, here_tokens), F32)]
        out_specs = [tok(3 * width), tok(width), tok(per_group)]
        outs.append(parts(count))
        out_specs.append(quart())
        if l == 0:
            operands, specs = [tokens] + operands, [shifted] + specs
        else:
            operands, specs = [kp["x", l]] + operands, [quart()] + specs
            outs = [pltpu.HBM((width, here_tokens), BF16)] + outs
            out_specs = [tok(width)] + out_specs
        res = call(
            functools.partial(attend_body, l == 0, per_group, groups), "attend", operands, outs, (),
            (count,), specs, out_specs, flops=here_tokens * (6 * square + 4 * width * length), vmem=VMEM_ATTEND,
        )
        if l:
            kp["xl", l] = res.pop(0)
        kp["qkv", l], kp["ctx", l], kp["lse", l] = res[:3]
        if l:
            kp["far", l] = swap(res[3], sent(c, ("far", l)))
        else:
            kp["parts"] = res[3]

    def early(c, l):
        first, count = chunks[c]
        kp = keep[c]
        n = count * QUARTER
        names = ("out_t", "up_t", "down_t")
        hidden = pltpu.VMEM((groups * nup * width, n), BF16)
        outs = [parts(count), pltpu.HBM((fg, n), F32), pltpu.HBM((fg, n), BF16), pltpu.HBM((fg, n), BF16),
                pltpu.HBM((2, n), F32)] + [pltpu.HBM((groups * nup * width, n), BF16)] * 2
        res = call(
            functools.partial(early_body, groups, first * QUARTER, n), "early",
            [kp["far", l], x_parts, *(dense[l][name] for name in names), vecs[l]], outs, [here],
            scratch=[*weight_places(names), hidden, hidden, pltpu.SemaphoreType.DMA((2 * groups,))],
            far=range(2, 5), far_outs=[5, 6],
            flops=2 * n * groups * square * (groups + 2 * nup),
        )
        kp["x", l + 1] = swap(res[0], sent(c, ("x", l + 1)))
        kp["res", l] = res[1]
        kp["kept", l] = res[2:]

    def grads_before(c, key):
        return [] if c == 0 else list(keep[c - 1][key])

    side_run = (3 * groups + 2) // 2
    stash = pltpu.HBM((groups, side_run, half, 2 * width), BF16)
    stash_places = [
        pltpu.VMEM((groups, 2 * side_run, half, 2 * width), BF16),
        pltpu.SemaphoreType.DMA((8 * groups,)),
    ]

    def middle(c, l):
        first, count = chunks[c]
        kp = keep[c]
        n = count * QUARTER
        before = grads_before(c, ("grads", l))
        hidden = pltpu.VMEM((groups * nup * width, n), BF16)
        names = ("out_t", "up_t", "down_t", "down", "up", "out")
        w_at = 3
        res = call(
            functools.partial(middle_body, groups, first * QUARTER, n, bool(before)), "middle",
            [kp["far", l], cot_parts, kp["res", l - 1], *(dense[l][name] for name in names), vecs[l], *before],
            [parts(count, 2 * width), pltpu.HBM((fg, n), F32), stash, stash], [here, core_at],
            scratch=[hidden, hidden, *stash_places, *weight_places(names)],
            far=[*range(w_at, w_at + 6), w_at + 7, w_at + 8], far_outs=[2, 3],
            flops=6 * n * groups * square * (groups + 2 * nup),
        )
        kp["dctx", l] = swap(res[0], sent(c, ("dctx", l)))
        kp["dr", l], kp["grads", l] = res[1], res[2:]

    def late(c, l):
        first, count = chunks[c]
        kp = keep[c]
        n = count * QUARTER
        before = grads_before(c, ("grads", l))
        names = ("down", "up", "out")
        w_at = 8
        hidden = pltpu.VMEM((groups * nup * width, n), BF16)
        res = call(
            functools.partial(late_body, groups, bool(before)), "late",
            [kp["dx", l + 1], kp["far", l], kp["dr", l + 1], *kp["kept", l],
             *(dense[l][name] for name in names), vecs[l], *before],
            [parts(count, 2 * width), stash, stash], [here, core_at],
            scratch=[*stash_places, *weight_places(names), hidden, hidden, pltpu.SemaphoreType.DMA((2 * groups,))],
            far=[w_at - 2, w_at - 1, *range(w_at, w_at + 3), w_at + 4, w_at + 5], far_outs=[1, 2],
            flops=4 * n * groups * square * (groups + 2 * nup),
        )
        kp["dctx", l] = swap(res[0], sent(c, ("dctx", l)))
        kp["grads", l] = res[1:]

    def attend_back(c, l):
        first, count = chunks[c]
        kp = keep[c]
        here_tokens = count * length
        shifted = pl.BlockSpec((width, length), lambda i, *s: (0, i + first))
        seg_spec = pl.BlockSpec((1, 1, length), lambda i, *s: (i + first, 0, 0))
        operands = [kp["dctx", l], kp["ctx", l], kp["qkv", l], kp["lse", l], tokens if l == 0 else kp["xl", l], segs,
                    w_qkv[l]]
        specs = [quart(2 * width), tok(width), tok(3 * width), tok(per_group), shifted if l == 0 else tok(width),
                                      seg_spec, whole(3, width, width)]
        outs = [jax.ShapeDtypeStruct((3, half, 2 * width), BF16), table(width, 2)]
        out_specs = [whole(3, half, 2 * width), whole(width, 2)]
        scratch = [pltpu.VMEM((width, length), BF16), pltpu.VMEM((3, width, width), F32),
                   pltpu.VMEM((2, width, LANES), F32)]
        name = "grad" if l == 0 else "out"
        aliases, follows = None, state[name] is not None
        if follows:
            aliases = {len(operands): 0}
            operands.append(state[name])
            specs.append(pl.BlockSpec(memory_space=pl.ANY))
        if l:
            outs = [parts(count)] + outs
            out_specs = [quart()] + out_specs
            scratch.append(pltpu.VMEM((width, length), F32))
        res = call(
            functools.partial(attend_back_body, l == 0, per_group, groups, follows), "attend_back", operands,
            [table(width, tokens_here)] + outs, (), (count,), specs, [shifted] + out_specs, scratch, aliases,
            here_tokens * (12 * square + 10 * width * length),
            after=[gate] if l == 0 and follows else (), vmem=VMEM_ATTEND,
        )
        state[name] = res[0]
        if l:
            kp["dx", l] = swap(res[1], sent(c, ("dx", l)))
        kp["gqkv", l], kp["gvec", l] = res[-2:]

    def both(key, l):
        return sum(kp[key, l].astype(F32) for kp in keep)

    def scattered(l):
        kept, give = keep[-1]["grads", l]
        give, _ = lax.optimization_barrier((give, keep[0]["dctx", l]))
        got = peer(give, 1, "row")
        if l:
            return lax.psum_scatter(kept + got, "grp", scatter_dimension=0)

        def part(k):
            return lax.dynamic_index_in_dim(kept, me ^ k, 0, False) + lax.dynamic_index_in_dim(got, me ^ k, 0, False)

        return sum(peer(part(k), k).astype(F32) if k else part(k).astype(F32) for k in range(groups)).astype(BF16)

    def side_blocks(l, after=None):
        rows = jnp.pad(both("gvec", l).T, ((0, half - 2), (0, width)))
        all_four = jnp.concatenate([both("gqkv", l), rows[None]], axis=0).astype(BF16)
        if after is not None:
            all_four, _ = lax.optimization_barrier((all_four, after))
        mine = lax.dynamic_slice_in_dim(all_four, 2 * core, 2)
        return mine + peer(lax.dynamic_slice_in_dim(all_four, 2 - 2 * core, 2), 1, "row")

    class ChipSum:
        def __init__(self, value):
            self.shape = value.shape
            self.flat = value.reshape(-1, 2 * width)
            self.rows = self.flat.shape[0] // 2
            self.high = lax.rem(own_row // 2, 2)

        def first(self, after=None):
            give = lax.dynamic_slice_in_dim(self.flat, (1 - self.high) * self.rows, self.rows)
            if after is not None:
                give, _ = lax.optimization_barrier((give, after))
            got = peer(give, 2, "row")
            self.mine = lax.dynamic_slice_in_dim(self.flat, self.high * self.rows, self.rows) + got
            return got

        def second(self, after=None):
            got, step = None, 4
            while step < lax.axis_size("row"):
                give = self.mine
                if after is not None:
                    give, _ = lax.optimization_barrier((give, after))
                got = peer(give, step, "row")
                self.mine = self.mine + got
                step *= 2
            return got

        def third(self):
            return peer(self.mine, 2, "row")

        def whole(self, other):
            first = self.high == 0
            parts = [jnp.where(first, self.mine, other), jnp.where(first, other, self.mine)]
            return jnp.concatenate(parts, axis=0).reshape(self.shape)

        def all(self, after=None):
            self.first(after)
            self.second()
            return self.whole(self.third())

    assert LAYERS == 2
    count = len(chunks)
    ends = [None] * LAYERS

    def run(f, l):
        for c in range(count):
            f(c, l)

    run(attend, 0)
    got, _ = lax.optimization_barrier((exchanged[0][0], Line.token))
    exchanged[0] = ahead = [got, peer(got, 1, "row")]
    for kp in keep:
        kp["far", 0] = ahead = swap(kp["parts"], ahead)
    arrange(0)
    run(early, 0)
    fetch(1, (keep[0]["far", 0], dense[0]["out"]))
    run(attend, 1)
    arrange(1)
    run(middle, 1)
    run(attend_back, 1)
    chips = ChipSum(jnp.concatenate([scattered(1), side_blocks(1)], axis=0))
    run(late, 0)
    gate = chips.first(keep[0]["dctx", 0])
    big = ChipSum(scattered(0)).all()
    run(attend_back, 0)
    second = chips.second()
    third = chips.third()
    total = chips.whole(third)
    ends[1] = [total, peer(total, 1, "row")]
    total = jnp.concatenate([big, ChipSum(side_blocks(0, second)).all()], axis=0)
    ends[0] = [total, peer(total, 1, "row")]
    sources = ends[0] + ends[1]

    span = side_run + 2

    def places_of(side, at):
        return jnp.where(side == core, 0, span) + at

    j, i = jnp.arange(3 * groups, dtype=jnp.int32), jnp.arange(3, dtype=jnp.int32)
    one = jnp.concatenate([places_of(i // 2, side_run + i % 2), places_of(j // side_run, j % side_run)])
    places = (jnp.arange(LAYERS, dtype=jnp.int32)[:, None] * (2 * span) + one[None, :]).reshape(-1)
    targets = own_row * capacity + jnp.arange(capacity, dtype=jnp.int32)
    match = ids.reshape(-1)[None, :] == targets[:, None]
    place = jnp.sum(jnp.where(match, places[None, :], 0), axis=1)
    place = jnp.where(jnp.any(match, axis=1), place, 1 << 20).astype(jnp.int32)
    own_grads = collect(place, sources, width).reshape(1, capacity, square)

    def vector_rows(l):
        odd = jnp.where(core == 1, sources[2 * l], sources[2 * l + 1])
        rest = odd[3 * groups - side_run]
        return jnp.concatenate([odd[side_run + 1, :2, :width], rest[: nv - 2, :width]], axis=0).astype(F32)

    summed_vectors = jnp.stack([vector_rows(l) for l in range(LAYERS)], axis=0)
    new_masters, new_first, new_second = adam_step(
        masters, own_grads, first_moment, second_moment, WEIGHT_DECAY, LEARN_RATE
    )
    new_vectors, new_vector_first, new_vector_second = adam_step(
        vectors, summed_vectors, vector_first, vector_second, 0.0, VECTOR_RATE
    )
    return (
        state["out"],
        state["grad"],
        new_masters,
        new_first,
        new_second,
        new_vectors,
        new_vector_first,
        new_vector_second,
    )


def solution(mesh):
    in_specs = (
        P("grp", "row"),
        P("row", None),
        P(),
        P("grp", "row", None),
        P("grp", "row", None),
        P("grp", "row", None),
        P(None, None, "grp"),
        P(None, None, "grp"),
        P(None, None, "grp"),
        P("grp", "row"),
    )
    out_specs = (
        P("grp", "row"),
        P("grp", "row"),
        P("grp", "row", None),
        P("grp", "row", None),
        P("grp", "row", None),
        P(None, None, "grp"),
        P(None, None, "grp"),
        P(None, None, "grp"),
    )
    return jax.shard_map(shards, mesh=mesh, in_specs=in_specs, out_specs=out_specs, check_vma=False)
```

```python
import functools
import math

import jax
import jax.numpy as jnp
import numpy as np
from jax import lax
from jax.experimental import pallas as pl
from jax.experimental.pallas import tpu as pltpu
from jax.sharding import PartitionSpec as P

HEADS = 12
LAYERS = 2
STEP = 7
BETA_ONE = 0.9
BETA_TWO = 0.999
LEARN_RATE = 0.1
VECTOR_RATE = 0.5
WEIGHT_DECAY = 0.01
ADAM_EPSILON = 1e-08
NORM_EPSILON = 1e-12
MASK_FILL = -1e30
AUG = 16
QUARTER = 128
LANES = 128
VMEM_LIMIT = 56 * 1024 * 1024
VMEM_ATTEND = 56 * 1024 * 1024
F32 = jnp.float32
BF16 = jnp.bfloat16


def CHUNKS(sequences):
    return [(sequences + 1) // 2, sequences // 2]


def nn(a, b):
    return lax.dot_general(a, b, (((1,), (0,)), ((), ())), preferred_element_type=F32)


def nt(a, b):
    return lax.dot_general(a, b, (((1,), (1,)), ((), ())), preferred_element_type=F32)


def tn(a, b):
    return lax.dot_general(a, b, (((0,), (0,)), ((), ())), preferred_element_type=F32)


def block_layout(groups, layers):
    counts = []
    block_matrix = []
    block_step = []
    for layer_index in range(layers):
        for matrix_type in range(6):
            amount = 1 if matrix_type < 3 else groups
            for position in range(amount):
                block_matrix.append(layer_index * 6 + matrix_type)
                block_step.append(position)
            counts.append(amount)
    return (
        np.array(counts, np.int32),
        np.array(block_matrix, np.int32),
        np.array(block_step, np.int32),
    )


def slot_index(owners, groups, layers, capacity):
    counts, block_matrix, block_step = block_layout(groups, layers)
    matrix_ids = jnp.arange(counts.shape[0], dtype=jnp.int32)
    same_owner = owners[:, None] == owners[None, :]
    earlier = matrix_ids[None, :] < matrix_ids[:, None]
    slot_of = jnp.sum(
        jnp.where(same_owner & earlier, jnp.asarray(counts, jnp.int32)[None, :], 0), axis=1
    )
    starts = owners * capacity + slot_of
    choose = (jnp.asarray(block_matrix, jnp.int32)[:, None] == matrix_ids[None, :]).astype(
        jnp.int32
    )
    return jnp.sum(choose * starts[None, :], axis=1) + jnp.asarray(block_step, jnp.int32)


def pack(square):
    half = square.shape[0] // 2
    return jnp.concatenate([square[:half], square[half:]], axis=1)


def unpack(packed):
    width = packed.shape[1] // 2
    return jnp.concatenate([packed[:, :width], packed[:, width:]], axis=0)


def lanes(value):
    total = value[:, :LANES]
    for at in range(LANES, value.shape[1], LANES):
        total = total + value[:, at : at + LANES]
    return total


def row_totals(value):
    return jnp.sum(lanes(value), axis=1, keepdims=True)


def accumulate(ref, index, value):
    first = pl.program_id(0) == 0

    @pl.when(first)
    def _():
        ref[index] = value

    @pl.when(jnp.logical_not(first))
    def _():
        ref[index] = ref[index] + value


def split3(value):
    high = value.astype(BF16)
    rest = value - high.astype(F32)
    mid = rest.astype(BF16)
    last = (rest - mid.astype(F32)).astype(BF16)
    return high, mid, last


def segment_rows(segs):
    row = lax.broadcasted_iota(jnp.int32, (AUG, segs.shape[1]), 0)
    same = row == segs
    query_rows = jnp.where(same | (row >= 4), 0.0, MASK_FILL)
    key_rows = jnp.where(same | ((row >= 4) & (row < 7)), 1.0, 0.0)
    return query_rows, key_rows.astype(BF16)


def with_rows(query_rows, value):
    high, mid, last = split3(-value)
    row = lax.broadcasted_iota(jnp.int32, query_rows.shape, 0)
    out = jnp.where(row == 4, high.astype(F32), query_rows)
    out = jnp.where(row == 5, mid.astype(F32), out)
    out = jnp.where(row == 6, last.astype(F32), out)
    return out.astype(BF16)


def norm_cdf(u):
    a = jnp.abs(u) * math.sqrt(0.5)
    t = 1.0 / (1.0 + 0.3275911 * a)
    bell = jnp.exp(-a * a)
    poly = t * (
        0.254829592
        + t * (-0.284496736 + t * (1.421413741 + t * (-1.453152027 + t * 1.061405429)))
    )
    tail = (0.5 * poly) * bell
    return jnp.where(u < 0, tail, 1.0 - tail), bell * (1.0 / math.sqrt(2.0 * math.pi))


def attend_body(first, per_group, groups, *refs):
    if first:
        x_ref, seg_ref, w_ref, vec_ref, qkv_ref, ctx_ref, lse_ref, sent = refs
    else:
        pieces, seg_ref, w_ref, vec_ref, x_ref, qkv_ref, ctx_ref, lse_ref, sent = refs
        for j in range(groups):
            x_ref[:, j * QUARTER : (j + 1) * QUARTER] = pieces[j]
    x = x_ref[...]
    width = x.shape[0]
    size = width // per_group
    vec = vec_ref[...]
    q = (nn(w_ref[0], x) + vec[:, 0:1]).astype(BF16)
    k = nn(w_ref[1], x).astype(BF16)
    v = (nn(w_ref[2], x) + vec[:, 1:2]).astype(BF16)
    qkv_ref[0:width] = q
    qkv_ref[width : 2 * width] = k
    qkv_ref[2 * width : 3 * width] = v
    query_rows, key_rows = segment_rows(seg_ref[0])
    query_rows = query_rows.astype(BF16)
    parts = [slice(h * size, (h + 1) * size) for h in range(per_group)]
    scaled = q * jnp.asarray(size ** (-0.5), BF16)
    scores = [
        tn(jnp.concatenate([k[p], key_rows], axis=0), jnp.concatenate([scaled[p], query_rows], axis=0))
        for p in parts
    ]
    tops = [jnp.max(s, axis=0, keepdims=True) for s in scores]
    powers = [jnp.exp(s - top) for s, top in zip(scores, tops)]
    totals = [jnp.sum(e, axis=0, keepdims=True) for e in powers]
    chances = [(e * (1.0 / total)).astype(BF16) for e, total in zip(powers, totals)]
    for h, p in enumerate(parts):
        ctx_ref[p] = nn(v[p], chances[h]).astype(BF16)
        lse_ref[h : h + 1] = tops[h] + jnp.log(totals[h])
    for j in range(groups):
        sent[j] = ctx_ref[:, j * QUARTER : (j + 1) * QUARTER]


def attend_back_body(first, per_group, groups, follows, pieces, *refs):
    ctx_ref, qkv_ref, lse_ref, x_ref, seg_ref, w_ref = refs[:6]
    refs = refs[6 + follows :]
    if first:
        dx_ref, gqkv_ref, acc_ref, dctx_ref, gsum_ref, asum_ref = refs
    else:
        out_ref, sent, gqkv_ref, acc_ref, dctx_ref, gsum_ref, asum_ref, dx_ref = refs
    width, length = ctx_ref.shape
    size = width // per_group
    scale = size ** (-0.5)
    for j in range(groups):
        cols = slice(j * QUARTER, (j + 1) * QUARTER)
        dctx_ref[:, cols] = pieces[j, :width]
        if not first:
            out_ref[:, cols] = pieces[j, width:].astype(F32)
    ctx = ctx_ref[...]
    dctx = dctx_ref[...]
    x = x_ref[...]
    query_rows, key_rows = segment_rows(seg_ref[0])
    zero_rows = jnp.zeros_like(query_rows)
    q = qkv_ref[0:width]
    k = qkv_ref[width : 2 * width]
    v = qkv_ref[2 * width : 3 * width]
    dq, dk, dv = [], [], []
    for h in range(per_group):
        part = slice(h * size, (h + 1) * size)
        qh, kh, vh, dch = q[part], k[part], v[part], dctx[part]
        qs = qh * jnp.asarray(scale, BF16)
        delta = jnp.sum(dch.astype(F32) * ctx[part].astype(F32), axis=0, keepdims=True)
        qa = jnp.concatenate([qs, with_rows(query_rows, lse_ref[h : h + 1])], axis=0)
        ka = jnp.concatenate([kh, key_rows], axis=0)
        da = jnp.concatenate([dch, with_rows(zero_rows, delta)], axis=0)
        va = jnp.concatenate([vh, key_rows], axis=0)
        p = jnp.exp(tn(ka, qa))
        ds = (p * tn(va, da)).astype(BF16)
        dv.append(nt(dch, p.astype(BF16)))
        dq.append(nn(kh, ds) * scale)
        dk.append(nt(qs, ds))
    dq, dk, dv = (jnp.concatenate(parts, axis=0) for parts in (dq, dk, dv))
    accumulate(asum_ref, 0, lanes(dq))
    accumulate(asum_ref, 1, lanes(dv))
    low = jnp.concatenate([grad.astype(BF16) for grad in (dq, dk, dv)], axis=0)
    dx = nn(jnp.concatenate([w_ref[at] for at in range(3)], axis=1), low)
    grads = nt(x, low)
    for at in range(3):
        accumulate(gsum_ref, at, grads[:, at * width : (at + 1) * width])
    dx_ref[...] = dx
    for j in range(groups):
        cols = slice(j * QUARTER, (j + 1) * QUARTER)
        if first:
            dx_ref[:, cols] = dx_ref[:, cols] + pieces[j, width:].astype(F32)
        else:
            sent[j] = dx_ref[:, cols].astype(BF16)

    @pl.when(pl.program_id(0) == pl.num_programs(0) - 1)
    def _():
        for at in range(3):
            gqkv_ref[at] = pack(gsum_ref[at].astype(BF16))
        acc_ref[...] = jnp.concatenate(
            [jnp.sum(asum_ref[row], axis=1, keepdims=True) for row in range(2)], axis=1
        )


def norm(value):
    centre = jnp.mean(value, axis=0, keepdims=True)
    off = value - centre
    inverse = lax.rsqrt(jnp.mean(off * off, axis=0, keepdims=True) + NORM_EPSILON)
    return off * inverse, inverse


def norm_back(grad, gain, normed, inverse):
    e = grad * gain
    return inverse * (
        e - jnp.mean(e, axis=0, keepdims=True) - normed * jnp.mean(e * normed, axis=0, keepdims=True)
    )


def columns(vec_ref, row):
    return jnp.concatenate([vec_ref[a][:, row : row + 1] for a in range(vec_ref.shape[0])], axis=0)


def layer_forward(x, ctx, w, vec_ref, hid_ref, gp_ref, done=lambda a: None):
    groups, width, nv = vec_ref.shape
    nup = nv - 8
    r1 = x + (nn(w["out_t"][...], ctx) + columns(vec_ref, 2))
    n1, i1 = norm(r1)
    y1 = n1 * columns(vec_ref, 4 + nup) + columns(vec_ref, 5 + nup)
    yl = y1.astype(BF16)
    branch = []
    for a in range(groups):
        own = yl[a * width : (a + 1) * width]
        for j in range(nup):
            rows = slice(j * width, (j + 1) * width)
            u = nn(w["up_t"][a, rows], own) + vec_ref[a][:, 3 + j : 4 + j]
            cdf, bell = norm_cdf(u)
            at = slice((a * nup + j) * width, (a * nup + j + 1) * width)
            hid_ref[at] = (u * cdf).astype(BF16)
            gp_ref[at] = (cdf + u * bell).astype(BF16)
        done(a)
        branch.append(nn(w["down_t"][a], hid_ref[a * nup * width : (a + 1) * nup * width]))
    r2 = y1 + (jnp.concatenate(branch, axis=0) + columns(vec_ref, 3 + nup))
    n2, i2 = norm(r2)
    x2 = n2 * columns(vec_ref, 6 + nup) + columns(vec_ref, 7 + nup)
    return x2, n1, i1, yl, n2, i2


def layer_backward(dy, ctx, w, vec_ref, n1, i1, yl, n2, i2, hid_ref, gp_ref, sums_out, ready=lambda a: None):
    put = sums_out.put
    groups, width, nv = vec_ref.shape
    nup = nv - 8
    hidden = nup * width
    sums = [None] * (nv - 2)
    sums[6 + nup - 2 + 0] = row_totals(dy * n2)
    sums[7 + nup - 2 + 0] = row_totals(dy)
    dz = norm_back(dy, columns(vec_ref, 6 + nup), n2, i2)
    sums[3 + nup - 2] = row_totals(dz)
    dzl = dz.astype(BF16)
    sums_out.ready()
    back = []
    bias = [[] for _ in range(nup)]
    for a in range(groups):
        own = slice(a * width, (a + 1) * width)
        every = slice(a * nup * width, (a + 1) * nup * width)
        ready(a)
        grads = nt(hid_ref[every], dzl[own])
        dh = nn(w["down"][a], dzl[own])
        lows = []
        for j in range(nup):
            rows = slice(j * width, (j + 1) * width)
            put(a, groups + nup + j, grads[rows])
            du = dh[rows] * gp_ref[(a * nup + j) * width : (a * nup + j + 1) * width].astype(F32)
            bias[j].append(row_totals(du))
            lows.append(du.astype(BF16))
        dul = jnp.concatenate(lows, axis=0)
        grads = nt(yl[own], dul)
        for j in range(nup):
            put(a, groups + j, grads[:, j * width : (j + 1) * width])
        back.append(nn(w["up"][a], dul))
        sums_out.send(a, groups, 2 * nup)
    for j in range(nup):
        sums[3 + j - 2] = jnp.concatenate(bias[j], axis=0)
    dy1 = dz + jnp.concatenate(back, axis=0)
    sums[4 + nup - 2] = row_totals(dy1 * n1)
    sums[5 + nup - 2] = row_totals(dy1)
    dr1 = norm_back(dy1, columns(vec_ref, 4 + nup), n1, i1)
    sums[0] = row_totals(dr1)
    dal = dr1.astype(BF16)
    dctx = nn(w["out"][...], dal).astype(BF16)
    context = ctx()
    for a in range(groups):
        own = nt(context[a * width : (a + 1) * width], dal)
        for b in range(groups):
            put(a, a ^ b, own[:, b * width : (b + 1) * width])
        sums_out.send(a, 0, groups)
    stack = jnp.concatenate(sums, axis=1)
    for a in range(groups):
        flat = jnp.concatenate(
            [stack[a * width : (a + 1) * width], jnp.zeros((width, LANES - len(sums)), F32)], axis=1
        ).T
        flat = flat[: width // 2]
        put(a, groups + 2 * nup, jnp.concatenate([flat, jnp.zeros_like(flat)], axis=1), packed=True)
        sums_out.send(a, groups + 2 * nup, 1)
    return dr1, dctx


WEIGHTS = ("out", "out_t", "up", "up_t", "down", "down_t")


class Fetched:
    def __init__(self, names, sources, places, sems):
        self.places = dict(zip(names, places))
        self.copies = {
            name: pltpu.make_async_copy(source, place, sems.at[at])
            for at, (name, source, place) in enumerate(zip(names, sources, places))
        }
        for copy in self.copies.values():
            copy.start()

    def __getitem__(self, name):
        copy = self.copies.pop(name, None)
        if copy is not None:
            copy.wait()
        return self.places[name]


class Sums:
    def __init__(self, me, core, keep_ref, give_ref, held_ref, before, sems):
        self.me, self.core, self.refs, self.held, self.sems = me, core, (keep_ref, give_ref), held_ref, sems
        self.run = keep_ref.shape[1]
        self.used, self.sent, self.loads, self.before = 0, [], [], before is not None
        if self.before:
            for a in range(held_ref.shape[0]):
                for side in range(2):
                    held = held_ref.at[a, pl.ds(side * self.run, self.run)]
                    self.loads.append(self.either(side, [ref.at[a ^ me] for ref in before], held, False))

    def either(self, side, places, held, out):
        sem = self.sems.at[self.used]
        self.used += 1
        keep, give = (
            pltpu.make_async_copy(held, place, sem) if out else pltpu.make_async_copy(place, held, sem)
            for place in places
        )
        pl.when(self.core == side)(keep.start)
        pl.when(self.core != side)(give.start)
        return keep

    def ready(self):
        for load in self.loads:
            load.wait()

    def put(self, a, j, block, packed=False):
        block = block if packed else pack(block)
        if self.before:
            block = block + self.held[a, j].astype(F32)
        self.held[a, j] = block.astype(BF16)

    def send(self, a, first, count):
        for side in range(2):
            low, high = max(first, side * self.run), min(first + count, (side + 1) * self.run)
            if low < high:
                part = pl.ds(low - side * self.run, high - low)
                places = [ref.at[a ^ self.me, part] for ref in self.refs]
                self.sent.append(self.either(side, places, self.held.at[a, pl.ds(low, high - low)], True))

    def finish(self):
        for copy in self.sent:
            copy.wait()


def joined(me, ref, rows=slice(None), cols=slice(None)):
    return jnp.concatenate([ref[a ^ me, rows, cols] for a in range(ref.shape[0])], axis=0)


def early_body(groups, first, count, me_ref, ctx_ref, x_ref, *refs):
    names = ("out_t", "up_t", "down_t")
    w_refs, vec_ref, sent = refs[:3], refs[3], refs[4]
    x2_ref, n1_ref, n2_ref, inv_ref, far_hid, far_gp = refs[5:11]
    w = Fetched(names, w_refs, refs[11:14], refs[14])
    hid_ref, gp_ref, sems = refs[15:]
    me, width = me_ref[0], vec_ref.shape[1]
    copies = []

    def done(a):
        rows = pl.ds(a * (hid_ref.shape[0] // groups), hid_ref.shape[0] // groups)
        for ref, far in ((hid_ref, far_hid), (gp_ref, far_gp)):
            copies.append(pltpu.make_async_copy(ref.at[rows], far.at[rows], sems.at[len(copies)]))
            copies[-1].start()

    start = joined(me, x_ref, cols=slice(first, first + count)).astype(F32)
    x2, n1, i1, _, n2, i2 = layer_forward(start, joined(me, ctx_ref), w, vec_ref, hid_ref, gp_ref, done)
    x2_ref[...] = x2
    for a in range(groups):
        sent[a ^ me] = x2[a * width : (a + 1) * width].astype(BF16)
    n1_ref[...] = n1.astype(BF16)
    n2_ref[...] = n2.astype(BF16)
    inv_ref[...] = jnp.concatenate([i1, i2], axis=0)
    for copy in copies:
        copy.wait()


def middle_body(groups, first, count, follows, me_ref, core_ref, ctx_ref, cot_ref, x_ref, *refs):
    names = ("out_t", "up_t", "down_t", "down", "up", "out")
    w_refs, vec_ref, refs = refs[:6], refs[6], refs[7:]
    before = None
    if follows:
        before, refs = refs[:2], refs[2:]
    sent, dr_ref, keep_ref, give_ref, hid_ref, gp_ref, held_ref, grad_sems = refs[:8]
    w = Fetched((*names, "cot"), (*w_refs, cot_ref), refs[8:15], refs[15])
    me, width = me_ref[0], vec_ref.shape[1]
    sums_out = Sums(me, core_ref[0], keep_ref, give_ref, held_ref, before, grad_sems)
    ctx = joined(me, ctx_ref)
    x2, n1, i1, yl, n2, i2 = layer_forward(x_ref[...], ctx, w, vec_ref, hid_ref, gp_ref)
    for a in range(groups):
        sent[a ^ me, width:] = x2[a * width : (a + 1) * width].astype(BF16)
    dy = joined(me, w["cot"], cols=slice(first, first + count)).astype(F32)
    dr1, dctx = layer_backward(dy, lambda: ctx, w, vec_ref, n1, i1, yl, n2, i2, hid_ref, gp_ref, sums_out)
    dr_ref[...] = dr1
    for a in range(groups):
        sent[a ^ me, :width] = dctx[a * width : (a + 1) * width]
    sums_out.finish()


def late_body(groups, follows, me_ref, core_ref, got_ref, ctx_ref, *refs):
    names = ("down", "up", "out")
    dr_ref, n1_ref, n2_ref, inv_ref, far_hid, far_gp = refs[:6]
    w_refs, vec_ref, refs = refs[6:9], refs[9], refs[10:]
    before = None
    if follows:
        before, refs = refs[:2], refs[2:]
    sent, keep_ref, give_ref, held_ref, grad_sems = refs[:5]
    w = Fetched((*names, "ctx"), (*w_refs, ctx_ref), refs[5:9], refs[9])
    hid_ref, gp_ref, sems = refs[10:]
    copies = []
    for a in range(groups):
        rows = pl.ds(a * (hid_ref.shape[0] // groups), hid_ref.shape[0] // groups)
        for ref, far in ((hid_ref, far_hid), (gp_ref, far_gp)):
            copies.append(pltpu.make_async_copy(far.at[rows], ref.at[rows], sems.at[len(copies)]))
            copies[-1].start()

    def ready(a):
        copies[2 * a].wait()
        copies[2 * a + 1].wait()

    me, width = me_ref[0], vec_ref.shape[1]
    sums_out = Sums(me, core_ref[0], keep_ref, give_ref, held_ref, before, grad_sems)
    nup = vec_ref.shape[2] - 8
    dy = dr_ref[...] + joined(me, got_ref).astype(F32)
    n1, n2 = n1_ref[...].astype(F32), n2_ref[...].astype(F32)
    yl = (n1 * columns(vec_ref, 4 + nup) + columns(vec_ref, 5 + nup)).astype(BF16)
    inv = inv_ref[...]
    dr1, dctx = layer_backward(
        dy, lambda: joined(me, w["ctx"]), w, vec_ref, n1, inv[0:1], yl, n2, inv[1:2], hid_ref, gp_ref, sums_out, ready
    )
    for a in range(groups):
        sent[a ^ me, :width] = dctx[a * width : (a + 1) * width]
        sent[a ^ me, width:] = dr1[a * width : (a + 1) * width].astype(BF16)
    sums_out.finish()


def scatter_body(groups, *refs):
    for source, out in zip(refs[: len(refs) // 2], refs[len(refs) // 2 :]):
        for j in range(groups):
            out[j] = source[:, j * QUARTER : (j + 1) * QUARTER].astype(BF16)


def scatter_quarters(arrays, groups):
    width, tokens = arrays[0].shape
    length = QUARTER * groups
    count = tokens // length
    return pl.pallas_call(
        functools.partial(scatter_body, groups),
        grid=(count,),
        in_specs=[pl.BlockSpec((width, length), lambda i: (0, i))] * len(arrays),
        out_specs=[pl.BlockSpec((groups, width, QUARTER), lambda i: (0, 0, i))] * len(arrays),
        out_shape=[jax.ShapeDtypeStruct((groups, width, QUARTER * count), BF16)] * len(arrays),
        name="scatter_quarters",
    )(*arrays)


def pick_body(jobs, ids_ref, source, *refs):
    outs, held, sems = refs[:-2], refs[-2], refs[-1]
    copies = []
    for at in range(held.shape[0]):
        copies.append(pltpu.make_async_copy(source.at[ids_ref[at]], held.at[at], sems.at[at]))
        copies[-1].start()
    at, out = 0, 0
    for count, times in jobs:
        for one in range(count):
            copies[at].wait()
            if times:
                for copy in range(times):
                    outs[out][copy, one] = held[at]
            else:
                block = unpack(held[at])
                outs[out][one] = block
                outs[out + 1][one] = block.T
            at += 1
        out += 1 if times else 2


def pick(jobs, ids, source):
    half, double = source.shape[1:]
    shapes = []
    for count, times in jobs:
        shapes += [(times, count, half, double)] if times else [(count, double // 2, double // 2)] * 2
    total = sum(count for count, _ in jobs)
    return pl.pallas_call(
        functools.partial(pick_body, jobs),
        grid_spec=pltpu.PrefetchScalarGridSpec(
            num_scalar_prefetch=1,
            grid=(1,),
            in_specs=[pl.BlockSpec(memory_space=pltpu.HBM)],
            out_specs=[pl.BlockSpec(shape, lambda i, ids, n=len(shape): (0,) * n) for shape in shapes],
            scratch_shapes=[pltpu.VMEM((total, half, double), BF16), pltpu.SemaphoreType.DMA((total,))],
        ),
        out_shape=[jax.ShapeDtypeStruct(shape, BF16) for shape in shapes],
        name="pick",
    )(ids, source)


def arrange_body(groups, nup, sources, core_ref, me_ref, *refs):
    far_blocks, refs = refs[:sources], refs[sources:]
    far, w, sems = dict(zip(WEIGHTS, refs[:6])), dict(zip(WEIGHTS, refs[6:12])), refs[12]
    held, load_sems = refs[13:-1], refs[-1]
    got, other = held[0], held[1] if sources == 2 else None
    copies = []

    def send(name, index):
        copies.append(pltpu.make_async_copy(w[name].at[index], far[name].at[index], sems.at[len(copies)]))
        copies[-1].start()

    me = me_ref[0]
    share = got.shape[1]
    width = got.shape[3] // 2
    even = core_ref[0] == 0
    loads = [
        [
            pltpu.make_async_copy(source.at[a ^ me], place.at[a], load_sems.at[at * groups + a])
            for at, (source, place) in enumerate(zip(far_blocks, held))
        ]
        for a in range(groups)
    ]
    for load in loads:
        for copy in load:
            copy.start()

    def block(a, j):
        if other is None:
            return unpack(got[a, j])
        near, distant = got[a, j % share], other[a, j % share]
        return unpack(jnp.where(even, near, distant) if j < share else jnp.where(even, distant, near))

    for a in range(groups):
        for copy in loads[a]:
            copy.wait()
        rows = slice(a * width, (a + 1) * width)
        line = [block(a, a ^ b) for b in range(groups)]
        w["out"][rows] = jnp.concatenate(line, axis=1)
        ups = [block(a, groups + j) for j in range(nup)]
        w["up"][a] = jnp.concatenate(ups, axis=1)
        w["up_t"][a] = jnp.concatenate([up.T for up in ups], axis=0)
        downs = [block(a, groups + nup + j) for j in range(nup)]
        w["down"][a] = jnp.concatenate(downs, axis=0)
        w["down_t"][a] = jnp.concatenate([down.T for down in downs], axis=1)
        send("out", pl.ds(a * width, width))
        for name in WEIGHTS[2:]:
            send(name, a)
    for b in range(groups):
        w["out_t"][b * width : (b + 1) * width] = jnp.concatenate(
            [block(a, a ^ b).T for a in range(groups)], axis=1
        )
        send("out_t", pl.ds(b * width, width))
    for copy in copies:
        copy.wait()


def collect_body(edges, ids_ref, *refs):
    sources, out_ref, held, sems = refs[: len(edges)], refs[-3], refs[-2], refs[-1]
    slots = out_ref.shape[0]
    for slot in range(slots):
        at, low = ids_ref[slot], 0
        for source, high in zip(sources, edges):

            @pl.when((at >= low) & (at < high))
            def _(source=source, place=at - low, slot=slot):
                pltpu.make_async_copy(source.at[place], held.at[slot], sems.at[slot]).start()

            low = high
    for slot in range(slots):
        there = ids_ref[slot] < edges[-1]

        @pl.when(there)
        def _(slot=slot):
            pltpu.make_async_copy(sources[0].at[0], held.at[slot], sems.at[slot]).wait()
            out_ref[slot] = unpack(held[slot]).astype(F32)

        @pl.when(jnp.logical_not(there))
        def _(slot=slot):
            out_ref[slot] = jnp.zeros(out_ref.shape[1:], F32)


def collect(places, sources, width):
    edges = tuple(int(edge) for edge in np.cumsum([source.shape[0] for source in sources]))
    slots, size = places.shape[0], sources[0].shape[1:]
    return pl.pallas_call(
        functools.partial(collect_body, edges),
        grid_spec=pltpu.PrefetchScalarGridSpec(
            num_scalar_prefetch=1,
            grid=(1,),
            in_specs=[HBM_SPEC] * len(sources),
            out_specs=pl.BlockSpec((slots, width, width), lambda i, ids: (0, 0, 0)),
            scratch_shapes=[pltpu.VMEM((slots, *size), BF16), pltpu.SemaphoreType.DMA((slots,))],
        ),
        out_shape=table(slots, width, width),
        name="collect",
    )(places, *sources)


def table(*shape):
    return jax.ShapeDtypeStruct(shape, F32)


class Line:
    token = None


HBM_SPEC = pl.BlockSpec(memory_space=pltpu.HBM)


def call(body, name, operands, outs, scalars=(), grid=None, specs=None, out_specs=None, scratch=(), aliases=None,
         flops=0, after=(), far=(), far_outs=(), vmem=VMEM_LIMIT):
    behind = [array for array in (Line.token, *after) if array is not None]
    skip, ahead = len(behind), len(scalars)
    plain, made = body, len(outs)
    inputs = len(operands)
    whole = pl.BlockSpec(memory_space=pltpu.VMEM)

    def body(*refs):
        first, refs = refs[:ahead], refs[ahead + skip :]
        ins, results, rest = refs[:inputs], refs[inputs : inputs + made], refs[inputs + made + 1 :]
        refs[inputs + made][...] = jnp.zeros((8, LANES), F32)
        plain(*first, *ins, *results, *rest)

    any_spec = pl.BlockSpec(memory_space=pl.ANY)
    moved = sum(math.prod(array.shape) * array.dtype.itemsize for array in (*operands, *outs))
    common = dict(
        out_shape=[*outs, table(8, LANES)],
        name=name,
        input_output_aliases={at + ahead + skip: to for at, to in (aliases or {}).items()},
        compiler_params=pltpu.CompilerParams(vmem_limit_bytes=vmem),
        cost_estimate=pl.CostEstimate(flops=int(flops), bytes_accessed=int(moved), transcendentals=0),
    )
    if grid is None:
        smem = pl.BlockSpec(memory_space=pltpu.SMEM)
        res = pl.pallas_call(
            body,
            in_specs=[smem] * ahead + [any_spec] * skip
            + [HBM_SPEC if at in far else whole for at in range(inputs)],
            out_specs=[HBM_SPEC if at in far_outs else whole for at in range(made)] + [whole],
            scratch_shapes=list(scratch),
            **common,
        )(*scalars, *behind, *operands)
    else:
        res = pl.pallas_call(
            body,
            grid_spec=pltpu.PrefetchScalarGridSpec(
                num_scalar_prefetch=ahead,
                grid=grid,
                in_specs=[any_spec] * skip + list(specs),
                out_specs=list(out_specs) + [pl.BlockSpec((8, LANES), lambda i, *s: (0, 0))],
                scratch_shapes=list(scratch),
            ),
            **common,
        )(*scalars, *behind, *operands)
    Line.token = res[-1]
    return list(res[:-1])


def peer(value, step, axis="grp"):
    count = lax.axis_size(axis)
    return lax.ppermute(value, axis, [(i, i ^ step) for i in range(count)])


def swap(parts, after=None):
    if after is not None:
        parts, _ = lax.optimization_barrier((parts, after))
    return lax.all_to_all(parts, "grp", split_axis=0, concat_axis=0)


def adam_step(param, grad, first, second, decay, rate):
    first_new = BETA_ONE * first + (1.0 - BETA_ONE) * grad
    second_new = BETA_TWO * second + (1.0 - BETA_TWO) * grad * grad
    first_hat = first_new / (1.0 - BETA_ONE**STEP)
    second_hat = second_new / (1.0 - BETA_TWO**STEP)
    updated = param - rate * (first_hat / (jnp.sqrt(second_hat) + ADAM_EPSILON) + decay * param)
    return (updated, first_new, second_new)


def shards(
    tokens,
    segments,
    owners,
    masters,
    first_moment,
    second_moment,
    vectors,
    vector_first,
    vector_second,
    cotangent,
):
    groups = lax.axis_size("grp")
    me = lax.axis_index("grp").astype(jnp.int32)
    own_row = lax.axis_index("row").astype(jnp.int32)
    core = lax.rem(own_row, 2)
    capacity = masters.shape[1]
    width, tokens_here = tokens.shape
    half = width // 2
    fg = groups * width
    sequences, length = segments.shape
    per_group = HEADS // groups
    nv = vectors.shape[1]
    nup = nv - 8
    per_layer = 3 + 3 * groups
    segs = segments.reshape(sequences, 1, length)
    order = jnp.arange(groups, dtype=jnp.int32) ^ me
    here, core_at = me.reshape(1), core.reshape(1)
    square = width * width

    block_index = slot_index(owners, groups, LAYERS, capacity)
    ids = block_index.reshape(LAYERS, per_layer)
    relative = jnp.take(ids[:, 3 : 3 + groups], order, axis=1, mode="clip")
    ids = jnp.concatenate([ids[:, :3], relative, ids[:, 3 + groups :]], axis=1)
    local_blocks = masters[0].astype(BF16).reshape(capacity, 2, half, width)
    local_blocks = jnp.concatenate([local_blocks[:, 0], local_blocks[:, 1]], axis=2)
    everyone = lax.all_gather(local_blocks, "row", axis=0, tiled=True)

    x_parts, cot_parts = (swap(part) for part in scatter_quarters([tokens, cotangent], groups))
    vec_all = jnp.stack([vectors] + [peer(vectors, k) for k in range(1, groups)]).transpose(1, 0, 3, 2)
    vecs = [vec_all[l] for l in range(LAYERS)]
    own_vecs = [vec_all[l, 0] for l in range(LAYERS)]

    share = (3 * groups) // 2
    dense, exchanged = [None] * LAYERS, [None] * LAYERS
    source, _ = lax.optimization_barrier((everyone, (vec_all, x_parts, cot_parts)))
    mine = lax.dynamic_slice(ids[0], (3 + core * share,), (share,))
    (send,) = pick([(share, groups)], mine, source)
    exchanged[0] = [swap(send)]
    others = [(3, 0) for _ in range(LAYERS)] + [(3 * groups, 1) for _ in range(1, LAYERS)]
    wanted = [ids[l, :3] for l in range(LAYERS)] + [ids[l, 3:] for l in range(1, LAYERS)]
    picked = pick(others, jnp.concatenate(wanted), source)
    w_qkv, w_turned = picked[0 : 2 * LAYERS : 2], picked[1 : 2 * LAYERS : 2]

    def fetch(l, after):
        own, _ = lax.optimization_barrier((picked[2 * LAYERS + l - 1][0], after))
        exchanged[l] = [lax.all_gather(own, "grp", axis=0)]

    def arrange(l):
        got = exchanged[l]
        shapes = [(fg, fg), (fg, fg), (groups, width, fg), (groups, fg, width), (groups, fg, width), (groups, width, fg)]
        smem = pl.BlockSpec(memory_space=pltpu.SMEM)
        res = pl.pallas_call(
            functools.partial(arrange_body, groups, nup, len(got)),
            in_specs=[smem, smem] + [HBM_SPEC] * len(got),
            out_specs=[HBM_SPEC] * 6,
            scratch_shapes=[pltpu.VMEM(shape, BF16) for shape in shapes] + [pltpu.SemaphoreType.DMA((6 * groups,))]
            + [pltpu.VMEM(array.shape, BF16) for array in got] + [pltpu.SemaphoreType.DMA((len(got) * groups,))],
            out_shape=[pltpu.HBM(shape, BF16) for shape in shapes],
            name="arrange",
            compiler_params=pltpu.CompilerParams(vmem_limit_bytes=VMEM_LIMIT),
        )(core_at, here, *got)
        dense[l] = dict(zip(WEIGHTS, res))

    def weight_places(names, *more):
        shapes = {"out": (fg, fg), "up": (groups, width, fg), "down": (groups, fg, width)}
        shapes |= {"out_t": (fg, fg), "up_t": (groups, fg, width), "down_t": (groups, width, fg)}
        places = [pltpu.VMEM(shapes[name], BF16) for name in names] + [pltpu.VMEM(shape, BF16) for shape in more]
        return places + [pltpu.SemaphoreType.DMA((len(places),))]

    chunks, at = [], 0
    for count in CHUNKS(sequences):
        chunks.append((at, count))
        at += count
    keep = [dict() for _ in chunks]
    state = {"out": None, "grad": None}
    Line.token = None

    def tok(rows):
        return pl.BlockSpec((rows, length), lambda i, *s: (0, i))

    def quart(rows=width):
        return pl.BlockSpec((groups, rows, QUARTER), lambda i, *s: (0, 0, i))

    def parts(count, rows=width):
        return jax.ShapeDtypeStruct((groups, rows, count * QUARTER), BF16)

    def whole(*shape):
        return pl.BlockSpec(shape, lambda i, *s: (0,) * len(shape))

    def sent(c, key):
        return keep[c - 1][key] if c else None

    def attend(c, l):
        first, count = chunks[c]
        kp = keep[c]
        here_tokens = count * length
        shifted = pl.BlockSpec((width, length), lambda i, *s: (0, i + first))
        seg_spec = pl.BlockSpec((1, 1, length), lambda i, *s: (i + first, 0, 0))
        operands = [segs, w_turned[l], own_vecs[l]]
        specs = [seg_spec, whole(3, width, width), whole(width, nv)]
        outs = [pltpu.HBM((3 * width, here_tokens), BF16), pltpu.HBM((width, here_tokens), BF16),
                pltpu.HBM((per_group, here_tokens), F32)]
        out_specs = [tok(3 * width), tok(width), tok(per_group)]
        outs.append(parts(count))
        out_specs.append(quart())
        if l == 0:
            operands, specs = [tokens] + operands, [shifted] + specs
        else:
            operands, specs = [kp["x", l]] + operands, [quart()] + specs
            outs = [pltpu.HBM((width, here_tokens), BF16)] + outs
            out_specs = [tok(width)] + out_specs
        res = call(
            functools.partial(attend_body, l == 0, per_group, groups), "attend", operands, outs, (),
            (count,), specs, out_specs, flops=here_tokens * (6 * square + 4 * width * length), vmem=VMEM_ATTEND,
        )
        if l:
            kp["xl", l] = res.pop(0)
        kp["qkv", l], kp["ctx", l], kp["lse", l] = res[:3]
        if l:
            kp["far", l] = swap(res[3], sent(c, ("far", l)))
        else:
            kp["parts"] = res[3]

    def early(c, l):
        first, count = chunks[c]
        kp = keep[c]
        n = count * QUARTER
        names = ("out_t", "up_t", "down_t")
        hidden = pltpu.VMEM((groups * nup * width, n), BF16)
        outs = [parts(count), pltpu.HBM((fg, n), F32), pltpu.HBM((fg, n), BF16), pltpu.HBM((fg, n), BF16),
                pltpu.HBM((2, n), F32)] + [pltpu.HBM((groups * nup * width, n), BF16)] * 2
        res = call(
            functools.partial(early_body, groups, first * QUARTER, n), "early",
            [kp["far", l], x_parts, *(dense[l][name] for name in names), vecs[l]], outs, [here],
            scratch=[*weight_places(names), hidden, hidden, pltpu.SemaphoreType.DMA((2 * groups,))],
            far=range(2, 5), far_outs=[5, 6],
            flops=2 * n * groups * square * (groups + 2 * nup),
        )
        kp["x", l + 1] = swap(res[0], sent(c, ("x", l + 1)))
        kp["res", l] = res[1]
        kp["kept", l] = res[2:]

    def grads_before(c, key):
        return [] if c == 0 else list(keep[c - 1][key])

    side_run = (3 * groups + 2) // 2
    stash = pltpu.HBM((groups, side_run, half, 2 * width), BF16)
    stash_places = [
        pltpu.VMEM((groups, 2 * side_run, half, 2 * width), BF16),
        pltpu.SemaphoreType.DMA((8 * groups,)),
    ]

    def middle(c, l):
        first, count = chunks[c]
        kp = keep[c]
        n = count * QUARTER
        before = grads_before(c, ("grads", l))
        hidden = pltpu.VMEM((groups * nup * width, n), BF16)
        names = ("out_t", "up_t", "down_t", "down", "up", "out")
        w_at = 3
        res = call(
            functools.partial(middle_body, groups, first * QUARTER, n, bool(before)), "middle",
            [kp["far", l], cot_parts, kp["res", l - 1], *(dense[l][name] for name in names), vecs[l], *before],
            [parts(count, 2 * width), pltpu.HBM((fg, n), F32), stash, stash], [here, core_at],
            scratch=[hidden, hidden, *stash_places, *weight_places(names, cot_parts.shape)],
            far=[1, *range(w_at, w_at + 6), w_at + 7, w_at + 8], far_outs=[2, 3],
            flops=6 * n * groups * square * (groups + 2 * nup),
        )
        kp["dctx", l] = swap(res[0], sent(c, ("dctx", l)))
        kp["dr", l], kp["grads", l] = res[1], res[2:]

    def late(c, l):
        first, count = chunks[c]
        kp = keep[c]
        n = count * QUARTER
        before = grads_before(c, ("grads", l))
        names = ("down", "up", "out")
        w_at = 8
        hidden = pltpu.VMEM((groups * nup * width, n), BF16)
        res = call(
            functools.partial(late_body, groups, bool(before)), "late",
            [kp["dx", l + 1], kp["far", l], kp["dr", l + 1], *kp["kept", l],
             *(dense[l][name] for name in names), vecs[l], *before],
            [parts(count, 2 * width), stash, stash], [here, core_at],
            scratch=[*stash_places, *weight_places(names, kp["far", l].shape), hidden, hidden,
                     pltpu.SemaphoreType.DMA((2 * groups,))],
            far=[1, w_at - 2, w_at - 1, *range(w_at, w_at + 3), w_at + 4, w_at + 5], far_outs=[1, 2],
            flops=4 * n * groups * square * (groups + 2 * nup),
        )
        kp["dctx", l] = swap(res[0], sent(c, ("dctx", l)))
        kp["grads", l] = res[1:]

    def attend_back(c, l):
        first, count = chunks[c]
        kp = keep[c]
        here_tokens = count * length
        shifted = pl.BlockSpec((width, length), lambda i, *s: (0, i + first))
        seg_spec = pl.BlockSpec((1, 1, length), lambda i, *s: (i + first, 0, 0))
        operands = [kp["dctx", l], kp["ctx", l], kp["qkv", l], kp["lse", l], tokens if l == 0 else kp["xl", l], segs,
                    w_qkv[l]]
        specs = [quart(2 * width), tok(width), tok(3 * width), tok(per_group), shifted if l == 0 else tok(width),
                                      seg_spec, whole(3, width, width)]
        outs = [jax.ShapeDtypeStruct((3, half, 2 * width), BF16), table(width, 2)]
        out_specs = [whole(3, half, 2 * width), whole(width, 2)]
        scratch = [pltpu.VMEM((width, length), BF16), pltpu.VMEM((3, width, width), F32),
                   pltpu.VMEM((2, width, LANES), F32)]
        name = "grad" if l == 0 else "out"
        aliases, follows = None, state[name] is not None
        if follows:
            aliases = {len(operands): 0}
            operands.append(state[name])
            specs.append(pl.BlockSpec(memory_space=pl.ANY))
        if l:
            outs = [parts(count)] + outs
            out_specs = [quart()] + out_specs
            scratch.append(pltpu.VMEM((width, length), F32))
        res = call(
            functools.partial(attend_back_body, l == 0, per_group, groups, follows), "attend_back", operands,
            [table(width, tokens_here)] + outs, (), (count,), specs, [shifted] + out_specs, scratch, aliases,
            here_tokens * (12 * square + 10 * width * length),
            after=[gate] if l == 0 and follows else (), vmem=VMEM_ATTEND,
        )
        state[name] = res[0]
        if l:
            kp["dx", l] = swap(res[1], sent(c, ("dx", l)))
        kp["gqkv", l], kp["gvec", l] = res[-2:]

    def both(key, l):
        return sum(kp[key, l].astype(F32) for kp in keep)

    def scattered(l):
        kept, give = keep[-1]["grads", l]
        give, _ = lax.optimization_barrier((give, keep[0]["dctx", l]))
        got = peer(give, 1, "row")
        if l:
            return lax.psum_scatter(kept + got, "grp", scatter_dimension=0)

        def part(k):
            return lax.dynamic_index_in_dim(kept, me ^ k, 0, False) + lax.dynamic_index_in_dim(got, me ^ k, 0, False)

        return sum(peer(part(k), k).astype(F32) if k else part(k).astype(F32) for k in range(groups)).astype(BF16)

    def side_blocks(l, after=None):
        rows = jnp.pad(both("gvec", l).T, ((0, half - 2), (0, width)))
        all_four = jnp.concatenate([both("gqkv", l), rows[None]], axis=0).astype(BF16)
        if after is not None:
            all_four, _ = lax.optimization_barrier((all_four, after))
        mine = lax.dynamic_slice_in_dim(all_four, 2 * core, 2)
        return mine + peer(lax.dynamic_slice_in_dim(all_four, 2 - 2 * core, 2), 1, "row")

    class ChipSum:
        def __init__(self, value):
            self.shape = value.shape
            self.flat = value.reshape(-1, 2 * width)
            self.rows = self.flat.shape[0] // 2
            self.high = lax.rem(own_row // 2, 2)

        def first(self, after=None):
            give = lax.dynamic_slice_in_dim(self.flat, (1 - self.high) * self.rows, self.rows)
            if after is not None:
                give, _ = lax.optimization_barrier((give, after))
            got = peer(give, 2, "row")
            self.mine = lax.dynamic_slice_in_dim(self.flat, self.high * self.rows, self.rows) + got
            return got

        def second(self, after=None):
            got, step = None, 4
            while step < lax.axis_size("row"):
                give = self.mine
                if after is not None:
                    give, _ = lax.optimization_barrier((give, after))
                got = peer(give, step, "row")
                self.mine = self.mine + got
                step *= 2
            return got

        def third(self):
            return peer(self.mine, 2, "row")

        def whole(self, other):
            first = self.high == 0
            parts = [jnp.where(first, self.mine, other), jnp.where(first, other, self.mine)]
            return jnp.concatenate(parts, axis=0).reshape(self.shape)

        def all(self, after=None):
            self.first(after)
            self.second()
            return self.whole(self.third())

    assert LAYERS == 2
    count = len(chunks)
    ends = [None] * LAYERS

    def run(f, l):
        for c in range(count):
            f(c, l)

    run(attend, 0)
    got, _ = lax.optimization_barrier((exchanged[0][0], Line.token))
    exchanged[0] = [got, peer(got, 1, "row")]
    ahead = got
    for kp in keep:
        kp["far", 0] = ahead = swap(kp["parts"], ahead)
    arrange(0)
    run(early, 0)
    fetch(1, (keep[0]["far", 0], dense[0]["out"]))
    run(attend, 1)
    arrange(1)
    run(middle, 1)
    run(attend_back, 1)
    chips = ChipSum(jnp.concatenate([scattered(1), side_blocks(1)], axis=0))
    run(late, 0)
    gate = chips.first(keep[0]["dctx", 0])
    big = ChipSum(scattered(0)).all()
    run(attend_back, 0)
    second = chips.second()
    third = chips.third()
    total = chips.whole(third)
    ends[1] = [total, peer(total, 1, "row")]
    total = jnp.concatenate([big, ChipSum(side_blocks(0, second)).all()], axis=0)
    ends[0] = [total, peer(total, 1, "row")]
    sources = ends[0] + ends[1]

    span = side_run + 2

    def places_of(side, at):
        return jnp.where(side == core, 0, span) + at

    j, i = jnp.arange(3 * groups, dtype=jnp.int32), jnp.arange(3, dtype=jnp.int32)
    one = jnp.concatenate([places_of(i // 2, side_run + i % 2), places_of(j // side_run, j % side_run)])
    places = (jnp.arange(LAYERS, dtype=jnp.int32)[:, None] * (2 * span) + one[None, :]).reshape(-1)
    targets = own_row * capacity + jnp.arange(capacity, dtype=jnp.int32)
    match = ids.reshape(-1)[None, :] == targets[:, None]
    place = jnp.sum(jnp.where(match, places[None, :], 0), axis=1)
    place = jnp.where(jnp.any(match, axis=1), place, 1 << 20).astype(jnp.int32)
    own_grads = collect(place, sources, width).reshape(1, capacity, square)

    def vector_rows(l):
        odd = jnp.where(core == 1, sources[2 * l], sources[2 * l + 1])
        rest = odd[3 * groups - side_run]
        return jnp.concatenate([odd[side_run + 1, :2, :width], rest[: nv - 2, :width]], axis=0).astype(F32)

    summed_vectors = jnp.stack([vector_rows(l) for l in range(LAYERS)], axis=1)
    new_masters, new_first, new_second = adam_step(
        masters, own_grads, first_moment, second_moment, WEIGHT_DECAY, LEARN_RATE
    )
    rows_first = (array.transpose(1, 0, 2) for array in (vectors, vector_first, vector_second))
    vector, first, second = rows_first
    new_vectors, new_vector_first, new_vector_second = (
        array.transpose(1, 0, 2) for array in adam_step(vector, summed_vectors, first, second, 0.0, VECTOR_RATE)
    )
    return (
        state["out"],
        state["grad"],
        new_masters,
        new_first,
        new_second,
        new_vectors,
        new_vector_first,
        new_vector_second,
    )


def solution(mesh):
    in_specs = (
        P("grp", "row"),
        P("row", None),
        P(),
        P("grp", "row", None),
        P("grp", "row", None),
        P("grp", "row", None),
        P(None, None, "grp"),
        P(None, None, "grp"),
        P(None, None, "grp"),
        P("grp", "row"),
    )
    out_specs = (
        P("grp", "row"),
        P("grp", "row"),
        P("grp", "row", None),
        P("grp", "row", None),
        P("grp", "row", None),
        P(None, None, "grp"),
        P(None, None, "grp"),
        P(None, None, "grp"),
    )
    return jax.shard_map(shards, mesh=mesh, in_specs=in_specs, out_specs=out_specs, check_vma=False)
```

```python
import functools
import math

import jax
import jax.numpy as jnp
import numpy as np
from jax import lax
from jax.experimental import pallas as pl
from jax.experimental.pallas import tpu as pltpu
from jax.sharding import PartitionSpec as P

HEADS = 12
LAYERS = 2
STEP = 7
BETA_ONE = 0.9
BETA_TWO = 0.999
LEARN_RATE = 0.1
VECTOR_RATE = 0.5
WEIGHT_DECAY = 0.01
ADAM_EPSILON = 1e-08
NORM_EPSILON = 1e-12
MASK_FILL = -1e30
AUG = 16
QUARTER = 128
LANES = 128
VMEM_LIMIT = 56 * 1024 * 1024
VMEM_ATTEND = 56 * 1024 * 1024
F32 = jnp.float32
BF16 = jnp.bfloat16


def CHUNKS(sequences):
    return [(sequences + 1) // 2, sequences // 2]


def nn(a, b):
    return lax.dot_general(a, b, (((1,), (0,)), ((), ())), preferred_element_type=F32)


def nt(a, b):
    return lax.dot_general(a, b, (((1,), (1,)), ((), ())), preferred_element_type=F32)


def tn(a, b):
    return lax.dot_general(a, b, (((0,), (0,)), ((), ())), preferred_element_type=F32)


def block_layout(groups, layers):
    counts = []
    block_matrix = []
    block_step = []
    for layer_index in range(layers):
        for matrix_type in range(6):
            amount = 1 if matrix_type < 3 else groups
            for position in range(amount):
                block_matrix.append(layer_index * 6 + matrix_type)
                block_step.append(position)
            counts.append(amount)
    return (
        np.array(counts, np.int32),
        np.array(block_matrix, np.int32),
        np.array(block_step, np.int32),
    )


def slot_index(owners, groups, layers, capacity):
    counts, block_matrix, block_step = block_layout(groups, layers)
    matrix_ids = jnp.arange(counts.shape[0], dtype=jnp.int32)
    same_owner = owners[:, None] == owners[None, :]
    earlier = matrix_ids[None, :] < matrix_ids[:, None]
    slot_of = jnp.sum(
        jnp.where(same_owner & earlier, jnp.asarray(counts, jnp.int32)[None, :], 0), axis=1
    )
    starts = owners * capacity + slot_of
    choose = (jnp.asarray(block_matrix, jnp.int32)[:, None] == matrix_ids[None, :]).astype(
        jnp.int32
    )
    return jnp.sum(choose * starts[None, :], axis=1) + jnp.asarray(block_step, jnp.int32)


def pack(square):
    half = square.shape[0] // 2
    return jnp.concatenate([square[:half], square[half:]], axis=1)


def unpack(packed):
    width = packed.shape[1] // 2
    return jnp.concatenate([packed[:, :width], packed[:, width:]], axis=0)


def lanes(value):
    total = value[:, :LANES]
    for at in range(LANES, value.shape[1], LANES):
        total = total + value[:, at : at + LANES]
    return total


def row_totals(value):
    return jnp.sum(lanes(value), axis=1, keepdims=True)


def accumulate(ref, index, value):
    first = pl.program_id(0) == 0

    @pl.when(first)
    def _():
        ref[index] = value

    @pl.when(jnp.logical_not(first))
    def _():
        ref[index] = ref[index] + value


def split3(value):
    high = value.astype(BF16)
    rest = value - high.astype(F32)
    mid = rest.astype(BF16)
    last = (rest - mid.astype(F32)).astype(BF16)
    return high, mid, last


def segment_rows(segs):
    row = lax.broadcasted_iota(jnp.int32, (AUG, segs.shape[1]), 0)
    same = row == segs
    query_rows = jnp.where(same | (row >= 4), 0.0, MASK_FILL)
    key_rows = jnp.where(same | ((row >= 4) & (row < 7)), 1.0, 0.0)
    return query_rows, key_rows.astype(BF16)


def with_rows(query_rows, value):
    high, mid, last = split3(-value)
    row = lax.broadcasted_iota(jnp.int32, query_rows.shape, 0)
    out = jnp.where(row == 4, high.astype(F32), query_rows)
    out = jnp.where(row == 5, mid.astype(F32), out)
    out = jnp.where(row == 6, last.astype(F32), out)
    return out.astype(BF16)


def norm_cdf(u):
    a = jnp.abs(u) * math.sqrt(0.5)
    t = 1.0 / (1.0 + 0.3275911 * a)
    bell = jnp.exp(-a * a)
    poly = t * (
        0.254829592
        + t * (-0.284496736 + t * (1.421413741 + t * (-1.453152027 + t * 1.061405429)))
    )
    tail = (0.5 * poly) * bell
    return jnp.where(u < 0, tail, 1.0 - tail), bell * (1.0 / math.sqrt(2.0 * math.pi))


def attend_body(first, per_group, groups, *refs):
    if first:
        x_ref, seg_ref, w_ref, vec_ref, qkv_ref, ctx_ref, lse_ref, sent = refs
    else:
        pieces, seg_ref, w_ref, vec_ref, x_ref, qkv_ref, ctx_ref, lse_ref, sent = refs
        for j in range(groups):
            x_ref[:, j * QUARTER : (j + 1) * QUARTER] = pieces[j]
    x = x_ref[...]
    width = x.shape[0]
    size = width // per_group
    vec = vec_ref[...]
    q = (nn(w_ref[0], x) + vec[:, 0:1]).astype(BF16)
    k = nn(w_ref[1], x).astype(BF16)
    v = (nn(w_ref[2], x) + vec[:, 1:2]).astype(BF16)
    qkv_ref[0:width] = q
    qkv_ref[width : 2 * width] = k
    qkv_ref[2 * width : 3 * width] = v
    query_rows, key_rows = segment_rows(seg_ref[0])
    query_rows = query_rows.astype(BF16)
    parts = [slice(h * size, (h + 1) * size) for h in range(per_group)]
    scaled = q * jnp.asarray(size ** (-0.5), BF16)
    scores = [
        tn(jnp.concatenate([k[p], key_rows], axis=0), jnp.concatenate([scaled[p], query_rows], axis=0))
        for p in parts
    ]
    tops = [jnp.max(s, axis=0, keepdims=True) for s in scores]
    powers = [jnp.exp(s - top) for s, top in zip(scores, tops)]
    totals = [jnp.sum(e, axis=0, keepdims=True) for e in powers]
    chances = [(e * (1.0 / total)).astype(BF16) for e, total in zip(powers, totals)]
    for h, p in enumerate(parts):
        ctx_ref[p] = nn(v[p], chances[h]).astype(BF16)
        lse_ref[h : h + 1] = tops[h] + jnp.log(totals[h])
    for j in range(groups):
        sent[j] = ctx_ref[:, j * QUARTER : (j + 1) * QUARTER]


def attend_back_body(first, per_group, groups, follows, pieces, *refs):
    ctx_ref, qkv_ref, lse_ref, x_ref, seg_ref, w_ref = refs[:6]
    refs = refs[6 + follows :]
    if first:
        dx_ref, gqkv_ref, acc_ref, dctx_ref, gsum_ref, asum_ref = refs
    else:
        out_ref, sent, gqkv_ref, acc_ref, dctx_ref, gsum_ref, asum_ref, dx_ref = refs
    width, length = ctx_ref.shape
    size = width // per_group
    scale = size ** (-0.5)
    for j in range(groups):
        cols = slice(j * QUARTER, (j + 1) * QUARTER)
        dctx_ref[:, cols] = pieces[j, :width]
        if not first:
            out_ref[:, cols] = pieces[j, width:].astype(F32)
    ctx = ctx_ref[...]
    dctx = dctx_ref[...]
    x = x_ref[...]
    query_rows, key_rows = segment_rows(seg_ref[0])
    zero_rows = jnp.zeros_like(query_rows)
    q = qkv_ref[0:width]
    k = qkv_ref[width : 2 * width]
    v = qkv_ref[2 * width : 3 * width]
    dq, dk, dv = [], [], []
    for h in range(per_group):
        part = slice(h * size, (h + 1) * size)
        qh, kh, vh, dch = q[part], k[part], v[part], dctx[part]
        qs = qh * jnp.asarray(scale, BF16)
        delta = jnp.sum(dch.astype(F32) * ctx[part].astype(F32), axis=0, keepdims=True)
        qa = jnp.concatenate([qs, with_rows(query_rows, lse_ref[h : h + 1])], axis=0)
        ka = jnp.concatenate([kh, key_rows], axis=0)
        da = jnp.concatenate([dch, with_rows(zero_rows, delta)], axis=0)
        va = jnp.concatenate([vh, key_rows], axis=0)
        p = jnp.exp(tn(ka, qa))
        ds = (p * tn(va, da)).astype(BF16)
        dv.append(nt(dch, p.astype(BF16)))
        dq.append(nn(kh, ds) * scale)
        dk.append(nt(qs, ds))
    dq, dk, dv = (jnp.concatenate(parts, axis=0) for parts in (dq, dk, dv))
    accumulate(asum_ref, 0, lanes(dq))
    accumulate(asum_ref, 1, lanes(dv))
    low = jnp.concatenate([grad.astype(BF16) for grad in (dq, dk, dv)], axis=0)
    dx = nn(jnp.concatenate([w_ref[at] for at in range(3)], axis=1), low)
    grads = nt(low, x)
    for at in range(3):
        accumulate(gsum_ref, at, grads[at * width : (at + 1) * width])
    dx_ref[...] = dx
    for j in range(groups):
        cols = slice(j * QUARTER, (j + 1) * QUARTER)
        if first:
            dx_ref[:, cols] = dx_ref[:, cols] + pieces[j, width:].astype(F32)
        else:
            sent[j] = dx_ref[:, cols].astype(BF16)

    @pl.when(pl.program_id(0) == pl.num_programs(0) - 1)
    def _():
        for at in range(3):
            gqkv_ref[at] = pack(gsum_ref[at].astype(BF16).T)
        acc_ref[...] = jnp.concatenate(
            [jnp.sum(asum_ref[row], axis=1, keepdims=True) for row in range(2)], axis=1
        )


def norm(value):
    centre = jnp.mean(value, axis=0, keepdims=True)
    off = value - centre
    inverse = lax.rsqrt(jnp.mean(off * off, axis=0, keepdims=True) + NORM_EPSILON)
    return off * inverse, inverse


def norm_back(grad, gain, normed, inverse):
    e = grad * gain
    return inverse * (
        e - jnp.mean(e, axis=0, keepdims=True) - normed * jnp.mean(e * normed, axis=0, keepdims=True)
    )


def columns(vec_ref, row):
    return jnp.concatenate([vec_ref[a][:, row : row + 1] for a in range(vec_ref.shape[0])], axis=0)


def layer_forward(x, ctx, w, vec_ref, hid_ref, gp_ref, done=lambda a: None):
    groups, width, nv = vec_ref.shape
    nup = nv - 8
    r1 = x + (nn(w["out_t"][...], ctx) + columns(vec_ref, 2))
    n1, i1 = norm(r1)
    y1 = n1 * columns(vec_ref, 4 + nup) + columns(vec_ref, 5 + nup)
    yl = y1.astype(BF16)
    branch = []
    for a in range(groups):
        own = yl[a * width : (a + 1) * width]
        for j in range(nup):
            rows = slice(j * width, (j + 1) * width)
            u = nn(w["up_t"][a, rows], own) + vec_ref[a][:, 3 + j : 4 + j]
            cdf, bell = norm_cdf(u)
            at = slice((a * nup + j) * width, (a * nup + j + 1) * width)
            hid_ref[at] = (u * cdf).astype(BF16)
            gp_ref[at] = (cdf + u * bell).astype(BF16)
        done(a)
        branch.append(nn(w["down_t"][a], hid_ref[a * nup * width : (a + 1) * nup * width]))
    r2 = y1 + (jnp.concatenate(branch, axis=0) + columns(vec_ref, 3 + nup))
    n2, i2 = norm(r2)
    x2 = n2 * columns(vec_ref, 6 + nup) + columns(vec_ref, 7 + nup)
    return x2, n1, i1, yl, n2, i2


def layer_backward(dy, ctx, w, vec_ref, n1, i1, yl, n2, i2, hid_ref, gp_ref, sums_out, ready=lambda a: None):
    put = sums_out.put
    groups, width, nv = vec_ref.shape
    nup = nv - 8
    hidden = nup * width
    sums = [None] * (nv - 2)
    sums[6 + nup - 2 + 0] = row_totals(dy * n2)
    sums[7 + nup - 2 + 0] = row_totals(dy)
    dz = norm_back(dy, columns(vec_ref, 6 + nup), n2, i2)
    sums[3 + nup - 2] = row_totals(dz)
    dzl = dz.astype(BF16)
    sums_out.ready()
    back = []
    bias = [[] for _ in range(nup)]
    for a in range(groups):
        own = slice(a * width, (a + 1) * width)
        every = slice(a * nup * width, (a + 1) * nup * width)
        ready(a)
        grads = nt(hid_ref[every], dzl[own])
        dh = nn(w["down"][a], dzl[own])
        lows = []
        for j in range(nup):
            rows = slice(j * width, (j + 1) * width)
            put(a, groups + nup + j, grads[rows])
            du = dh[rows] * gp_ref[(a * nup + j) * width : (a * nup + j + 1) * width].astype(F32)
            bias[j].append(row_totals(du))
            lows.append(du.astype(BF16))
        dul = jnp.concatenate(lows, axis=0)
        grads = nt(yl[own], dul)
        for j in range(nup):
            put(a, groups + j, grads[:, j * width : (j + 1) * width])
        back.append(nn(w["up"][a], dul))
        sums_out.send(a, groups, 2 * nup)
    for j in range(nup):
        sums[3 + j - 2] = jnp.concatenate(bias[j], axis=0)
    dy1 = dz + jnp.concatenate(back, axis=0)
    sums[4 + nup - 2] = row_totals(dy1 * n1)
    sums[5 + nup - 2] = row_totals(dy1)
    dr1 = norm_back(dy1, columns(vec_ref, 4 + nup), n1, i1)
    sums[0] = row_totals(dr1)
    dal = dr1.astype(BF16)
    dctx = nn(w["out"][...], dal).astype(BF16)
    context = ctx()
    for a in range(groups):
        own = nt(context[a * width : (a + 1) * width], dal)
        for b in range(groups):
            put(a, a ^ b, own[:, b * width : (b + 1) * width])
        sums_out.send(a, 0, groups)
    stack = jnp.concatenate(sums, axis=1)
    for a in range(groups):
        flat = jnp.concatenate(
            [stack[a * width : (a + 1) * width], jnp.zeros((width, LANES - len(sums)), F32)], axis=1
        ).T
        flat = flat[: width // 2]
        put(a, groups + 2 * nup, jnp.concatenate([flat, jnp.zeros_like(flat)], axis=1), packed=True)
        sums_out.send(a, groups + 2 * nup, 1)
    return dr1, dctx


WEIGHTS = ("out", "out_t", "up", "up_t", "down", "down_t")


class Fetched:
    def __init__(self, names, sources, places, sems):
        self.places = dict(zip(names, places))
        self.copies = {
            name: pltpu.make_async_copy(source, place, sems.at[at])
            for at, (name, source, place) in enumerate(zip(names, sources, places))
        }
        for copy in self.copies.values():
            copy.start()

    def __getitem__(self, name):
        copy = self.copies.pop(name, None)
        if copy is not None:
            copy.wait()
        return self.places[name]


class Sums:
    def __init__(self, me, core, keep_ref, give_ref, held_ref, before, sems):
        self.me, self.core, self.refs, self.held, self.sems = me, core, (keep_ref, give_ref), held_ref, sems
        self.run = keep_ref.shape[1]
        self.used, self.sent, self.loads, self.before = 0, [], [], before is not None
        if self.before:
            for a in range(held_ref.shape[0]):
                for side in range(2):
                    held = held_ref.at[a, pl.ds(side * self.run, self.run)]
                    self.loads.append(self.either(side, [ref.at[a ^ me] for ref in before], held, False))

    def either(self, side, places, held, out):
        sem = self.sems.at[self.used]
        self.used += 1
        keep, give = (
            pltpu.make_async_copy(held, place, sem) if out else pltpu.make_async_copy(place, held, sem)
            for place in places
        )
        pl.when(self.core == side)(keep.start)
        pl.when(self.core != side)(give.start)
        return keep

    def ready(self):
        for load in self.loads:
            load.wait()

    def put(self, a, j, block, packed=False):
        block = block if packed else pack(block)
        if self.before:
            block = block + self.held[a, j].astype(F32)
        self.held[a, j] = block.astype(BF16)

    def send(self, a, first, count):
        for side in range(2):
            low, high = max(first, side * self.run), min(first + count, (side + 1) * self.run)
            if low < high:
                part = pl.ds(low - side * self.run, high - low)
                places = [ref.at[a ^ self.me, part] for ref in self.refs]
                self.sent.append(self.either(side, places, self.held.at[a, pl.ds(low, high - low)], True))

    def finish(self):
        for copy in self.sent:
            copy.wait()


def joined(me, ref, rows=slice(None), cols=slice(None)):
    return jnp.concatenate([ref[a ^ me, rows, cols] for a in range(ref.shape[0])], axis=0)


def early_body(groups, first, count, me_ref, ctx_ref, x_ref, *refs):
    names = ("out_t", "up_t", "down_t")
    w_refs, vec_ref, sent = refs[:3], refs[3], refs[4]
    x2_ref, n1_ref, n2_ref, inv_ref, far_hid, far_gp = refs[5:11]
    w = Fetched(names, w_refs, refs[11:14], refs[14])
    hid_ref, gp_ref, sems = refs[15:]
    me, width = me_ref[0], vec_ref.shape[1]
    copies = []

    def done(a):
        rows = pl.ds(a * (hid_ref.shape[0] // groups), hid_ref.shape[0] // groups)
        for ref, far in ((hid_ref, far_hid), (gp_ref, far_gp)):
            copies.append(pltpu.make_async_copy(ref.at[rows], far.at[rows], sems.at[len(copies)]))
            copies[-1].start()

    start = joined(me, x_ref, cols=slice(first, first + count)).astype(F32)
    x2, n1, i1, _, n2, i2 = layer_forward(start, joined(me, ctx_ref), w, vec_ref, hid_ref, gp_ref, done)
    x2_ref[...] = x2
    for a in range(groups):
        sent[a ^ me] = x2[a * width : (a + 1) * width].astype(BF16)
    n1_ref[...] = n1.astype(BF16)
    n2_ref[...] = n2.astype(BF16)
    inv_ref[...] = jnp.concatenate([i1, i2], axis=0)
    for copy in copies:
        copy.wait()


def middle_body(groups, first, count, follows, me_ref, core_ref, ctx_ref, cot_ref, x_ref, *refs):
    names = ("out_t", "up_t", "down_t", "down", "up", "out")
    w_refs, vec_ref, refs = refs[:6], refs[6], refs[7:]
    before = None
    if follows:
        before, refs = refs[:2], refs[2:]
    sent, dr_ref, keep_ref, give_ref, hid_ref, gp_ref, held_ref, grad_sems = refs[:8]
    w = Fetched((*names, "cot"), (*w_refs, cot_ref), refs[8:15], refs[15])
    me, width = me_ref[0], vec_ref.shape[1]
    sums_out = Sums(me, core_ref[0], keep_ref, give_ref, held_ref, before, grad_sems)
    ctx = joined(me, ctx_ref)
    x2, n1, i1, yl, n2, i2 = layer_forward(x_ref[...], ctx, w, vec_ref, hid_ref, gp_ref)
    for a in range(groups):
        sent[a ^ me, width:] = x2[a * width : (a + 1) * width].astype(BF16)
    dy = joined(me, w["cot"], cols=slice(first, first + count)).astype(F32)
    dr1, dctx = layer_backward(dy, lambda: ctx, w, vec_ref, n1, i1, yl, n2, i2, hid_ref, gp_ref, sums_out)
    dr_ref[...] = dr1
    for a in range(groups):
        sent[a ^ me, :width] = dctx[a * width : (a + 1) * width]
    sums_out.finish()


def late_body(groups, follows, me_ref, core_ref, got_ref, ctx_ref, *refs):
    names = ("down", "up", "out")
    dr_ref, n1_ref, n2_ref, inv_ref, far_hid, far_gp = refs[:6]
    w_refs, vec_ref, refs = refs[6:9], refs[9], refs[10:]
    before = None
    if follows:
        before, refs = refs[:2], refs[2:]
    sent, keep_ref, give_ref, held_ref, grad_sems = refs[:5]
    w = Fetched((*names, "ctx"), (*w_refs, ctx_ref), refs[5:9], refs[9])
    hid_ref, gp_ref, sems = refs[10:]
    copies = []
    for a in range(groups):
        rows = pl.ds(a * (hid_ref.shape[0] // groups), hid_ref.shape[0] // groups)
        for ref, far in ((hid_ref, far_hid), (gp_ref, far_gp)):
            copies.append(pltpu.make_async_copy(far.at[rows], ref.at[rows], sems.at[len(copies)]))
            copies[-1].start()

    def ready(a):
        copies[2 * a].wait()
        copies[2 * a + 1].wait()

    me, width = me_ref[0], vec_ref.shape[1]
    sums_out = Sums(me, core_ref[0], keep_ref, give_ref, held_ref, before, grad_sems)
    nup = vec_ref.shape[2] - 8
    dy = dr_ref[...] + joined(me, got_ref).astype(F32)
    n1, n2 = n1_ref[...].astype(F32), n2_ref[...].astype(F32)
    yl = (n1 * columns(vec_ref, 4 + nup) + columns(vec_ref, 5 + nup)).astype(BF16)
    inv = inv_ref[...]
    dr1, dctx = layer_backward(
        dy, lambda: joined(me, w["ctx"]), w, vec_ref, n1, inv[0:1], yl, n2, inv[1:2], hid_ref, gp_ref, sums_out, ready
    )
    for a in range(groups):
        sent[a ^ me, :width] = dctx[a * width : (a + 1) * width]
        sent[a ^ me, width:] = dr1[a * width : (a + 1) * width].astype(BF16)
    sums_out.finish()


def scatter_body(groups, *refs):
    for source, out in zip(refs[: len(refs) // 2], refs[len(refs) // 2 :]):
        for j in range(groups):
            out[j] = source[:, j * QUARTER : (j + 1) * QUARTER].astype(BF16)


def scatter_quarters(arrays, groups):
    width, tokens = arrays[0].shape
    length = QUARTER * groups
    count = tokens // length
    return pl.pallas_call(
        functools.partial(scatter_body, groups),
        grid=(count,),
        in_specs=[pl.BlockSpec((width, length), lambda i: (0, i))] * len(arrays),
        out_specs=[pl.BlockSpec((groups, width, QUARTER), lambda i: (0, 0, i))] * len(arrays),
        out_shape=[jax.ShapeDtypeStruct((groups, width, QUARTER * count), BF16)] * len(arrays),
        name="scatter_quarters",
    )(*arrays)


def pick_body(jobs, ids_ref, source, *refs):
    outs, held, sems = refs[:-2], refs[-2], refs[-1]
    copies = []
    for at in range(held.shape[0]):
        copies.append(pltpu.make_async_copy(source.at[ids_ref[at]], held.at[at], sems.at[at]))
        copies[-1].start()
    at, out = 0, 0
    for count, times in jobs:
        for one in range(count):
            copies[at].wait()
            if times:
                for copy in range(times):
                    outs[out][copy, one] = held[at]
            else:
                block = unpack(held[at])
                outs[out][one] = block
                outs[out + 1][one] = block.T
            at += 1
        out += 1 if times else 2


def pick(jobs, ids, source):
    half, double = source.shape[1:]
    shapes = []
    for count, times in jobs:
        shapes += [(times, count, half, double)] if times else [(count, double // 2, double // 2)] * 2
    total = sum(count for count, _ in jobs)
    return pl.pallas_call(
        functools.partial(pick_body, jobs),
        grid_spec=pltpu.PrefetchScalarGridSpec(
            num_scalar_prefetch=1,
            grid=(1,),
            in_specs=[pl.BlockSpec(memory_space=pltpu.HBM)],
            out_specs=[pl.BlockSpec(shape, lambda i, ids, n=len(shape): (0,) * n) for shape in shapes],
            scratch_shapes=[pltpu.VMEM((total, half, double), BF16), pltpu.SemaphoreType.DMA((total,))],
        ),
        out_shape=[jax.ShapeDtypeStruct(shape, BF16) for shape in shapes],
        name="pick",
    )(ids, source)


def arrange_body(groups, nup, sources, core_ref, me_ref, *refs):
    far_blocks, refs = refs[:sources], refs[sources:]
    far, w, sems = dict(zip(WEIGHTS, refs[:6])), dict(zip(WEIGHTS, refs[6:12])), refs[12]
    held, load_sems = refs[13:-1], refs[-1]
    got, other = held[0], held[1] if sources == 2 else None
    copies = []

    def send(name, index):
        copies.append(pltpu.make_async_copy(w[name].at[index], far[name].at[index], sems.at[len(copies)]))
        copies[-1].start()

    me = me_ref[0]
    share = got.shape[1]
    width = got.shape[3] // 2
    even = core_ref[0] == 0
    loads = [
        [
            pltpu.make_async_copy(source.at[a ^ me], place.at[a], load_sems.at[at * groups + a])
            for at, (source, place) in enumerate(zip(far_blocks, held))
        ]
        for a in range(groups)
    ]
    for load in loads:
        for copy in load:
            copy.start()

    def block(a, j):
        if other is None:
            return unpack(got[a, j])
        near, distant = got[a, j % share], other[a, j % share]
        return unpack(jnp.where(even, near, distant) if j < share else jnp.where(even, distant, near))

    for a in range(groups):
        for copy in loads[a]:
            copy.wait()
        rows = slice(a * width, (a + 1) * width)
        line = [block(a, a ^ b) for b in range(groups)]
        w["out"][rows] = jnp.concatenate(line, axis=1)
        ups = [block(a, groups + j) for j in range(nup)]
        w["up"][a] = jnp.concatenate(ups, axis=1)
        w["up_t"][a] = jnp.concatenate([up.T for up in ups], axis=0)
        downs = [block(a, groups + nup + j) for j in range(nup)]
        w["down"][a] = jnp.concatenate(downs, axis=0)
        w["down_t"][a] = jnp.concatenate([down.T for down in downs], axis=1)
        send("out", pl.ds(a * width, width))
        for name in WEIGHTS[2:]:
            send(name, a)
    for b in range(groups):
        w["out_t"][b * width : (b + 1) * width] = jnp.concatenate(
            [block(a, a ^ b).T for a in range(groups)], axis=1
        )
        send("out_t", pl.ds(b * width, width))
    for copy in copies:
        copy.wait()


def collect_body(edges, ids_ref, *refs):
    sources, out_ref, held, sems = refs[: len(edges)], refs[-3], refs[-2], refs[-1]
    slots = out_ref.shape[0]
    for slot in range(slots):
        at, low = ids_ref[slot], 0
        for source, high in zip(sources, edges):

            @pl.when((at >= low) & (at < high))
            def _(source=source, place=at - low, slot=slot):
                pltpu.make_async_copy(source.at[place], held.at[slot], sems.at[slot]).start()

            low = high
    for slot in range(slots):
        there = ids_ref[slot] < edges[-1]

        @pl.when(there)
        def _(slot=slot):
            pltpu.make_async_copy(sources[0].at[0], held.at[slot], sems.at[slot]).wait()
            out_ref[slot] = unpack(held[slot]).astype(F32)

        @pl.when(jnp.logical_not(there))
        def _(slot=slot):
            out_ref[slot] = jnp.zeros(out_ref.shape[1:], F32)


def collect(places, sources, width):
    edges = tuple(int(edge) for edge in np.cumsum([source.shape[0] for source in sources]))
    slots, size = places.shape[0], sources[0].shape[1:]
    return pl.pallas_call(
        functools.partial(collect_body, edges),
        grid_spec=pltpu.PrefetchScalarGridSpec(
            num_scalar_prefetch=1,
            grid=(1,),
            in_specs=[HBM_SPEC] * len(sources),
            out_specs=pl.BlockSpec((slots, width, width), lambda i, ids: (0, 0, 0)),
            scratch_shapes=[pltpu.VMEM((slots, *size), BF16), pltpu.SemaphoreType.DMA((slots,))],
        ),
        out_shape=table(slots, width, width),
        name="collect",
    )(places, *sources)


def table(*shape):
    return jax.ShapeDtypeStruct(shape, F32)


class Line:
    token = None


HBM_SPEC = pl.BlockSpec(memory_space=pltpu.HBM)


def call(body, name, operands, outs, scalars=(), grid=None, specs=None, out_specs=None, scratch=(), aliases=None,
         flops=0, after=(), far=(), far_outs=(), vmem=VMEM_LIMIT):
    behind = [array for array in (Line.token, *after) if array is not None]
    skip, ahead = len(behind), len(scalars)
    plain, made = body, len(outs)
    inputs = len(operands)
    whole = pl.BlockSpec(memory_space=pltpu.VMEM)

    def body(*refs):
        first, refs = refs[:ahead], refs[ahead + skip :]
        ins, results, rest = refs[:inputs], refs[inputs : inputs + made], refs[inputs + made + 1 :]
        refs[inputs + made][...] = jnp.zeros((8, LANES), F32)
        plain(*first, *ins, *results, *rest)

    any_spec = pl.BlockSpec(memory_space=pl.ANY)
    moved = sum(math.prod(array.shape) * array.dtype.itemsize for array in (*operands, *outs))
    common = dict(
        out_shape=[*outs, table(8, LANES)],
        name=name,
        input_output_aliases={at + ahead + skip: to for at, to in (aliases or {}).items()},
        compiler_params=pltpu.CompilerParams(vmem_limit_bytes=vmem),
        cost_estimate=pl.CostEstimate(flops=int(flops), bytes_accessed=int(moved), transcendentals=0),
    )
    if grid is None:
        smem = pl.BlockSpec(memory_space=pltpu.SMEM)
        res = pl.pallas_call(
            body,
            in_specs=[smem] * ahead + [any_spec] * skip
            + [HBM_SPEC if at in far else whole for at in range(inputs)],
            out_specs=[HBM_SPEC if at in far_outs else whole for at in range(made)] + [whole],
            scratch_shapes=list(scratch),
            **common,
        )(*scalars, *behind, *operands)
    else:
        res = pl.pallas_call(
            body,
            grid_spec=pltpu.PrefetchScalarGridSpec(
                num_scalar_prefetch=ahead,
                grid=grid,
                in_specs=[any_spec] * skip + list(specs),
                out_specs=list(out_specs) + [pl.BlockSpec((8, LANES), lambda i, *s: (0, 0))],
                scratch_shapes=list(scratch),
            ),
            **common,
        )(*scalars, *behind, *operands)
    Line.token = res[-1]
    return list(res[:-1])


def peer(value, step, axis="grp"):
    count = lax.axis_size(axis)
    return lax.ppermute(value, axis, [(i, i ^ step) for i in range(count)])


def swap(parts, after=None):
    if after is not None:
        parts, _ = lax.optimization_barrier((parts, after))
    return lax.all_to_all(parts, "grp", split_axis=0, concat_axis=0)


def adam_step(param, grad, first, second, decay, rate):
    first_new = BETA_ONE * first + (1.0 - BETA_ONE) * grad
    second_new = BETA_TWO * second + (1.0 - BETA_TWO) * grad * grad
    first_hat = first_new / (1.0 - BETA_ONE**STEP)
    second_hat = second_new / (1.0 - BETA_TWO**STEP)
    updated = param - rate * (first_hat / (jnp.sqrt(second_hat) + ADAM_EPSILON) + decay * param)
    return (updated, first_new, second_new)


def shards(
    tokens,
    segments,
    owners,
    masters,
    first_moment,
    second_moment,
    vectors,
    vector_first,
    vector_second,
    cotangent,
):
    groups = lax.axis_size("grp")
    me = lax.axis_index("grp").astype(jnp.int32)
    own_row = lax.axis_index("row").astype(jnp.int32)
    core = lax.rem(own_row, 2)
    capacity = masters.shape[1]
    width, tokens_here = tokens.shape
    half = width // 2
    fg = groups * width
    sequences, length = segments.shape
    per_group = HEADS // groups
    nv = vectors.shape[1]
    nup = nv - 8
    per_layer = 3 + 3 * groups
    segs = segments.reshape(sequences, 1, length)
    order = jnp.arange(groups, dtype=jnp.int32) ^ me
    here, core_at = me.reshape(1), core.reshape(1)
    square = width * width

    block_index = slot_index(owners, groups, LAYERS, capacity)
    ids = block_index.reshape(LAYERS, per_layer)
    relative = jnp.take(ids[:, 3 : 3 + groups], order, axis=1, mode="clip")
    ids = jnp.concatenate([ids[:, :3], relative, ids[:, 3 + groups :]], axis=1)
    local_blocks = masters[0].astype(BF16).reshape(capacity, 2, half, width)
    local_blocks = jnp.concatenate([local_blocks[:, 0], local_blocks[:, 1]], axis=2)
    everyone = lax.all_gather(local_blocks, "row", axis=0, tiled=True)

    x_parts, cot_parts = (swap(part) for part in scatter_quarters([tokens, cotangent], groups))
    vec_all = jnp.stack([vectors] + [peer(vectors, k) for k in range(1, groups)]).transpose(1, 0, 3, 2)
    vecs = [vec_all[l] for l in range(LAYERS)]
    own_vecs = [vec_all[l, 0] for l in range(LAYERS)]

    share = (3 * groups) // 2
    dense, exchanged = [None] * LAYERS, [None] * LAYERS
    source, _ = lax.optimization_barrier((everyone, (vec_all, x_parts, cot_parts)))
    mine = lax.dynamic_slice(ids[0], (3 + core * share,), (share,))
    (send,) = pick([(share, groups)], mine, source)
    exchanged[0] = [swap(send)]
    others = [(3, 0) for _ in range(LAYERS)] + [(3 * groups, 1) for _ in range(1, LAYERS)]
    wanted = [ids[l, :3] for l in range(LAYERS)] + [ids[l, 3:] for l in range(1, LAYERS)]
    picked = pick(others, jnp.concatenate(wanted), source)
    w_qkv, w_turned = picked[0 : 2 * LAYERS : 2], picked[1 : 2 * LAYERS : 2]

    def fetch(l, after):
        own, _ = lax.optimization_barrier((picked[2 * LAYERS + l - 1][0], after))
        exchanged[l] = [lax.all_gather(own, "grp", axis=0)]

    def arrange(l):
        got = exchanged[l]
        shapes = [(fg, fg), (fg, fg), (groups, width, fg), (groups, fg, width), (groups, fg, width), (groups, width, fg)]
        smem = pl.BlockSpec(memory_space=pltpu.SMEM)
        res = pl.pallas_call(
            functools.partial(arrange_body, groups, nup, len(got)),
            in_specs=[smem, smem] + [HBM_SPEC] * len(got),
            out_specs=[HBM_SPEC] * 6,
            scratch_shapes=[pltpu.VMEM(shape, BF16) for shape in shapes] + [pltpu.SemaphoreType.DMA((6 * groups,))]
            + [pltpu.VMEM(array.shape, BF16) for array in got] + [pltpu.SemaphoreType.DMA((len(got) * groups,))],
            out_shape=[pltpu.HBM(shape, BF16) for shape in shapes],
            name="arrange",
            compiler_params=pltpu.CompilerParams(vmem_limit_bytes=VMEM_LIMIT),
        )(core_at, here, *got)
        dense[l] = dict(zip(WEIGHTS, res))

    def weight_places(names, *more):
        shapes = {"out": (fg, fg), "up": (groups, width, fg), "down": (groups, fg, width)}
        shapes |= {"out_t": (fg, fg), "up_t": (groups, fg, width), "down_t": (groups, width, fg)}
        places = [pltpu.VMEM(shapes[name], BF16) for name in names] + [pltpu.VMEM(shape, BF16) for shape in more]
        return places + [pltpu.SemaphoreType.DMA((len(places),))]

    chunks, at = [], 0
    for count in CHUNKS(sequences):
        chunks.append((at, count))
        at += count
    keep = [dict() for _ in chunks]
    state = {"out": None, "grad": None}
    Line.token = None

    def tok(rows):
        return pl.BlockSpec((rows, length), lambda i, *s: (0, i))

    def quart(rows=width):
        return pl.BlockSpec((groups, rows, QUARTER), lambda i, *s: (0, 0, i))

    def parts(count, rows=width):
        return jax.ShapeDtypeStruct((groups, rows, count * QUARTER), BF16)

    def whole(*shape):
        return pl.BlockSpec(shape, lambda i, *s: (0,) * len(shape))

    def sent(c, key):
        return keep[c - 1][key] if c else None

    def attend(c, l):
        first, count = chunks[c]
        kp = keep[c]
        here_tokens = count * length
        shifted = pl.BlockSpec((width, length), lambda i, *s: (0, i + first))
        seg_spec = pl.BlockSpec((1, 1, length), lambda i, *s: (i + first, 0, 0))
        operands = [segs, w_turned[l], own_vecs[l]]
        specs = [seg_spec, whole(3, width, width), whole(width, nv)]
        outs = [pltpu.HBM((3 * width, here_tokens), BF16), pltpu.HBM((width, here_tokens), BF16),
                pltpu.HBM((per_group, here_tokens), F32)]
        out_specs = [tok(3 * width), tok(width), tok(per_group)]
        outs.append(parts(count))
        out_specs.append(quart())
        if l == 0:
            operands, specs = [tokens] + operands, [shifted] + specs
        else:
            operands, specs = [kp["x", l]] + operands, [quart()] + specs
            outs = [pltpu.HBM((width, here_tokens), BF16)] + outs
            out_specs = [tok(width)] + out_specs
        res = call(
            functools.partial(attend_body, l == 0, per_group, groups), "attend", operands, outs, (),
            (count,), specs, out_specs, flops=here_tokens * (6 * square + 4 * width * length), vmem=VMEM_ATTEND,
        )
        if l:
            kp["xl", l] = res.pop(0)
        kp["qkv", l], kp["ctx", l], kp["lse", l] = res[:3]
        if l:
            kp["far", l] = swap(res[3], sent(c, ("far", l)))
        else:
            kp["parts"] = res[3]

    def early(c, l):
        first, count = chunks[c]
        kp = keep[c]
        n = count * QUARTER
        names = ("out_t", "up_t", "down_t")
        hidden = pltpu.VMEM((groups * nup * width, n), BF16)
        outs = [parts(count), pltpu.HBM((fg, n), F32), pltpu.HBM((fg, n), BF16), pltpu.HBM((fg, n), BF16),
                pltpu.HBM((2, n), F32)] + [pltpu.HBM((groups * nup * width, n), BF16)] * 2
        res = call(
            functools.partial(early_body, groups, first * QUARTER, n), "early",
            [kp["far", l], x_parts, *(dense[l][name] for name in names), vecs[l]], outs, [here],
            scratch=[*weight_places(names), hidden, hidden, pltpu.SemaphoreType.DMA((2 * groups,))],
            far=range(2, 5), far_outs=[5, 6],
            flops=2 * n * groups * square * (groups + 2 * nup),
        )
        kp["x", l + 1] = swap(res[0], sent(c, ("x", l + 1)))
        kp["res", l] = res[1]
        kp["kept", l] = res[2:]

    def grads_before(c, key):
        return [] if c == 0 else list(keep[c - 1][key])

    side_run = (3 * groups + 2) // 2
    stash = pltpu.HBM((groups, side_run, half, 2 * width), BF16)
    stash_places = [
        pltpu.VMEM((groups, 2 * side_run, half, 2 * width), BF16),
        pltpu.SemaphoreType.DMA((8 * groups,)),
    ]

    def middle(c, l):
        first, count = chunks[c]
        kp = keep[c]
        n = count * QUARTER
        before = grads_before(c, ("grads", l))
        hidden = pltpu.VMEM((groups * nup * width, n), BF16)
        names = ("out_t", "up_t", "down_t", "down", "up", "out")
        w_at = 3
        res = call(
            functools.partial(middle_body, groups, first * QUARTER, n, bool(before)), "middle",
            [kp["far", l], cot_parts, kp["res", l - 1], *(dense[l][name] for name in names), vecs[l], *before],
            [parts(count, 2 * width), pltpu.HBM((fg, n), F32), stash, stash], [here, core_at],
            scratch=[hidden, hidden, *stash_places, *weight_places(names, cot_parts.shape)],
            far=[1, *range(w_at, w_at + 6), w_at + 7, w_at + 8], far_outs=[2, 3],
            flops=6 * n * groups * square * (groups + 2 * nup),
        )
        kp["dctx", l] = swap(res[0], sent(c, ("dctx", l)))
        kp["dr", l], kp["grads", l] = res[1], res[2:]

    def late(c, l):
        first, count = chunks[c]
        kp = keep[c]
        n = count * QUARTER
        before = grads_before(c, ("grads", l))
        names = ("down", "up", "out")
        w_at = 8
        hidden = pltpu.VMEM((groups * nup * width, n), BF16)
        res = call(
            functools.partial(late_body, groups, bool(before)), "late",
            [kp["dx", l + 1], kp["far", l], kp["dr", l + 1], *kp["kept", l],
             *(dense[l][name] for name in names), vecs[l], *before],
            [parts(count, 2 * width), stash, stash], [here, core_at],
            scratch=[*stash_places, *weight_places(names, kp["far", l].shape), hidden, hidden,
                     pltpu.SemaphoreType.DMA((2 * groups,))],
            far=[1, w_at - 2, w_at - 1, *range(w_at, w_at + 3), w_at + 4, w_at + 5], far_outs=[1, 2],
            flops=4 * n * groups * square * (groups + 2 * nup),
        )
        kp["dctx", l] = swap(res[0], sent(c, ("dctx", l)))
        kp["grads", l] = res[1:]

    def attend_back(c, l):
        first, count = chunks[c]
        kp = keep[c]
        here_tokens = count * length
        shifted = pl.BlockSpec((width, length), lambda i, *s: (0, i + first))
        seg_spec = pl.BlockSpec((1, 1, length), lambda i, *s: (i + first, 0, 0))
        operands = [kp["dctx", l], kp["ctx", l], kp["qkv", l], kp["lse", l], tokens if l == 0 else kp["xl", l], segs,
                    w_qkv[l]]
        specs = [quart(2 * width), tok(width), tok(3 * width), tok(per_group), shifted if l == 0 else tok(width),
                                      seg_spec, whole(3, width, width)]
        outs = [jax.ShapeDtypeStruct((3, half, 2 * width), BF16), table(width, 2)]
        out_specs = [whole(3, half, 2 * width), whole(width, 2)]
        scratch = [pltpu.VMEM((width, length), BF16), pltpu.VMEM((3, width, width), F32),
                   pltpu.VMEM((2, width, LANES), F32)]
        name = "grad" if l == 0 else "out"
        aliases, follows = None, state[name] is not None
        if follows:
            aliases = {len(operands): 0}
            operands.append(state[name])
            specs.append(pl.BlockSpec(memory_space=pl.ANY))
        if l:
            outs = [parts(count)] + outs
            out_specs = [quart()] + out_specs
            scratch.append(pltpu.VMEM((width, length), F32))
        res = call(
            functools.partial(attend_back_body, l == 0, per_group, groups, follows), "attend_back", operands,
            [table(width, tokens_here)] + outs, (), (count,), specs, [shifted] + out_specs, scratch, aliases,
            here_tokens * (12 * square + 10 * width * length),
            after=[gate] if l == 0 and follows else (), vmem=VMEM_ATTEND,
        )
        state[name] = res[0]
        if l:
            kp["dx", l] = swap(res[1], sent(c, ("dx", l)))
        kp["gqkv", l], kp["gvec", l] = res[-2:]

    def both(key, l):
        return sum(kp[key, l].astype(F32) for kp in keep)

    def scattered(l):
        kept, give = keep[-1]["grads", l]
        give, _ = lax.optimization_barrier((give, keep[0]["dctx", l]))
        got = peer(give, 1, "row")
        if l:
            return lax.psum_scatter(kept + got, "grp", scatter_dimension=0)

        def part(k):
            return lax.dynamic_index_in_dim(kept, me ^ k, 0, False) + lax.dynamic_index_in_dim(got, me ^ k, 0, False)

        return sum(peer(part(k), k).astype(F32) if k else part(k).astype(F32) for k in range(groups)).astype(BF16)

    def side_blocks(l, after=None):
        rows = jnp.pad(both("gvec", l).T, ((0, half - 2), (0, width)))
        all_four = jnp.concatenate([both("gqkv", l), rows[None]], axis=0).astype(BF16)
        if after is not None:
            all_four, _ = lax.optimization_barrier((all_four, after))
        mine = lax.dynamic_slice_in_dim(all_four, 2 * core, 2)
        return mine + peer(lax.dynamic_slice_in_dim(all_four, 2 - 2 * core, 2), 1, "row")

    class ChipSum:
        def __init__(self, value):
            self.shape = value.shape
            self.flat = value.reshape(-1, 2 * width)
            self.rows = self.flat.shape[0] // 2
            self.high = lax.rem(own_row // 2, 2)

        def first(self, after=None):
            give = lax.dynamic_slice_in_dim(self.flat, (1 - self.high) * self.rows, self.rows)
            if after is not None:
                give, _ = lax.optimization_barrier((give, after))
            got = peer(give, 2, "row")
            self.mine = lax.dynamic_slice_in_dim(self.flat, self.high * self.rows, self.rows) + got
            return got

        def second(self, after=None):
            got, step = None, 4
            while step < lax.axis_size("row"):
                give = self.mine
                if after is not None:
                    give, _ = lax.optimization_barrier((give, after))
                got = peer(give, step, "row")
                self.mine = self.mine + got
                step *= 2
            return got

        def third(self):
            return peer(self.mine, 2, "row")

        def whole(self, other):
            first = self.high == 0
            parts = [jnp.where(first, self.mine, other), jnp.where(first, other, self.mine)]
            return jnp.concatenate(parts, axis=0).reshape(self.shape)

        def all(self, after=None):
            self.first(after)
            self.second()
            return self.whole(self.third())

    assert LAYERS == 2
    count = len(chunks)
    ends = [None] * LAYERS

    def run(f, l):
        for c in range(count):
            f(c, l)

    run(attend, 0)
    got, _ = lax.optimization_barrier((exchanged[0][0], Line.token))
    exchanged[0] = [got, peer(got, 1, "row")]
    ahead = got
    for kp in keep:
        kp["far", 0] = ahead = swap(kp["parts"], ahead)
    arrange(0)
    run(early, 0)
    fetch(1, (keep[0]["far", 0], dense[0]["out"]))
    run(attend, 1)
    arrange(1)
    run(middle, 1)
    run(attend_back, 1)
    chips = ChipSum(jnp.concatenate([scattered(1), side_blocks(1)], axis=0))
    run(late, 0)
    gate = chips.first(keep[0]["dctx", 0])
    big = ChipSum(scattered(0)).all()
    run(attend_back, 0)
    second = chips.second()
    third = chips.third()
    total = chips.whole(third)
    ends[1] = [total, peer(total, 1, "row")]
    total = jnp.concatenate([big, ChipSum(side_blocks(0, second)).all()], axis=0)
    ends[0] = [total, peer(total, 1, "row")]
    sources = ends[0] + ends[1]

    span = side_run + 2

    def places_of(side, at):
        return jnp.where(side == core, 0, span) + at

    j, i = jnp.arange(3 * groups, dtype=jnp.int32), jnp.arange(3, dtype=jnp.int32)
    one = jnp.concatenate([places_of(i // 2, side_run + i % 2), places_of(j // side_run, j % side_run)])
    places = (jnp.arange(LAYERS, dtype=jnp.int32)[:, None] * (2 * span) + one[None, :]).reshape(-1)
    targets = own_row * capacity + jnp.arange(capacity, dtype=jnp.int32)
    match = ids.reshape(-1)[None, :] == targets[:, None]
    place = jnp.sum(jnp.where(match, places[None, :], 0), axis=1)
    place = jnp.where(jnp.any(match, axis=1), place, 1 << 20).astype(jnp.int32)
    own_grads = collect(place, sources, width).reshape(1, capacity, square)

    def vector_rows(l):
        odd = jnp.where(core == 1, sources[2 * l], sources[2 * l + 1])
        rest = odd[3 * groups - side_run]
        return jnp.concatenate([odd[side_run + 1, :2, :width], rest[: nv - 2, :width]], axis=0).astype(F32)

    summed_vectors = jnp.stack([vector_rows(l) for l in range(LAYERS)], axis=1)
    new_masters, new_first, new_second = adam_step(
        masters, own_grads, first_moment, second_moment, WEIGHT_DECAY, LEARN_RATE
    )
    rows_first = (array.transpose(1, 0, 2) for array in (vectors, vector_first, vector_second))
    vector, first, second = rows_first
    new_vectors, new_vector_first, new_vector_second = (
        array.transpose(1, 0, 2) for array in adam_step(vector, summed_vectors, first, second, 0.0, VECTOR_RATE)
    )
    return (
        state["out"],
        state["grad"],
        new_masters,
        new_first,
        new_second,
        new_vectors,
        new_vector_first,
        new_vector_second,
    )


def solution(mesh):
    in_specs = (
        P("grp", "row"),
        P("row", None),
        P(),
        P("grp", "row", None),
        P("grp", "row", None),
        P("grp", "row", None),
        P(None, None, "grp"),
        P(None, None, "grp"),
        P(None, None, "grp"),
        P("grp", "row"),
    )
    out_specs = (
        P("grp", "row"),
        P("grp", "row"),
        P("grp", "row", None),
        P("grp", "row", None),
        P("grp", "row", None),
        P(None, None, "grp"),
        P(None, None, "grp"),
        P(None, None, "grp"),
    )
    return jax.shard_map(shards, mesh=mesh, in_specs=in_specs, out_specs=out_specs, check_vma=False)
```
